32 devices in a mesh: orb: 4 (over y, x), gx: 4 (over z), gy: 2 (over core).
Axes of the slice: x: 2, y: 2, z: 4, core: 2. Of those that a mesh axis runs over, the one named last changes fastest.
Arguments:
- orbitals: float32 [16, 512, 256], P('orb', 'gx', 'gy'), may hold values from -6 to 6
- potentials: float32 [64, 512, 256], P('orb', 'gx', 'gy'), may hold values from -6 to 6
- coefficients: float32 [5, 512, 256], P(None, 'gx', 'gy'), may hold values from 0.25 to 1
- metric: float32 [512, 256], P('gx', 'gy'), may hold values from 0.5 to 4.5, as said below
- sweep_counts: int32 [64], P('orb'), may hold values from 4 to 8, as said below
Outputs:
- new_orbitals: float32 [16, 512, 256], P('orb', 'gx', 'gy')
- new_potentials: float32 [64, 512, 256], P('orb', 'gx', 'gy')
The draws below stay inside these ranges and needn't reach their ends.
Inputs may be any that keep to these rules, and one draw needn't show every extreme that they name: `sweep_counts`: each pair gets between 4 and 8 sweeps; both ends occur. `metric`: positive volume elements.
All inputs are finite; a program needn't handle non-finite values.
Results may differ from the reference program's by a relative error of at most 0.0003.
Values sent between devices are 32-bit elements; how exact they have to be, the bound alone decides.
No kernel may reach another device: no remote copies, remote signals or barrier semaphores. Data moves between devices by JAX's collectives and lax.ppermute only.
A program may use at most 64 MiB of HBM per device.

```python
import jax
import jax.numpy as jnp
from jax import lax

SWEEPS = 8
ORB_DEV = 4
NORB = 16
PAIRS = 64
NU = 512
NV = 256
N_ORB = 4


def draw_metric(key, part):
    column = jnp.arange(NV, dtype=jnp.float32) / NV
    rough = jax.random.uniform(key, (NU, NV), jnp.float32, 0.5, 1.5)
    return (1.0 + 2.0 * column)[None, :] * rough


def draw_sweep_counts(key, part):
    counts = jax.random.randint(key, (PAIRS,), SWEEPS // 2, SWEEPS + 1, dtype=jnp.int32)
    return counts.at[0].set(SWEEPS).at[1].set(SWEEPS // 2)


def steps_of(key, dims, split, least, high):
    def one(axis_at, blocks):
        heights = jax.random.uniform(jax.random.fold_in(jax.random.fold_in(key, 6), axis_at), (blocks,), jnp.float32, least / len(split), high / len(split))
        return jnp.repeat(jnp.exp(heights), dims[axis_at] // blocks).reshape((-1,) + (1,) * (len(dims) - axis_at - 1))

    factor_of = one(*split[0])
    for cut in split[1:]:
        factor_of = factor_of * one(*cut)
    return factor_of


def gaussian(own_key, shape, deviation, most, cuts=(), held_as=jnp.bfloat16):
    level = steps_of(own_key, shape, cuts, -0.22, 0.18) if cuts else 1.0
    values = jax.random.normal(own_key, shape, jnp.float32) * deviation * level
    return jnp.minimum(jnp.maximum(values, -most), most).astype(held_as)


def setup_inputs(seed: int = 0) -> dict:
    keys = jax.random.split(jax.random.key(seed), 6)
    return {
        "orbitals": gaussian(keys[0], (NORB, NU, NV), 1.0, 6.0, ((0, 4), (1, 4), (2, 2)), jnp.float32),
        "potentials": gaussian(keys[1], (PAIRS, NU, NV), 1.0, 6.0, ((0, 4), (1, 4), (2, 2)), jnp.float32),
        "coefficients": jnp.clip(0.25 + 0.75 * jax.random.uniform(keys[2], (5, NU, NV), jnp.float32) ** steps_of(keys[2], (5, NU, NV), ((1, 4), (2, 2)), -0.2, 0.2), 0.25, 1.0),
        "metric": draw_metric(jax.random.fold_in(keys[5], 71), 0),
        "sweep_counts": draw_sweep_counts(jax.random.fold_in(keys[5], 71), 0),
    }


relaxation = 0.8
screening = 0.02
step_size = 0.1

def relaxed_sweep(field, source, coefs, active):
    padded = jnp.pad(field, 1)
    neighbours = coefs[0] * padded[:-2, 1:-1] + coefs[1] * padded[2:, 1:-1]
    neighbours = neighbours + coefs[2] * padded[1:-1, 2:] + coefs[3] * padded[1:-1, :-2]
    neighbours = neighbours + coefs[4] * (padded[:-2, 2:] + padded[2:, :-2] - padded[:-2, :-2] - padded[2:, 2:])
    diagonal = (1.0 + screening) * (coefs[0] + coefs[1] + coefs[2] + coefs[3] + 4.0 * coefs[4])
    return field + relaxation * active * ((neighbours + source) / diagonal - field)

def reference(orbitals, potentials, coefficients, metric, sweep_counts):
    pair_count = potentials.shape[0]
    pair_index = jnp.arange(pair_count, dtype=jnp.int32)
    group_index = pair_index // (ORB_DEV * ORB_DEV)
    within = pair_index % (ORB_DEV * ORB_DEV)
    first_orb = (group_index * ORB_DEV + within // ORB_DEV).astype(jnp.int32)
    second_orb = ((group_index - 1 + N_ORB) % N_ORB * ORB_DEV + within % ORB_DEV).astype(jnp.int32)

    def pair_step(exchange_sum, pair_item):
        field, first, second, counts = pair_item
        source = metric * (orbitals[first] * orbitals[second])
        for sweep in range(SWEEPS):
            active = (counts > sweep).astype(orbitals.dtype)
            field = relaxed_sweep(field, source, coefficients, active)
        exchange_sum = exchange_sum.at[first].add(field * orbitals[second])
        exchange_sum = exchange_sum.at[second].add(field * orbitals[first])
        return (exchange_sum, field)
    start_sum = jnp.zeros(orbitals.shape, orbitals.dtype)
    exchange_sum, new_potentials = lax.scan(pair_step, start_sum, (potentials, first_orb, second_orb, sweep_counts))
    updated = orbitals - step_size * exchange_sum
    norm_sums = lax.optimization_barrier(jnp.sum(metric[None] * updated * updated, axis=(1, 2)))
    rescale = jnp.sqrt(NU * NV / norm_sums)
    return (updated * rescale[:, None, None], new_potentials)
```

```python
import functools

import jax
import jax.numpy as jnp
from jax import lax
from jax.experimental import pallas as pl
from jax.experimental.pallas import tpu as pltpu
from jax.sharding import PartitionSpec as P

SWEEPS = 8

relaxation = 0.8
screening = 0.02
step_size = 0.1

LANES = 128
SUB = 8
HALO = 8
STRIP = 32
BLOCKS = LANES // STRIP
VMEM_LIMIT = 40 * 1024 * 1024

VMEM = pl.BlockSpec(memory_space=pltpu.VMEM)
SMEM = pl.BlockSpec(memory_space=pltpu.SMEM)
ANY = pl.BlockSpec(memory_space=pl.ANY)


def f32(*shape):
    return jax.ShapeDtypeStruct(shape, jnp.float32)


def params(limit=VMEM_LIMIT):
    return pltpu.CompilerParams(vmem_limit_bytes=limit)


def lane_of(rows=SUB):
    return lax.broadcasted_iota(jnp.int32, (rows, LANES), 1)


def packed(fields):
    rows = fields[0].shape[0]
    block = lane_of(rows) // STRIP
    out = jnp.zeros((rows, LANES), jnp.float32)
    for at, value in enumerate(fields):
        turned = pltpu.roll(value, (STRIP * at + STRIP // 2) % LANES, 1)
        out = jnp.where(block == at, turned, out)
    return out


def replicated(value, at):
    one = jnp.where(lane_of(value.shape[0]) // STRIP == at, value, 0.0)
    one = one + pltpu.roll(one, STRIP, 1)
    return one + pltpu.roll(one, 2 * STRIP, 1)


def pack_kernel(v_ref, o_ref, m_ref, c_ref, e_ref):
    own = o_ref.shape[0]
    e_ref[0] = packed([o_ref[k] for k in range(own)])
    for first in range(own):
        e_ref[1 + first] = packed([v_ref[first * own + k] for k in range(own)])
    e_ref[1 + own] = packed([m_ref[...], c_ref[0], c_ref[1], c_ref[2]])
    e_ref[2 + own] = packed([c_ref[3], c_ref[4]])


def pack_edges(potentials, orbitals, metric, coefficients):
    own, rows, lanes = orbitals.shape
    return pl.pallas_call(
        pack_kernel,
        out_shape=f32(own + 3, rows, lanes),
        in_specs=[VMEM] * 4,
        out_specs=VMEM,
        compiler_params=params(),
        name="pack_edges",
    )(potentials, orbitals, metric, coefficients)


def rows_kernel(sides, par_ref, v_ref, o_ref, m_ref, c_ref, *refs):
    e_refs, (pay_a, pay_b), sems = refs[:sides], refs[sides : sides + 2], refs[sides + 2]
    own, rows, _ = o_ref.shape
    pairs = v_ref.shape[0]
    groups = e_refs[0].shape[0]
    odd = par_ref[0]
    copies = []

    def send(source, pay, start, at, count):
        copy = pltpu.make_async_copy(
            source.at[:, pl.ds(start, HALO), :], pay.at[pl.ds(at, count)], sems.at[len(copies)]
        )
        copy.start()
        copies.append(copy)

    for pay, start in ((pay_a, (1 - odd) * (rows - HALO)), (pay_b, odd * (rows - HALO))):
        start = pl.multiple_of(start, HALO)
        send(o_ref, pay, start, 0, own)
        at = own + sides
        send(v_ref, pay, start, at, pairs)
        at += pairs
        send(m_ref, pay, start, at, 1)
        send(c_ref, pay, start, at + 1, 5)
        at += 6
        for side, e_ref in enumerate(e_refs):
            send(e_ref.at[pl.ds(0, 1)], pay, start, own + side, 1)
            send(e_ref.at[pl.ds(1, groups - 1)], pay, start, at, groups - 1)
            at += groups - 1
    for copy in copies:
        copy.wait()


def row_payloads(odd, potentials, orbitals, metric, coefficients, received):
    own, rows, lanes = orbitals.shape
    sides = len(received)
    fields = own + potentials.shape[0] + 6 + sides * received[0].shape[0]
    return pl.pallas_call(
        functools.partial(rows_kernel, sides),
        out_shape=(f32(fields, HALO, lanes),) * 2,
        in_specs=[SMEM] + [ANY] * (4 + sides),
        out_specs=(ANY, ANY),
        scratch_shapes=[pltpu.SemaphoreType.DMA((2 * (4 + 2 * sides),))],
        compiler_params=params(),
        name="row_payloads",
    )(odd, potentials, orbitals, metric[None], coefficients, *received)


def spread(ref, count, *index):
    return [ref[(*index, pl.ds(t, SUB, stride=count), slice(None))] for t in range(count)]


def spread_store(ref, values, *index):
    count = len(values)
    for t, value in enumerate(values):
        ref[(*index, pl.ds(t, SUB, stride=count), slice(None))] = value


def scaled_coefs(coefs):
    total = coefs[0] + coefs[1] + coefs[2] + coefs[3] + 4.0 * coefs[4]
    diagonal = (1.0 + screening) * total
    return relaxation / jnp.where(diagonal == 0.0, 1.0, diagonal)


def swept(field, source, coefs, mask_west=None, mask_east=None):
    count = len(field)
    east = [pltpu.roll(v, LANES - 1, 1) for v in field]
    west = [pltpu.roll(v, 1, 1) for v in field]
    if mask_west is not None:
        west = [jnp.where(mask_west, 0.0, w) for w in west]
        east = [jnp.where(mask_east, 0.0, e) for e in east]
    slope = [e - w for e, w in zip(east, west)]

    def above(values, t):
        return values[t - 1] if t else pltpu.roll(values[count - 1], 1, 0)

    def below(values, t):
        return values[t + 1] if t < count - 1 else pltpu.roll(values[0], SUB - 1, 0)

    out = []
    for t in range(count):
        value = (1.0 - relaxation) * field[t] + source(t)
        value = value + coefs(0, t) * above(field, t) + coefs(1, t) * below(field, t)
        value = value + coefs(2, t) * east[t] + coefs(3, t) * west[t]
        out.append(value + coefs(4, t) * (above(slope, t) - below(slope, t)))
    return out


def relaxed(count, field, source, coefs, masks):
    west, east, dead = masks
    field = swept(field, source, coefs, west, east)
    field = [jnp.where(dead, 0.0, v) for v in field]

    def body(_, values):
        return tuple(swept(list(values), source, coefs))

    return list(lax.fori_loop(1, count, body, tuple(field)))


def lane_masks(odd):
    lane = lane_of()
    west = (lane == 0) & (odd == 0)
    east = (lane == LANES - 1) & (odd == 1)
    dead = lane == (1 - odd) * (LANES - 1)
    return west, east, dead


def interior_kernel(odd_ref, n_ref, v_ref, o_ref, p_ref, m_ref, c_ref, out_ref, cf, ms, sr):
    own, rows, _ = o_ref.shape
    count = rows // SUB
    masks = lane_masks(odd_ref[1])
    dead = masks[2]
    metric = spread(m_ref, count)
    raw = [spread(c_ref, count, n) for n in range(5)]
    for t in range(count):
        scale = scaled_coefs([raw[n][t] for n in range(5)])
        scale = jnp.where(dead, 0.0, scale)
        ms[t] = scale * metric[t]
        for n in range(5):
            cf[n, t] = scale * raw[n][t]

    def pair(p, carry):
        first, second = p // own, p % own
        o, q = spread(o_ref, count, first), spread(p_ref, count, second)
        for t in range(count):
            sr[t] = ms[t] * (o[t] * q[t])
        field = spread(v_ref, count, p)
        field = relaxed(n_ref[p], field, lambda t: sr[t], lambda n, t: cf[n, t], masks)
        spread_store(out_ref, field, p)
        return carry

    lax.fori_loop(0, v_ref.shape[0], pair, 0)


def interior(odd, counts, potentials, orbitals, partner, metric, coefficients):
    own, rows, lanes = orbitals.shape
    count = rows // SUB
    return pl.pallas_call(
        interior_kernel,
        out_shape=f32(*potentials.shape),
        in_specs=[SMEM, SMEM] + [VMEM] * 5,
        out_specs=VMEM,
        scratch_shapes=[
            pltpu.VMEM((5, count, SUB, lanes), jnp.float32),
            pltpu.VMEM((count, SUB, lanes), jnp.float32),
            pltpu.VMEM((count, SUB, lanes), jnp.float32),
        ],
        compiler_params=params(),
        name="interior",
    )(odd, counts, potentials, orbitals, partner, metric, coefficients)


def boundary_kernel(
    sides, odd_ref, n_ref, v_ref, o_ref, p_ref, m_ref, c_ref, inner_ref, e_ref, *refs
):
    recv = refs[:sides]
    ra_ref, rb_ref, p2_ref, pe_ref = refs[sides : sides + 4]
    out_ref, home_ref, back_ref = refs[sides + 4 : sides + 7]
    rb, rcf, rms, rsr, st, scf, sms, ssr, sv = refs[sides + 7 :]
    own, rows, _ = o_ref.shape
    pairs = v_ref.shape[0]
    groups = e_ref.shape[0]
    row_odd, col_odd = odd_ref[0], odd_ref[1]
    lane = lane_of()
    low_is_a = row_odd == 1

    def beyond(at):
        a, b = ra_ref[at], rb_ref[at]
        return jnp.where(low_is_a, a, b), jnp.where(low_is_a, b, a)

    def beyond_partner(at):
        a, b = p2_ref[at], p2_ref[own + sides + at]
        return jnp.where(low_is_a, a, b), jnp.where(low_is_a, b, a)

    v_at, m_at = own + sides, own + sides + pairs
    e_at = m_at + 6
    band = 3 * SUB

    def fill(at, low, high, top, bottom):
        rb[at, 0:SUB] = low
        rb[at, SUB:band] = top
        rb[at, band : band + 2 * SUB] = bottom
        rb[at, band + 2 * SUB : 2 * band] = high

    def fill_from(at, ends, ref, index):
        fill(
            at, *ends, ref[(*index, slice(0, 2 * SUB))], ref[(*index, slice(rows - 2 * SUB, rows))]
        )

    ends_o = [beyond(k) for k in range(own)]
    ends_p = [beyond_partner(k) for k in range(own)]
    ends_v = [beyond(v_at + k) for k in range(pairs)]
    ends_m = beyond(m_at)
    ends_c = [beyond(m_at + 1 + n) for n in range(5)]
    for k in range(pairs):
        fill_from(k, ends_v[k], v_ref, (k,))
    for k in range(own):
        fill_from(pairs + k, ends_o[k], o_ref, (k,))
        fill_from(pairs + own + k, ends_p[k], p_ref, (k,))
    fill_from(pairs + 2 * own, ends_m, m_ref, ())
    for n in range(5):
        fill_from(pairs + 2 * own + 1 + n, ends_c[n], c_ref, (n,))

    count = 2 * band // SUB
    masks = lane_masks(col_odd)
    metric = spread(rb, count, pairs + 2 * own)
    raw = [spread(rb, count, pairs + 2 * own + 1 + n) for n in range(5)]
    for t in range(count):
        scale = jnp.where(masks[2], 0.0, scaled_coefs([raw[n][t] for n in range(5)]))
        rms[t] = scale * metric[t]
        for n in range(5):
            rcf[n, t] = scale * raw[n][t]

    def row_pair(p, carry):
        first, second = p // own, p % own
        o, q = spread(rb, count, pairs + first), spread(rb, count, pairs + own + second)
        for t in range(count):
            rsr[t] = rms[t] * (o[t] * q[t])
        field = spread(rb, count, p)
        field = relaxed(n_ref[p], field, lambda t: rsr[t], lambda n, t: rcf[n, t], masks)
        spread_store(rb, field, p)
        inner_ref[p, 0:SUB] = rb[p, SUB : 2 * SUB]
        inner_ref[p, rows - SUB : rows] = rb[p, band + SUB : band + 2 * SUB]
        return carry

    lax.fori_loop(0, pairs, row_pair, 0)

    tall = rows + 2 * SUB
    high = tall // SUB
    corner_own = {}
    for end in range(2):
        corner_own[end] = [packed([ends_o[k][end] for k in range(own)])]
        for first in range(own):
            corner_own[end].append(
                packed([ends_v[first * own + k][end] for k in range(own)])
            )
        corner_own[end].append(packed([ends_m[end]] + [ends_c[n][end] for n in range(3)]))
        corner_own[end].append(packed([ends_c[n][end] for n in range(3, 5)]))
        corner_own[end].append(packed([ends_p[k][end] for k in range(own)]))
    own_partner = packed([p_ref[k] for k in range(own)])

    for side in range(sides):
        left_own = (col_odd == 0) if side == 0 else (col_odd == 1)
        from_own = jnp.where(left_own, lane % STRIP, STRIP - 1 - lane % STRIP) < STRIP // 2
        from_own_tall = (
            jnp.where(left_own, lane_of(rows) % STRIP, STRIP - 1 - lane_of(rows) % STRIP)
            < STRIP // 2
        )
        for g in range(groups + 1):
            if g == groups:
                mine, theirs = own_partner, pe_ref[side]
                ends = beyond_partner(own + side)
            else:
                mine, theirs = e_ref[g], recv[side][g]
                ends = (
                    beyond(own + side)
                    if g == 0
                    else beyond(e_at + side * (groups - 1) + g - 1)
                )
            st[g, SUB : SUB + rows] = jnp.where(from_own_tall, mine, theirs)
            st[g, 0:SUB] = jnp.where(from_own, corner_own[0][g], ends[0])
            st[g, SUB + rows : tall] = jnp.where(from_own, corner_own[1][g], ends[1])

        mg, cg = spread(st, high, own + 1), spread(st, high, own + 2)
        for t in range(high):
            cs = [replicated(mg[t], 1 + n) for n in range(3)]
            cs += [replicated(cg[t], n) for n in range(2)]
            scale = scaled_coefs(cs)
            sms[t] = scale * replicated(mg[t], 0)
            for n in range(5):
                scf[n, t] = scale * cs[n]

        def strip_group(g, carry):
            o, q = spread(st, high, 0), spread(st, high, groups)
            for t in range(high):
                ssr[t] = sms[t] * (replicated(o[t], g) * q[t])
            steps = jnp.zeros((SUB, LANES), jnp.int32)
            for k in range(own):
                steps = jnp.where(lane // STRIP == k, n_ref[g * own + k], steps)

            def body(s, values):
                new = swept(list(values), lambda t: ssr[t], lambda n, t: scf[n, t])
                return tuple(jnp.where(steps > s, n, v) for n, v in zip(new, values))

            field = tuple(spread(st, high, 1 + g))
            field = lax.fori_loop(0, SWEEPS, body, field)
            spread_store(sv, list(field), g)
            return carry

        lax.fori_loop(0, own, strip_group, 0)

        right = left_own
        edge = jnp.where(right, LANES - 1 - lane, lane) < HALO

        def merge(r, carry):
            at = pl.multiple_of(r * SUB, SUB)
            for first in range(own):
                strip = sv[first, pl.ds(at + SUB, SUB)]
                for second in range(own):
                    p = first * own + second
                    turned = pltpu.roll(strip, (-(STRIP * second + STRIP // 2)) % LANES, 1)
                    old = inner_ref[p, pl.ds(at, SUB)]
                    inner_ref[p, pl.ds(at, SUB)] = jnp.where(edge, turned, old)
            return carry

        lax.fori_loop(0, rows // SUB, merge, 0)

    def sums(r, carry):
        at = pl.multiple_of(r * SUB, SUB)
        o = [o_ref[k, pl.ds(at, SUB)] for k in range(own)]
        q = [p_ref[k, pl.ds(at, SUB)] for k in range(own)]
        home, back = [0.0] * own, [0.0] * own
        for first in range(own):
            for second in range(own):
                p = first * own + second
                v = inner_ref[p, pl.ds(at, SUB)]
                out_ref[p, pl.ds(at, SUB)] = v
                home[first] = home[first] + v * q[second]
                back[second] = back[second] + v * o[first]
        for k in range(own):
            home_ref[k, pl.ds(at, SUB)] = o[k] - step_size * home[k]
            back_ref[k, pl.ds(at, SUB)] = back[k]
        return carry

    lax.fori_loop(0, rows // SUB, sums, 0)


def boundary(
    odd, counts, potentials, orbitals, partner, metric, coefficients, inner, edges, received,
    rows_a, rows_b, partner_rows, partner_edges,
):
    own, rows, lanes = orbitals.shape
    sides = len(received)
    groups = edges.shape[0]
    pairs = potentials.shape[0]
    count, high = 6, rows // SUB + 2
    fields = pairs + 2 * own + 6
    return pl.pallas_call(
        functools.partial(boundary_kernel, sides),
        out_shape=(f32(*potentials.shape), f32(*orbitals.shape), f32(*orbitals.shape)),
        in_specs=[SMEM, SMEM] + [VMEM] * (7 + sides + 4),
        out_specs=(VMEM, VMEM, VMEM),
        scratch_shapes=[
            pltpu.VMEM((fields, count * SUB, lanes), jnp.float32),
            pltpu.VMEM((5, count, SUB, lanes), jnp.float32),
            pltpu.VMEM((count, SUB, lanes), jnp.float32),
            pltpu.VMEM((count, SUB, lanes), jnp.float32),
            pltpu.VMEM((groups + 1, high * SUB, lanes), jnp.float32),
            pltpu.VMEM((5, high, SUB, lanes), jnp.float32),
            pltpu.VMEM((high, SUB, lanes), jnp.float32),
            pltpu.VMEM((high, SUB, lanes), jnp.float32),
            pltpu.VMEM((own, high * SUB, lanes), jnp.float32),
        ],
        compiler_params=params(),
        name="boundary",
    )(
        odd, counts, potentials, orbitals, partner, metric, coefficients, inner, edges, *received,
        rows_a, rows_b, partner_rows, partner_edges,
    )


def norm_kernel(home_ref, recv_ref, m_ref, upd_ref, norm_ref):
    own = home_ref.shape[0]
    norm_ref[...] = jnp.zeros_like(norm_ref)
    for k in range(own):
        updated = home_ref[k] - step_size * recv_ref[k]
        upd_ref[k] = updated
        weighted = m_ref[...] * updated * updated
        norm_ref[k : k + 1] = jnp.sum(weighted, axis=0, keepdims=True)


def partial_norms(home, received, metric):
    own, _, lanes = home.shape
    return pl.pallas_call(
        norm_kernel,
        out_shape=(f32(*home.shape), f32(-(-own // SUB) * SUB, lanes)),
        in_specs=[VMEM] * 3,
        out_specs=(VMEM, VMEM),
        compiler_params=params(),
        name="partial_norms",
    )(home, received, metric)


def scale_kernel(cells, upd_ref, norm_ref, other_ref, out_ref):
    for k in range(upd_ref.shape[0]):
        total = norm_ref[k : k + 1] + other_ref[k : k + 1]
        norm = jnp.sum(total, axis=1, keepdims=True)
        out_ref[k] = upd_ref[k] * jnp.sqrt(cells / norm)


def rescaled(updated, norms, others, cells):
    return pl.pallas_call(
        functools.partial(scale_kernel, float(cells)),
        out_shape=f32(*updated.shape),
        in_specs=[VMEM] * 3,
        out_specs=VMEM,
        compiler_params=params(),
        name="rescaled",
    )(updated, norms, others)


def shifted(value, axis, by):
    size = lax.axis_size(axis)
    return lax.ppermute(value, axis, [(i, (i + by) % size) for i in range(size)])


def pair_swaps(size):
    even = [(i, i + 1) for i in range(0, size - 1, 2)]
    odd = [(i, i + 1) for i in range(1, size - 1, 2)]
    return [p + [(b, a) for a, b in p] for p in (even, odd)]


def local(orbitals, potentials, coefficients, metric, sweep_counts):
    own, rows, lanes = orbitals.shape
    gx, gy = lax.axis_size("gx"), lax.axis_size("gy")
    odd = jnp.stack([lax.axis_index("gx") % 2, lax.axis_index("gy") % 2]).astype(jnp.int32)
    col_swaps = [p for p in pair_swaps(gy) if p]
    row_swaps = pair_swaps(gx)

    partner = shifted(orbitals, "orb", 1)
    edges = pack_edges(potentials, orbitals, metric, coefficients)
    received = [lax.ppermute(edges, "gy", swap) for swap in col_swaps]
    pay_a, pay_b = row_payloads(odd, potentials, orbitals, metric, coefficients, received)
    rows_a = lax.ppermute(pay_a, "gx", row_swaps[0])
    rows_b = lax.ppermute(pay_b, "gx", row_swaps[1])
    sides = len(received)
    lead = own + sides
    beside = [rows_a[:lead], rows_b[:lead]]
    beside += [r[0].reshape(rows // SUB, SUB, lanes) for r in received]
    second = shifted(jnp.concatenate(beside, 0), "orb", 1)
    partner_rows = second[: 2 * lead]
    partner_edges = second[2 * lead :].reshape(sides, rows, lanes)

    inner = interior(odd, sweep_counts, potentials, orbitals, partner, metric, coefficients)
    fields, home, back = boundary(
        odd, sweep_counts, potentials, orbitals, partner, metric, coefficients, inner, edges,
        received, rows_a, rows_b, partner_rows, partner_edges,
    )
    updated, norms = partial_norms(home, shifted(back, "orb", -1), metric)
    hops = [("gy", 1 << k) for k in range(gy.bit_length() - 1)]
    hops += [("gx", 1 << k) for k in range(gx.bit_length() - 1)]
    for at, (axis, by) in enumerate(hops):
        size = lax.axis_size(axis)
        other = lax.ppermute(norms, axis, [(i, i ^ by) for i in range(size)])
        if at < len(hops) - 1:
            norms = norms + other
    return (rescaled(updated, norms, other, rows * lanes * gx * gy), fields)


def solution(mesh):
    return jax.shard_map(
        local,
        mesh=mesh,
        in_specs=(
            P("orb", "gx", "gy"),
            P("orb", "gx", "gy"),
            P(None, "gx", "gy"),
            P("gx", "gy"),
            P("orb"),
        ),
        out_specs=(P("orb", "gx", "gy"), P("orb", "gx", "gy")),
        check_vma=False,
    )
```

```python
import functools

import jax
import jax.numpy as jnp
from jax import lax
from jax.experimental import pallas as pl
from jax.experimental.pallas import tpu as pltpu
from jax.sharding import PartitionSpec as P

SWEEPS = 8

relaxation = 0.8
screening = 0.02
step_size = 0.1

LANES = 128
SUB = 8
HALO = 8
STRIP = 32
LEAST = 4
GROUP = 4
BANDS = 8
AHEAD = 16
VMEM_LIMIT = 40 * 1024 * 1024

VMEM = pl.BlockSpec(memory_space=pltpu.VMEM)
SMEM = pl.BlockSpec(memory_space=pltpu.SMEM)
ANY = pl.BlockSpec(memory_space=pl.ANY)


def f32(*shape):
    return jax.ShapeDtypeStruct(shape, jnp.float32)


def params(limit=VMEM_LIMIT):
    return pltpu.CompilerParams(vmem_limit_bytes=limit)


def lane_of(rows=SUB):
    return lax.broadcasted_iota(jnp.int32, (rows, LANES), 1)


def packed(fields):
    rows = fields[0].shape[0]
    block = lane_of(rows) // STRIP
    out = jnp.zeros((rows, LANES), jnp.float32)
    for at, value in enumerate(fields):
        turned = pltpu.roll(value, (STRIP * at + STRIP // 2) % LANES, 1)
        out = jnp.where(block == at, turned, out)
    return out


def replicated(value, at):
    one = jnp.where(lane_of(value.shape[0]) // STRIP == at, value, 0.0)
    one = one + pltpu.roll(one, STRIP, 1)
    return one + pltpu.roll(one, 2 * STRIP, 1)


def spread(ref, count, *index):
    return [ref[(*index, pl.ds(t, SUB, stride=count), slice(None))] for t in range(count)]


def spread_store(ref, values, *index):
    count = len(values)
    for t, value in enumerate(values):
        ref[(*index, pl.ds(t, SUB, stride=count), slice(None))] = value


def scaled_coefs(coefs):
    total = coefs[0] + coefs[1] + coefs[2] + coefs[3] + 4.0 * coefs[4]
    diagonal = (1.0 + screening) * total
    return relaxation / jnp.where(diagonal == 0.0, 1.0, diagonal)


def sweep(fields, count, old, new, source, coefs, west=None, east=None, dead=None, keep=None):
    held, to_east, to_west, slopes = {}, {}, {}, {}

    def issue(k, t):
        value = old[k, t]
        held[k, t] = value
        e, w = pltpu.roll(value, LANES - 1, 1), pltpu.roll(value, 1, 1)
        if west is not None:
            w, e = jnp.where(west, 0.0, w), jnp.where(east, 0.0, e)
        to_east[k, t], to_west[k, t] = e, w

    def field(k, t):
        return held[k, t]

    def slope(k, t):
        if (k, t) not in slopes:
            slopes[k, t] = to_east[k, t] - to_west[k, t]
        return slopes[k, t]

    def above(get, k, t):
        return get(k, t - 1) if t else pltpu.roll(get(k, count - 1), 1, 0)

    def below(get, k, t):
        return get(k, t + 1) if t < count - 1 else pltpu.roll(get(k, 0), SUB - 1, 0)

    order = []
    for k in range(fields):
        order += [(k, count - 1)] + [(k, t) for t in range(count - 1)]
    done = 0
    for at in range(fields * count):
        k, t = divmod(at, count)
        until = min(len(order), max(at + AHEAD, k * count + min(t + 3, count)))
        while done < until:
            issue(*order[done])
            done += 1
        value = (1.0 - relaxation) * field(k, t) + source[k, t]
        value = value + coefs[0, t] * above(field, k, t) + coefs[1, t] * below(field, k, t)
        value = value + coefs[2, t] * to_east[k, t] + coefs[3, t] * to_west[k, t]
        value = value + coefs[4, t] * (above(slope, k, t) - below(slope, k, t))
        if dead is not None:
            value = jnp.where(dead, 0.0, value)
        if keep is not None:
            value = jnp.where(keep[k], value, field(k, t))
        new[k, t] = value


def relax(steps, count, here, there, source, coefs, masks):
    fields = len(steps)
    west, east, dead = masks
    pair = (here, there)
    sweep(fields, count, here, there, source, coefs, west, east, dead)
    for s in range(1, LEAST):
        sweep(fields, count, pair[s % 2], pair[1 - s % 2], source, coefs)
    top = functools.reduce(jnp.maximum, steps)

    def body(turn, carry):
        for s in range(2):
            at = LEAST + 2 * turn + s
            keep = [jnp.full((SUB, LANES), n, jnp.int32) > at for n in steps]
            sweep(fields, count, pair[s], pair[1 - s], source, coefs, keep=keep)
        return carry

    lax.fori_loop(0, (top - LEAST + 1) // 2, body, 0)


def lane_masks(odd):
    lane = lane_of()
    west = (lane == 0) & (odd == 0)
    east = (lane == LANES - 1) & (odd == 1)
    dead = lane == (1 - odd) * (LANES - 1)
    return west, east, dead


def prepare_kernel(odd_ref, v_ref, o_ref, m_ref, c_ref, vs_ref, om_ref, cf_ref, e_ref):
    own, rows, _ = o_ref.shape
    count = rows // SUB
    e_ref[0] = packed([o_ref[k] for k in range(own)])
    for first in range(own):
        e_ref[1 + first] = packed([v_ref[first * own + k] for k in range(own)])
    e_ref[1 + own] = packed([m_ref[...], c_ref[0], c_ref[1], c_ref[2]])
    e_ref[2 + own] = packed([c_ref[3], c_ref[4]])
    dead = lane_masks(odd_ref[1])[2]
    metric = spread(m_ref, count)
    raw = [spread(c_ref, count, n) for n in range(5)]
    weights = []
    for t in range(count):
        scale = jnp.where(dead, 0.0, scaled_coefs([raw[n][t] for n in range(5)]))
        weights.append(scale * metric[t])
        for n in range(5):
            cf_ref[n, t] = scale * raw[n][t]
    for k in range(own):
        for t, value in enumerate(spread(o_ref, count, k)):
            om_ref[k, t] = weights[t] * value

    def one(p, carry):
        for t, value in enumerate(spread(v_ref, count, p)):
            vs_ref[p, t] = value
        return carry

    lax.fori_loop(0, v_ref.shape[0], one, 0)


def prepare(odd, potentials, orbitals, metric, coefficients):
    own, rows, lanes = orbitals.shape
    count = rows // SUB
    return pl.pallas_call(
        prepare_kernel,
        out_shape=(
            f32(potentials.shape[0], count, SUB, lanes),
            f32(own, count, SUB, lanes),
            f32(5, count, SUB, lanes),
            f32(own + 3, rows, lanes),
        ),
        in_specs=[SMEM] + [VMEM] * 4,
        out_specs=(VMEM,) * 4,
        compiler_params=params(),
        name="prepare",
    )(odd, potentials, orbitals, metric, coefficients)


def rows_kernel(par_ref, o_ref, v_ref, m_ref, c_ref, pay_a, pay_b, sems):
    rows = o_ref.shape[1]
    odd = par_ref[0]
    copies = []
    for pay, start in ((pay_a, (1 - odd) * (rows - HALO)), (pay_b, odd * (rows - HALO))):
        start = pl.multiple_of(start, HALO)
        at = 0
        for ref in (o_ref, v_ref, m_ref, c_ref):
            count = ref.shape[0]
            copy = pltpu.make_async_copy(
                ref.at[:, pl.ds(start, HALO), :], pay.at[pl.ds(at, count)], sems.at[len(copies)]
            )
            copy.start()
            copies.append(copy)
            at += count
    for copy in copies:
        copy.wait()


def row_payloads(odd, orbitals, potentials, metric, coefficients):
    own, _, lanes = orbitals.shape
    fields = own + potentials.shape[0] + 1 + coefficients.shape[0]
    return pl.pallas_call(
        rows_kernel,
        out_shape=(f32(fields, HALO, lanes),) * 2,
        in_specs=[SMEM] + [ANY] * 4,
        out_specs=(ANY, ANY),
        scratch_shapes=[pltpu.SemaphoreType.DMA((8,))],
        compiler_params=params(),
        name="row_payloads",
    )(odd, orbitals, potentials, metric[None], coefficients)


def interior_kernel(groups, before, odd_ref, n_ref, by_ref, vs_ref, om_ref, cf_ref, p_ref, *refs):
    out_ref, qs, sr, va, vb = refs[-5:]
    own, count = om_ref.shape[:2]
    masks = lane_masks(odd_ref[1])
    if before:
        earlier = refs[0]

        def keep(k, carry):
            out_ref[by_ref[k]] = earlier[by_ref[k]]
            return carry

        lax.fori_loop(0, before * GROUP, keep, 0)
    for k in range(own):
        for t, value in enumerate(spread(p_ref, count, k)):
            qs[k, t] = value

    def group(g, carry):
        pairs = [by_ref[g * GROUP + k] for k in range(GROUP)]
        for k, p in enumerate(pairs):
            first, second = p // own, p % own
            for t in range(count):
                sr[k, t] = om_ref[first, t] * qs[second, t]
                va[k, t] = vs_ref[p, t]
        relax([n_ref[p] for p in pairs], count, va, vb, sr, cf_ref, masks)
        for k, p in enumerate(pairs):
            spread_store(out_ref, [va[k, t] for t in range(count)], p)
        return carry

    lax.fori_loop(before, before + groups, group, 0)


def interior(groups, before, odd, counts, order, ready, partner, *earlier):
    spread_v, weighted, coefs, _ = ready
    pairs, count, _, lanes = spread_v.shape
    own, rows, _ = partner.shape
    four = pltpu.VMEM((GROUP, count, SUB, lanes), jnp.float32)
    return pl.pallas_call(
        functools.partial(interior_kernel, groups, before),
        out_shape=f32(pairs, rows, lanes),
        in_specs=[SMEM] * 3 + [VMEM] * (4 + len(earlier)),
        out_specs=VMEM,
        scratch_shapes=[pltpu.VMEM((own, count, SUB, lanes), jnp.float32), four, four, four],
        compiler_params=params(),
        name=f"interior{before}",
    )(odd, counts, order, spread_v, weighted, coefs, partner, *earlier)


def beyond(odd, a, b):
    low_is_a = odd == 1
    return jnp.where(low_is_a, a, b), jnp.where(low_is_a, b, a)


def edges_kernel(odd_ref, e_ref, ra_ref, rb_ref, p2_ref, p_ref, out_ref):
    own, rows, _ = p_ref.shape
    odd = odd_ref[0]
    groups = e_ref.shape[0]
    for g in range(groups):
        out_ref[g, SUB : SUB + rows] = e_ref[g]
    out_ref[groups, SUB : SUB + rows] = packed([p_ref[k] for k in range(own)])
    pairs = own * own
    ends = [beyond(odd, ra_ref[f], rb_ref[f]) for f in range(own + pairs + 6)]
    ends += [beyond(odd, p2_ref[k], p2_ref[own + k]) for k in range(own)]
    lists = [range(own)] + [range(own * (1 + k), own * (2 + k)) for k in range(own)]
    at = own + pairs
    lists += [range(at, at + 4), range(at + 4, at + 6), range(at + 6, at + 6 + own)]
    for g, fields in enumerate(lists):
        out_ref[g, 0:SUB] = packed([ends[f][0] for f in fields])
        out_ref[g, SUB + rows :] = packed([ends[f][1] for f in fields])


def tall_edges(odd, edges, rows_a, rows_b, partner_rows, partner):
    groups, rows, lanes = edges.shape
    return pl.pallas_call(
        edges_kernel,
        out_shape=f32(groups + 1, rows + 2 * SUB, lanes),
        in_specs=[SMEM] + [VMEM] * 5,
        out_specs=VMEM,
        compiler_params=params(),
        name="tall_edges",
    )(odd, edges, rows_a, rows_b, partner_rows, partner)


def bands_kernel(
    odd_ref, n_ref, by_ref, v_ref, o_ref, p_ref, m_ref, c_ref, ra_ref, rb_ref, p2_ref,
    out_ref, band, cf, ms, sr, va, vb,
):
    own, rows, _ = o_ref.shape
    pairs = v_ref.shape[0]
    odd = odd_ref[0]
    tall = 3 * SUB
    count = 2 * tall // SUB

    def fill(at, ends, ref, *index):
        band[at, 0:SUB] = ends[0]
        band[at, SUB:tall] = ref[(*index, slice(0, 2 * SUB))]
        band[at, tall : tall + 2 * SUB] = ref[(*index, slice(rows - 2 * SUB, rows))]
        band[at, tall + 2 * SUB : 2 * tall] = ends[1]

    def received(f):
        return beyond(odd, ra_ref[f], rb_ref[f])

    def fill_pair(p, carry):
        fill(p, received(own + p), v_ref, p)
        return carry

    lax.fori_loop(0, pairs, fill_pair, 0, unroll=4)
    o_at, p_at = pairs, pairs + own
    m_at = p_at + own
    for k in range(own):
        fill(o_at + k, received(k), o_ref, k)
        fill(p_at + k, beyond(odd, p2_ref[k], p2_ref[own + k]), p_ref, k)
    fill(m_at, received(own + pairs), m_ref)
    for n in range(5):
        fill(m_at + 1 + n, received(own + pairs + 1 + n), c_ref, n)

    masks = lane_masks(odd_ref[1])
    metric = spread(band, count, m_at)
    raw = [spread(band, count, m_at + 1 + n) for n in range(5)]
    for t in range(count):
        scale = jnp.where(masks[2], 0.0, scaled_coefs([raw[n][t] for n in range(5)]))
        ms[t] = scale * metric[t]
        for n in range(5):
            cf[n, t] = scale * raw[n][t]

    def group(g, carry):
        chosen = [by_ref[g * BANDS + k] for k in range(BANDS)]
        for k, p in enumerate(chosen):
            o, q = spread(band, count, o_at + p // own), spread(band, count, p_at + p % own)
            v = spread(band, count, p)
            for t in range(count):
                sr[k, t] = ms[t] * (o[t] * q[t])
                va[k, t] = v[t]
        relax([n_ref[p] for p in chosen], count, va, vb, sr, cf, masks)
        for k, p in enumerate(chosen):
            spread_store(band, [va[k, t] for t in range(count)], p)
            out_ref[p, 0] = band[p, SUB : 2 * SUB]
            out_ref[p, 1] = band[p, tall + SUB : tall + 2 * SUB]
        return carry

    lax.fori_loop(0, pairs // BANDS, group, 0)


def bands(odd, counts, order, potentials, orbitals, partner, metric, coefficients, *received):
    own, rows, lanes = orbitals.shape
    pairs = potentials.shape[0]
    count = 6
    some = pltpu.VMEM((BANDS, count, SUB, lanes), jnp.float32)
    return pl.pallas_call(
        bands_kernel,
        out_shape=f32(pairs, 2, SUB, lanes),
        in_specs=[SMEM] * 3 + [VMEM] * 8,
        out_specs=VMEM,
        scratch_shapes=[
            pltpu.VMEM((pairs + 2 * own + 6, count * SUB, lanes), jnp.float32),
            pltpu.VMEM((5, count, SUB, lanes), jnp.float32),
            pltpu.VMEM((count, SUB, lanes), jnp.float32),
            some,
            some,
            some,
        ],
        compiler_params=params(),
        name="bands",
    )(odd, counts, order, potentials, orbitals, partner, metric, coefficients, *received)


def finish_kernel(sides, odd_ref, n_ref, inner_ref, ends_ref, o_ref, p_ref, e_ref, *refs):
    recv = refs[:sides]
    v_ref, home_ref, back_ref = refs[sides : sides + 3]
    st, cf, ms, sr, va, vb, sv, full, sems = refs[sides + 3 :]
    own, rows, _ = o_ref.shape
    groups, tall, _ = e_ref.shape
    count = tall // SUB
    lane = lane_of()
    block = lane // STRIP

    for side in range(sides):
        left_own = odd_ref[1] == side
        within = lane_of(tall) % STRIP
        from_own = jnp.where(left_own, within, STRIP - 1 - within) < STRIP // 2
        for g in range(groups):
            st[g] = jnp.where(from_own, e_ref[g], recv[side][g])
        first_group, second_group = spread(st, count, own + 1), spread(st, count, own + 2)
        for t in range(count):
            cs = [replicated(first_group[t], 1 + n) for n in range(3)]
            cs += [replicated(second_group[t], n) for n in range(2)]
            scale = scaled_coefs(cs)
            ms[t] = scale * replicated(first_group[t], 0)
            for n in range(5):
                cf[n, t] = scale * cs[n]
        o, q = spread(st, count, 0), spread(st, count, groups - 1)
        for t in range(count):
            weighted = ms[t] * q[t]
            for g in range(own):
                sr[g, t] = replicated(o[t], g) * weighted
        steps = []
        for g in range(own):
            for t, value in enumerate(spread(st, count, 1 + g)):
                va[g, t] = value
            n = jnp.zeros((SUB, LANES), jnp.int32)
            for k in range(own):
                n = jnp.where(block == k, n_ref[g * own + k], n)
            steps.append(n)

        def body(turn, carry):
            for s in range(2):
                keep = [n > 2 * turn + s for n in steps]
                sweep(own, count, (va, vb)[s], (vb, va)[s], sr, cf, keep=keep)
            return carry

        lax.fori_loop(0, SWEEPS // 2, body, 0)
        for g in range(own):
            spread_store(sv, [va[g, t] for t in range(count)], side * own + g)

    def merge(r, carry):
        at = pl.multiple_of(r * SUB, SUB)
        o = [o_ref[k, pl.ds(at, SUB)] for k in range(own)]
        q = [p_ref[k, pl.ds(at, SUB)] for k in range(own)]
        home, back = [0.0] * own, [0.0] * own
        for first in range(own):
            strips = [sv[side * own + first, pl.ds(at + SUB, SUB)] for side in range(sides)]
            for second in range(own):
                p = first * own + second
                value = inner_ref[p, pl.ds(at, SUB)]
                value = jnp.where(r == 0, ends_ref[p, 0], value)
                value = jnp.where(r == rows // SUB - 1, ends_ref[p, 1], value)
                for side in range(sides):
                    right = odd_ref[1] == side
                    edge = jnp.where(right, LANES - 1 - lane, lane) < HALO
                    turned = pltpu.roll(
                        strips[side], (-(STRIP * second + STRIP // 2)) % LANES, 1
                    )
                    value = jnp.where(edge, turned, value)
                full[p, pl.ds(at, SUB)] = value
                home[first] = home[first] + value * q[second]
                back[second] = back[second] + value * o[first]
        for k in range(own):
            home_ref[k, pl.ds(at, SUB)] = o[k] - step_size * home[k]
            back_ref[k, pl.ds(at, SUB)] = back[k]
        copy_out(r).start()
        return carry

    def copy_out(r):
        at = pl.multiple_of(r * SUB, SUB)
        return pltpu.make_async_copy(
            full.at[:, pl.ds(at, SUB), :], v_ref.at[:, pl.ds(at, SUB), :], sems.at[r]
        )

    lax.fori_loop(0, rows // SUB, merge, 0)

    def finished(r, carry):
        copy_out(r).wait()
        return carry

    lax.fori_loop(0, rows // SUB, finished, 0)


def finish(odd, counts, inner, ends, orbitals, partner, edges, received):
    own, rows, lanes = orbitals.shape
    sides = len(received)
    groups, tall, _ = edges.shape
    count = tall // SUB
    strips = pltpu.VMEM((own, count, SUB, lanes), jnp.float32)
    return pl.pallas_call(
        functools.partial(finish_kernel, sides),
        out_shape=(f32(*inner.shape), f32(*orbitals.shape), f32(*orbitals.shape)),
        in_specs=[SMEM] * 2 + [VMEM] * (5 + sides),
        out_specs=(ANY, VMEM, VMEM),
        scratch_shapes=[
            pltpu.VMEM((groups, tall, lanes), jnp.float32),
            pltpu.VMEM((5, count, SUB, lanes), jnp.float32),
            pltpu.VMEM((count, SUB, lanes), jnp.float32),
            strips,
            strips,
            strips,
            pltpu.VMEM((sides * own, tall, lanes), jnp.float32),
            pltpu.VMEM(inner.shape, jnp.float32),
            pltpu.SemaphoreType.DMA((rows // SUB,)),
        ],
        compiler_params=params(),
        name="finish",
    )(odd, counts, inner, ends, orbitals, partner, edges, *received)


def norm_kernel(home_ref, recv_ref, m_ref, upd_ref, norm_ref):
    own = home_ref.shape[0]
    norm_ref[...] = jnp.zeros_like(norm_ref)
    for k in range(own):
        updated = home_ref[k] - step_size * recv_ref[k]
        upd_ref[k] = updated
        weighted = m_ref[...] * updated * updated
        norm_ref[k : k + 1] = jnp.sum(weighted, axis=0, keepdims=True)


def partial_norms(home, received, metric):
    own, _, lanes = home.shape
    return pl.pallas_call(
        norm_kernel,
        out_shape=(f32(*home.shape), f32(-(-own // SUB) * SUB, lanes)),
        in_specs=[VMEM] * 3,
        out_specs=(VMEM, VMEM),
        compiler_params=params(),
        name="partial_norms",
    )(home, received, metric)


def scale_kernel(cells, upd_ref, norm_ref, other_ref, out_ref):
    for k in range(upd_ref.shape[0]):
        total = norm_ref[k : k + 1] + other_ref[k : k + 1]
        norm = jnp.sum(total, axis=1, keepdims=True)
        out_ref[k] = upd_ref[k] * jnp.sqrt(cells / norm)


def rescaled(updated, norms, others, cells):
    return pl.pallas_call(
        functools.partial(scale_kernel, float(cells)),
        out_shape=f32(*updated.shape),
        in_specs=[VMEM] * 3,
        out_specs=VMEM,
        compiler_params=params(),
        name="rescaled",
    )(updated, norms, others)


def shifted(value, axis, by):
    size = lax.axis_size(axis)
    return lax.ppermute(value, axis, [(i, (i + by) % size) for i in range(size)])


def pair_swaps(size):
    even = [(i, i + 1) for i in range(0, size - 1, 2)]
    odd = [(i, i + 1) for i in range(1, size - 1, 2)]
    return [p + [(b, a) for a, b in p] for p in (even, odd)]


def by_count(counts):
    at = jnp.arange(counts.shape[0], dtype=jnp.int32)
    more = counts[None] > counts[:, None]
    tie = (counts[None] == counts[:, None]) & (at[None] < at[:, None])
    rank = jnp.sum((more | tie).astype(jnp.int32), axis=1)
    return jnp.sum(jnp.where(rank[None] == at[:, None], at[None], 0), axis=1)


def local(orbitals, potentials, coefficients, metric, sweep_counts):
    own, rows, lanes = orbitals.shape
    gx, gy = lax.axis_size("gx"), lax.axis_size("gy")
    odd = jnp.stack([lax.axis_index("gx") % 2, lax.axis_index("gy") % 2]).astype(jnp.int32)
    order = by_count(sweep_counts)
    col_swaps = [p for p in pair_swaps(gy) if p]
    row_swaps = pair_swaps(gx)
    half = potentials.shape[0] // GROUP // 2

    partner = shifted(orbitals, "orb", 1)
    pay_a, pay_b = row_payloads(odd, orbitals, potentials, metric, coefficients)
    rows_a = lax.ppermute(pay_a, "gx", row_swaps[0])
    ready = prepare(odd, potentials, orbitals, metric, coefficients)
    pay_b, ready = lax.optimization_barrier((pay_b, ready))
    rows_b = lax.ppermute(pay_b, "gx", row_swaps[1])
    inner = interior(half, 0, odd, sweep_counts, order, ready, partner)
    beside = jnp.concatenate([rows_a[:own], rows_b[:own]], 0)
    beside, inner = lax.optimization_barrier((beside, inner))
    partner_rows = shifted(beside, "orb", 1)
    inner = interior(half, half, odd, sweep_counts, order, ready, partner, inner)
    partner_rows, inner = lax.optimization_barrier((partner_rows, inner))
    edges = tall_edges(odd, ready[3], rows_a, rows_b, partner_rows, partner)
    received = [lax.ppermute(edges, "gy", swap) for swap in col_swaps]
    ends = bands(
        odd, sweep_counts, order, potentials, orbitals, partner, metric, coefficients,
        rows_a, rows_b, partner_rows,
    )
    fields, home, back = finish(
        odd, sweep_counts, inner, ends, orbitals, partner, edges, received
    )
    updated, norms = partial_norms(home, shifted(back, "orb", -1), metric)
    hops = [("gy", 1 << k) for k in range(gy.bit_length() - 1)]
    hops += [("gx", 1 << k) for k in range(gx.bit_length() - 1)]
    for at, (axis, by) in enumerate(hops):
        size = lax.axis_size(axis)
        other = lax.ppermute(norms, axis, [(i, i ^ by) for i in range(size)])
        if at < len(hops) - 1:
            norms = norms + other
    return (rescaled(updated, norms, other, rows * lanes * gx * gy), fields)


def solution(mesh):
    return jax.shard_map(
        local,
        mesh=mesh,
        in_specs=(
            P("orb", "gx", "gy"),
            P("orb", "gx", "gy"),
            P(None, "gx", "gy"),
            P("gx", "gy"),
            P("orb"),
        ),
        out_specs=(P("orb", "gx", "gy"), P("orb", "gx", "gy")),
        check_vma=False,
    )
```

```python
import functools

import jax
import jax.numpy as jnp
from jax import lax
from jax.experimental import pallas as pl
from jax.experimental.pallas import tpu as pltpu
from jax.sharding import PartitionSpec as P

SWEEPS = 8

relaxation = 0.8
screening = 0.02
step_size = 0.1

LANES = 128
SUB = 8
HALO = 8
STRIP = 32
LEAST = 4
GROUP = 4
BANDS = 8
AHEAD = 16
VMEM_LIMIT = 40 * 1024 * 1024

VMEM = pl.BlockSpec(memory_space=pltpu.VMEM)
SMEM = pl.BlockSpec(memory_space=pltpu.SMEM)
ANY = pl.BlockSpec(memory_space=pl.ANY)
HBM = pl.BlockSpec(memory_space=pltpu.HBM)


def f32(*shape):
    return jax.ShapeDtypeStruct(shape, jnp.float32)


def params(limit=VMEM_LIMIT):
    return pltpu.CompilerParams(vmem_limit_bytes=limit)


def lane_of(rows=SUB):
    return lax.broadcasted_iota(jnp.int32, (rows, LANES), 1)


def packed(fields):
    rows = fields[0].shape[0]
    block = lane_of(rows) // STRIP
    out = jnp.zeros((rows, LANES), jnp.float32)
    for at, value in enumerate(fields):
        turned = pltpu.roll(value, (STRIP * at + STRIP // 2) % LANES, 1)
        out = jnp.where(block == at, turned, out)
    return out


def replicated(value, at):
    one = jnp.where(lane_of(value.shape[0]) // STRIP == at, value, 0.0)
    one = one + pltpu.roll(one, STRIP, 1)
    return one + pltpu.roll(one, 2 * STRIP, 1)


def spread(ref, count, *index):
    return [ref[(*index, pl.ds(t, SUB, stride=count), slice(None))] for t in range(count)]


def spread_store(ref, values, *index):
    count = len(values)
    for t, value in enumerate(values):
        ref[(*index, pl.ds(t, SUB, stride=count), slice(None))] = value


def scaled_coefs(coefs):
    total = coefs[0] + coefs[1] + coefs[2] + coefs[3] + 4.0 * coefs[4]
    diagonal = (1.0 + screening) * total
    return relaxation / jnp.where(diagonal == 0.0, 1.0, diagonal)


def sweep(fields, count, old, new, source, coefs, west=None, east=None, dead=None, keep=None):
    held, to_east, to_west, slopes = {}, {}, {}, {}

    def issue(k, t):
        value = old[k, t]
        held[k, t] = value
        e, w = pltpu.roll(value, LANES - 1, 1), pltpu.roll(value, 1, 1)
        if west is not None:
            w, e = jnp.where(west, 0.0, w), jnp.where(east, 0.0, e)
        to_east[k, t], to_west[k, t] = e, w

    def field(k, t):
        return held[k, t]

    def slope(k, t):
        if (k, t) not in slopes:
            slopes[k, t] = to_east[k, t] - to_west[k, t]
        return slopes[k, t]

    def above(get, k, t):
        return get(k, t - 1) if t else pltpu.roll(get(k, count - 1), 1, 0)

    def below(get, k, t):
        return get(k, t + 1) if t < count - 1 else pltpu.roll(get(k, 0), SUB - 1, 0)

    order = []
    for k in range(fields):
        order += [(k, count - 1)] + [(k, t) for t in range(count - 1)]
    done = 0
    for at in range(fields * count):
        k, t = divmod(at, count)
        until = min(len(order), max(at + AHEAD, k * count + min(t + 3, count)))
        while done < until:
            issue(*order[done])
            done += 1
        value = (1.0 - relaxation) * field(k, t) + source[k, t]
        value = value + coefs[0, t] * above(field, k, t) + coefs[1, t] * below(field, k, t)
        value = value + coefs[2, t] * to_east[k, t] + coefs[3, t] * to_west[k, t]
        value = value + coefs[4, t] * (above(slope, k, t) - below(slope, k, t))
        if dead is not None:
            value = jnp.where(dead, 0.0, value)
        if keep is not None:
            value = jnp.where(keep[k], value, field(k, t))
        new[k, t] = value


def relax(steps, count, here, there, source, coefs, masks):
    fields = len(steps)
    west, east, dead = masks
    pair = (here, there)
    sweep(fields, count, here, there, source, coefs, west, east, dead)
    for s in range(1, LEAST):
        sweep(fields, count, pair[s % 2], pair[1 - s % 2], source, coefs)
    top = functools.reduce(jnp.maximum, steps)

    def body(turn, carry):
        for s in range(2):
            at = LEAST + 2 * turn + s
            keep = [jnp.full((SUB, LANES), n, jnp.int32) > at for n in steps]
            sweep(fields, count, pair[s], pair[1 - s], source, coefs, keep=keep)
        return carry

    lax.fori_loop(0, (top - LEAST + 1) // 2, body, 0)


def lane_masks(odd):
    lane = lane_of()
    west = (lane == 0) & (odd == 0)
    east = (lane == LANES - 1) & (odd == 1)
    dead = lane == (1 - odd) * (LANES - 1)
    return west, east, dead


def prepare_kernel(odd_ref, v_ref, o_ref, m_ref, c_ref, vs_ref, om_ref, cf_ref, e_ref):
    own, rows, _ = o_ref.shape
    count = rows // SUB
    e_ref[0] = packed([o_ref[k] for k in range(own)])
    for first in range(own):
        e_ref[1 + first] = packed([v_ref[first * own + k] for k in range(own)])
    e_ref[1 + own] = packed([m_ref[...], c_ref[0], c_ref[1], c_ref[2]])
    e_ref[2 + own] = packed([c_ref[3], c_ref[4]])
    dead = lane_masks(odd_ref[1])[2]
    metric = spread(m_ref, count)
    raw = [spread(c_ref, count, n) for n in range(5)]
    weights = []
    for t in range(count):
        scale = jnp.where(dead, 0.0, scaled_coefs([raw[n][t] for n in range(5)]))
        weights.append(scale * metric[t])
        for n in range(5):
            cf_ref[n, t] = scale * raw[n][t]
    for k in range(own):
        for t, value in enumerate(spread(o_ref, count, k)):
            om_ref[k, t] = weights[t] * value

    def one(p, carry):
        for t, value in enumerate(spread(v_ref, count, p)):
            vs_ref[p, t] = value
        return carry

    lax.fori_loop(0, v_ref.shape[0], one, 0)


def prepare(odd, potentials, orbitals, metric, coefficients):
    own, rows, lanes = orbitals.shape
    count = rows // SUB
    return pl.pallas_call(
        prepare_kernel,
        out_shape=(
            f32(potentials.shape[0], count, SUB, lanes),
            f32(own, count, SUB, lanes),
            f32(5, count, SUB, lanes),
            f32(own + 3, rows, lanes),
        ),
        in_specs=[SMEM] + [VMEM] * 4,
        out_specs=(VMEM,) * 4,
        compiler_params=params(),
        name="prepare",
    )(odd, potentials, orbitals, metric, coefficients)


def rows_kernel(par_ref, o_ref, v_ref, m_ref, c_ref, pay_a, pay_b, sems):
    rows = o_ref.shape[1]
    odd = par_ref[0]
    copies = []
    for pay, start in ((pay_a, (1 - odd) * (rows - HALO)), (pay_b, odd * (rows - HALO))):
        start = pl.multiple_of(start, HALO)
        at = 0
        for ref in (o_ref, v_ref, m_ref, c_ref):
            count = ref.shape[0]
            copy = pltpu.make_async_copy(
                ref.at[:, pl.ds(start, HALO), :], pay.at[pl.ds(at, count)], sems.at[len(copies)]
            )
            copy.start()
            copies.append(copy)
            at += count
    for copy in copies:
        copy.wait()


def row_payloads(odd, orbitals, potentials, metric, coefficients):
    own, _, lanes = orbitals.shape
    fields = own + potentials.shape[0] + 1 + coefficients.shape[0]
    return pl.pallas_call(
        rows_kernel,
        out_shape=(f32(fields, HALO, lanes),) * 2,
        in_specs=[SMEM] + [HBM] * 4,
        out_specs=(ANY, ANY),
        scratch_shapes=[pltpu.SemaphoreType.DMA((8,))],
        compiler_params=params(),
        name="row_payloads",
    )(odd, orbitals, potentials, metric[None], coefficients)


def interior_kernel(groups, before, odd_ref, n_ref, by_ref, vs_ref, om_ref, cf_ref, p_ref, *refs):
    out_ref, qs, sr, va, vb = refs[-5:]
    own, count = om_ref.shape[:2]
    masks = lane_masks(odd_ref[1])
    if before:
        earlier = refs[0]

        def keep(k, carry):
            out_ref[by_ref[k]] = earlier[by_ref[k]]
            return carry

        lax.fori_loop(0, before * GROUP, keep, 0)
    for k in range(own):
        for t, value in enumerate(spread(p_ref, count, k)):
            qs[k, t] = value

    def group(g, carry):
        pairs = [by_ref[g * GROUP + k] for k in range(GROUP)]
        for k, p in enumerate(pairs):
            first, second = p // own, p % own
            for t in range(count):
                sr[k, t] = om_ref[first, t] * qs[second, t]
                va[k, t] = vs_ref[p, t]
        relax([n_ref[p] for p in pairs], count, va, vb, sr, cf_ref, masks)
        for k, p in enumerate(pairs):
            spread_store(out_ref, [va[k, t] for t in range(count)], p)
        return carry

    lax.fori_loop(before, before + groups, group, 0)


def interior(groups, before, odd, counts, order, ready, partner, *earlier):
    spread_v, weighted, coefs, _ = ready
    pairs, count, _, lanes = spread_v.shape
    own, rows, _ = partner.shape
    four = pltpu.VMEM((GROUP, count, SUB, lanes), jnp.float32)
    return pl.pallas_call(
        functools.partial(interior_kernel, groups, before),
        out_shape=f32(pairs, rows, lanes),
        in_specs=[SMEM] * 3 + [VMEM] * (4 + len(earlier)),
        out_specs=VMEM,
        scratch_shapes=[pltpu.VMEM((own, count, SUB, lanes), jnp.float32), four, four, four],
        compiler_params=params(),
        name=f"interior{before}",
    )(odd, counts, order, spread_v, weighted, coefs, partner, *earlier)


def beyond(odd_ref, a, b):
    low_is_a = odd_ref[0] == 1
    b = jnp.where(odd_ref[2] == 1, b, 0.0)
    return jnp.where(low_is_a, a, b), jnp.where(low_is_a, b, a)


def edges_kernel(odd_ref, e_ref, ra_ref, rb_ref, p2_ref, p_ref, out_ref):
    own, rows, _ = p_ref.shape
    groups = e_ref.shape[0]
    for g in range(groups):
        out_ref[g, SUB : SUB + rows] = e_ref[g]
    out_ref[groups, SUB : SUB + rows] = packed([p_ref[k] for k in range(own)])
    pairs = own * own
    ends = [beyond(odd_ref, ra_ref[f], rb_ref[f]) for f in range(own + pairs + 6)]
    ends += [beyond(odd_ref, p2_ref[k], p2_ref[own + k]) for k in range(own)]
    lists = [range(own)] + [range(own * (1 + k), own * (2 + k)) for k in range(own)]
    at = own + pairs
    lists += [range(at, at + 4), range(at + 4, at + 6), range(at + 6, at + 6 + own)]
    for g, fields in enumerate(lists):
        out_ref[g, 0:SUB] = packed([ends[f][0] for f in fields])
        out_ref[g, SUB + rows :] = packed([ends[f][1] for f in fields])


def tall_edges(odd, edges, rows_a, rows_b, partner_rows, partner):
    groups, rows, lanes = edges.shape
    return pl.pallas_call(
        edges_kernel,
        out_shape=f32(groups + 1, rows + 2 * SUB, lanes),
        in_specs=[SMEM] + [VMEM] * 5,
        out_specs=VMEM,
        compiler_params=params(),
        name="tall_edges",
    )(odd, edges, rows_a, rows_b, partner_rows, partner)


def bands_kernel(
    odd_ref, n_ref, by_ref, v_ref, o_ref, p_ref, m_ref, c_ref, ra_ref, rb_ref, p2_ref,
    out_ref, band, cf, ms, sr, va, vb,
):
    own, rows, _ = o_ref.shape
    pairs = v_ref.shape[0]
    tall = 3 * SUB
    count = 2 * tall // SUB

    def fill(at, ends, ref, *index):
        band[at, 0:SUB] = ends[0]
        band[at, SUB:tall] = ref[(*index, slice(0, 2 * SUB))]
        band[at, tall : tall + 2 * SUB] = ref[(*index, slice(rows - 2 * SUB, rows))]
        band[at, tall + 2 * SUB : 2 * tall] = ends[1]

    def received(f):
        return beyond(odd_ref, ra_ref[f], rb_ref[f])

    def fill_pair(p, carry):
        fill(p, received(own + p), v_ref, p)
        return carry

    lax.fori_loop(0, pairs, fill_pair, 0, unroll=4)
    o_at, p_at = pairs, pairs + own
    m_at = p_at + own
    for k in range(own):
        fill(o_at + k, received(k), o_ref, k)
        fill(p_at + k, beyond(odd_ref, p2_ref[k], p2_ref[own + k]), p_ref, k)
    fill(m_at, received(own + pairs), m_ref)
    for n in range(5):
        fill(m_at + 1 + n, received(own + pairs + 1 + n), c_ref, n)

    masks = lane_masks(odd_ref[1])
    metric = spread(band, count, m_at)
    raw = [spread(band, count, m_at + 1 + n) for n in range(5)]
    for t in range(count):
        scale = jnp.where(masks[2], 0.0, scaled_coefs([raw[n][t] for n in range(5)]))
        ms[t] = scale * metric[t]
        for n in range(5):
            cf[n, t] = scale * raw[n][t]

    def group(g, carry):
        chosen = [by_ref[g * BANDS + k] for k in range(BANDS)]
        for k, p in enumerate(chosen):
            o, q = spread(band, count, o_at + p // own), spread(band, count, p_at + p % own)
            v = spread(band, count, p)
            for t in range(count):
                sr[k, t] = ms[t] * (o[t] * q[t])
                va[k, t] = v[t]
        relax([n_ref[p] for p in chosen], count, va, vb, sr, cf, masks)
        for k, p in enumerate(chosen):
            spread_store(band, [va[k, t] for t in range(count)], p)
            out_ref[p, 0] = band[p, SUB : 2 * SUB]
            out_ref[p, 1] = band[p, tall + SUB : tall + 2 * SUB]
        return carry

    lax.fori_loop(0, pairs // BANDS, group, 0)


def bands(odd, counts, order, potentials, orbitals, partner, metric, coefficients, *received):
    own, rows, lanes = orbitals.shape
    pairs = potentials.shape[0]
    count = 6
    some = pltpu.VMEM((BANDS, count, SUB, lanes), jnp.float32)
    return pl.pallas_call(
        bands_kernel,
        out_shape=f32(pairs, 2, SUB, lanes),
        in_specs=[SMEM] * 3 + [VMEM] * 8,
        out_specs=VMEM,
        scratch_shapes=[
            pltpu.VMEM((pairs + 2 * own + 6, count * SUB, lanes), jnp.float32),
            pltpu.VMEM((5, count, SUB, lanes), jnp.float32),
            pltpu.VMEM((count, SUB, lanes), jnp.float32),
            some,
            some,
            some,
        ],
        compiler_params=params(),
        name="bands",
    )(odd, counts, order, potentials, orbitals, partner, metric, coefficients, *received)


def finish_kernel(sides, odd_ref, n_ref, inner_ref, ends_ref, o_ref, p_ref, e_ref, *refs):
    recv = refs[:sides]
    v_ref, home_ref, back_ref = refs[sides : sides + 3]
    st, cf, ms, sr, va, vb, sv, full, sems = refs[sides + 3 :]
    own, rows, _ = o_ref.shape
    groups, tall, _ = e_ref.shape
    count = tall // SUB
    lane = lane_of()
    block = lane // STRIP

    for side in range(sides):
        left_own = odd_ref[1] == side
        within = lane_of(tall) % STRIP
        from_own = jnp.where(left_own, within, STRIP - 1 - within) < STRIP // 2
        for g in range(groups):
            st[g] = jnp.where(from_own, e_ref[g], recv[side][g])
        first_group, second_group = spread(st, count, own + 1), spread(st, count, own + 2)
        for t in range(count):
            cs = [replicated(first_group[t], 1 + n) for n in range(3)]
            cs += [replicated(second_group[t], n) for n in range(2)]
            scale = scaled_coefs(cs)
            ms[t] = scale * replicated(first_group[t], 0)
            for n in range(5):
                cf[n, t] = scale * cs[n]
        o, q = spread(st, count, 0), spread(st, count, groups - 1)
        for t in range(count):
            weighted = ms[t] * q[t]
            for g in range(own):
                sr[g, t] = replicated(o[t], g) * weighted
        steps = []
        for g in range(own):
            for t, value in enumerate(spread(st, count, 1 + g)):
                va[g, t] = value
            n = jnp.zeros((SUB, LANES), jnp.int32)
            for k in range(own):
                n = jnp.where(block == k, n_ref[g * own + k], n)
            steps.append(n)

        def body(turn, carry):
            for s in range(2):
                keep = [n > 2 * turn + s for n in steps]
                sweep(own, count, (va, vb)[s], (vb, va)[s], sr, cf, keep=keep)
            return carry

        lax.fori_loop(0, SWEEPS // 2, body, 0)
        for g in range(own):
            spread_store(sv, [va[g, t] for t in range(count)], side * own + g)

    def merge(r, carry):
        at = pl.multiple_of(r * SUB, SUB)
        o = [o_ref[k, pl.ds(at, SUB)] for k in range(own)]
        q = [p_ref[k, pl.ds(at, SUB)] for k in range(own)]
        home, back = [0.0] * own, [0.0] * own
        for first in range(own):
            strips = [sv[side * own + first, pl.ds(at + SUB, SUB)] for side in range(sides)]
            for second in range(own):
                p = first * own + second
                value = inner_ref[p, pl.ds(at, SUB)]
                value = jnp.where(r == 0, ends_ref[p, 0], value)
                value = jnp.where(r == rows // SUB - 1, ends_ref[p, 1], value)
                for side in range(sides):
                    right = odd_ref[1] == side
                    edge = jnp.where(right, LANES - 1 - lane, lane) < HALO
                    turned = pltpu.roll(
                        strips[side], (-(STRIP * second + STRIP // 2)) % LANES, 1
                    )
                    value = jnp.where(edge, turned, value)
                full[p, pl.ds(at, SUB)] = value
                home[first] = home[first] + value * q[second]
                back[second] = back[second] + value * o[first]
        for k in range(own):
            home_ref[k, pl.ds(at, SUB)] = o[k] - step_size * home[k]
            back_ref[k, pl.ds(at, SUB)] = back[k]
        copy_out(r).start()
        return carry

    def copy_out(r):
        at = pl.multiple_of(r * SUB, SUB)
        return pltpu.make_async_copy(
            full.at[:, pl.ds(at, SUB), :], v_ref.at[:, pl.ds(at, SUB), :], sems.at[r]
        )

    lax.fori_loop(0, rows // SUB, merge, 0, unroll=4)

    def finished(r, carry):
        copy_out(r).wait()
        return carry

    lax.fori_loop(0, rows // SUB, finished, 0)


def finish(odd, counts, inner, ends, orbitals, partner, edges, received):
    own, rows, lanes = orbitals.shape
    sides = len(received)
    groups, tall, _ = edges.shape
    count = tall // SUB
    strips = pltpu.VMEM((own, count, SUB, lanes), jnp.float32)
    return pl.pallas_call(
        functools.partial(finish_kernel, sides),
        out_shape=(f32(*inner.shape), f32(*orbitals.shape), f32(*orbitals.shape)),
        in_specs=[SMEM] * 2 + [VMEM] * (5 + sides),
        out_specs=(ANY, VMEM, VMEM),
        scratch_shapes=[
            pltpu.VMEM((groups, tall, lanes), jnp.float32),
            pltpu.VMEM((5, count, SUB, lanes), jnp.float32),
            pltpu.VMEM((count, SUB, lanes), jnp.float32),
            strips,
            strips,
            strips,
            pltpu.VMEM((sides * own, tall, lanes), jnp.float32),
            pltpu.VMEM(inner.shape, jnp.float32),
            pltpu.SemaphoreType.DMA((rows // SUB,)),
        ],
        compiler_params=params(),
        name="finish",
    )(odd, counts, inner, ends, orbitals, partner, edges, *received)


def norm_kernel(home_ref, recv_ref, m_ref, upd_ref, norm_ref):
    own = home_ref.shape[0]
    norm_ref[...] = jnp.zeros_like(norm_ref)
    for k in range(own):
        updated = home_ref[k] - step_size * recv_ref[k]
        upd_ref[k] = updated
        weighted = m_ref[...] * updated * updated
        norm_ref[k : k + 1] = jnp.sum(weighted, axis=0, keepdims=True)


def partial_norms(home, received, metric):
    own, _, lanes = home.shape
    return pl.pallas_call(
        norm_kernel,
        out_shape=(f32(*home.shape), f32(-(-own // SUB) * SUB, lanes)),
        in_specs=[VMEM] * 3,
        out_specs=(VMEM, VMEM),
        compiler_params=params(),
        name="partial_norms",
    )(home, received, metric)


def scale_kernel(cells, upd_ref, norm_ref, other_ref, out_ref):
    for k in range(upd_ref.shape[0]):
        total = norm_ref[k : k + 1] + other_ref[k : k + 1]
        norm = jnp.sum(total, axis=1, keepdims=True)
        out_ref[k] = upd_ref[k] * jnp.sqrt(cells / norm)


def rescaled(updated, norms, others, cells):
    return pl.pallas_call(
        functools.partial(scale_kernel, float(cells)),
        out_shape=f32(*updated.shape),
        in_specs=[VMEM] * 3,
        out_specs=VMEM,
        compiler_params=params(),
        name="rescaled",
    )(updated, norms, others)


def shifted(value, axis, by):
    size = lax.axis_size(axis)
    return lax.ppermute(value, axis, [(i, (i + by) % size) for i in range(size)])


def pair_swaps(size):
    even = [(i, i + 1) for i in range(0, size - 1, 2)]
    odd = [(i, i + 1) for i in range(1, size - 1, 2)]
    return [p + [(b, a) for a, b in p] for p in (even, odd)]


def row_swap(swap, gx, gy):
    to = dict(swap)
    pairs = []
    for i in range(gx):
        for j in range(gy):
            pairs.append((i * gy + j, to[i] * gy + j if i in to else i * gy + (j ^ 1)))
    return pairs


def norm_hops(gx, gy):
    hops = [[(i, i ^ (1 << k)) for i in range(gx * gy)] for k in range(gy.bit_length() - 1)]
    for k in range(gx.bit_length() - 1):
        hops.append([(i, i ^ (gy << k) ^ 1) for i in range(gx * gy)])
    return hops


def by_count(counts):
    at = jnp.arange(counts.shape[0], dtype=jnp.int32)
    more = counts[None] > counts[:, None]
    tie = (counts[None] == counts[:, None]) & (at[None] < at[:, None])
    rank = jnp.sum((more | tie).astype(jnp.int32), axis=1)
    return jnp.sum(jnp.where(rank[None] == at[:, None], at[None], 0), axis=1)


def local(orbitals, potentials, coefficients, metric, sweep_counts):
    own, rows, lanes = orbitals.shape
    gx, gy = lax.axis_size("gx"), lax.axis_size("gy")
    row_at = lax.axis_index("gx")
    inside = (row_at > 0) & (row_at < gx - 1)
    odd = jnp.stack([row_at % 2, lax.axis_index("gy") % 2, inside]).astype(jnp.int32)
    order = by_count(sweep_counts)
    col_swaps = [p for p in pair_swaps(gy) if p]
    row_swaps = [row_swap(p, gx, gy) for p in pair_swaps(gx)]
    half = potentials.shape[0] // GROUP // 2

    partner = shifted(orbitals, "orb", 1)
    pay_a, pay_b = row_payloads(odd, orbitals, potentials, metric, coefficients)
    rows_a = lax.ppermute(pay_a, ("gx", "gy"), row_swaps[0])
    ready = prepare(odd, potentials, orbitals, metric, coefficients)
    pay_b, ready = lax.optimization_barrier((pay_b, ready))
    rows_b = lax.ppermute(pay_b, ("gx", "gy"), row_swaps[1])
    inner = interior(half, 0, odd, sweep_counts, order, ready, partner)
    rows_a, rows_b, inner = lax.optimization_barrier((rows_a, rows_b, inner))
    beside = jnp.concatenate([rows_a[:own], rows_b[:own]], 0)
    partner_rows = shifted(beside, "orb", 1)
    inner = interior(half, half, odd, sweep_counts, order, ready, partner, inner)
    partner_rows, inner = lax.optimization_barrier((partner_rows, inner))
    edges = tall_edges(odd, ready[3], rows_a, rows_b, partner_rows, partner)
    received = [lax.ppermute(edges, "gy", swap) for swap in col_swaps]
    ends = bands(
        odd, sweep_counts, order, potentials, orbitals, partner, metric, coefficients,
        rows_a, rows_b, partner_rows,
    )
    fields, home, back = finish(
        odd, sweep_counts, inner, ends, orbitals, partner, edges, received
    )
    updated, norms = partial_norms(home, shifted(back, "orb", -1), metric)
    hops = norm_hops(gx, gy)
    for at, hop in enumerate(hops):
        other = lax.ppermute(norms, ("gx", "gy"), hop)
        if at < len(hops) - 1:
            norms = norms + other
    return (rescaled(updated, norms, other, rows * lanes * gx * gy), fields)


def solution(mesh):
    return jax.shard_map(
        local,
        mesh=mesh,
        in_specs=(
            P("orb", "gx", "gy"),
            P("orb", "gx", "gy"),
            P(None, "gx", "gy"),
            P("gx", "gy"),
            P("orb"),
        ),
        out_specs=(P("orb", "gx", "gy"), P("orb", "gx", "gy")),
        check_vma=False,
    )
```

```python
import functools

import jax
import jax.numpy as jnp
from jax import lax
from jax.experimental import pallas as pl
from jax.experimental.pallas import tpu as pltpu
from jax.sharding import PartitionSpec as P

SWEEPS = 8

relaxation = 0.8
screening = 0.02
step_size = 0.1

LANES = 128
SUB = 8
HALO = 8
STRIP = 32
BLOCKS = LANES // STRIP
LEAST = 4
GROUP = 4
BANDS = 8
AHEAD = 16
VMEM_LIMIT = 40 * 1024 * 1024

VMEM = pl.BlockSpec(memory_space=pltpu.VMEM)
SMEM = pl.BlockSpec(memory_space=pltpu.SMEM)
ANY = pl.BlockSpec(memory_space=pl.ANY)
HBM = pl.BlockSpec(memory_space=pltpu.HBM)


def f32(*shape):
    return jax.ShapeDtypeStruct(shape, jnp.float32)


def params(limit=VMEM_LIMIT):
    return pltpu.CompilerParams(vmem_limit_bytes=limit)


def lane_of(rows=SUB):
    return lax.broadcasted_iota(jnp.int32, (rows, LANES), 1)


def packed(fields):
    rows = fields[0].shape[0]
    block = lane_of(rows) // STRIP
    out = jnp.zeros((rows, LANES), jnp.float32)
    for at, value in enumerate(fields):
        turned = pltpu.roll(value, (STRIP * at + STRIP // 2) % LANES, 1)
        out = jnp.where(block == at, turned, out)
    return out


def replicated(value, at):
    one = jnp.where(lane_of(value.shape[0]) // STRIP == at, value, 0.0)
    one = one + pltpu.roll(one, STRIP, 1)
    return one + pltpu.roll(one, 2 * STRIP, 1)


def spread(ref, count, *index):
    return [ref[(*index, pl.ds(t, SUB, stride=count), slice(None))] for t in range(count)]


def spread_store(ref, values, *index):
    count = len(values)
    for t, value in enumerate(values):
        ref[(*index, pl.ds(t, SUB, stride=count), slice(None))] = value


def scaled_coefs(coefs):
    total = coefs[0] + coefs[1] + coefs[2] + coefs[3] + 4.0 * coefs[4]
    diagonal = (1.0 + screening) * total
    return relaxation / jnp.where(diagonal == 0.0, 1.0, diagonal)


def sweep(fields, count, old, new, source, coefs, west=None, east=None, dead=None, keep=None):
    held, to_east, to_west, slopes = {}, {}, {}, {}

    def issue(k, t):
        value = old[k, t]
        held[k, t] = value
        e, w = pltpu.roll(value, LANES - 1, 1), pltpu.roll(value, 1, 1)
        if west is not None:
            w, e = jnp.where(west, 0.0, w), jnp.where(east, 0.0, e)
        to_east[k, t], to_west[k, t] = e, w

    def field(k, t):
        return held[k, t]

    def slope(k, t):
        if (k, t) not in slopes:
            slopes[k, t] = to_east[k, t] - to_west[k, t]
        return slopes[k, t]

    def above(get, k, t):
        return get(k, t - 1) if t else pltpu.roll(get(k, count - 1), 1, 0)

    def below(get, k, t):
        return get(k, t + 1) if t < count - 1 else pltpu.roll(get(k, 0), SUB - 1, 0)

    order = []
    for k in range(fields):
        order += [(k, count - 1)] + [(k, t) for t in range(count - 1)]
    done = 0
    for at in range(fields * count):
        k, t = divmod(at, count)
        until = min(len(order), max(at + AHEAD, k * count + min(t + 3, count)))
        while done < until:
            issue(*order[done])
            done += 1
        value = (1.0 - relaxation) * field(k, t) + source[k, t]
        value = value + coefs[0, t] * above(field, k, t) + coefs[1, t] * below(field, k, t)
        value = value + coefs[2, t] * to_east[k, t] + coefs[3, t] * to_west[k, t]
        value = value + coefs[4, t] * (above(slope, k, t) - below(slope, k, t))
        if dead is not None:
            value = jnp.where(dead, 0.0, value)
        if keep is not None:
            value = jnp.where(keep[k], value, field(k, t))
        new[k, t] = value


def relax(steps, count, here, there, source, coefs, masks):
    fields = len(steps)
    west, east, dead = masks
    pair = (here, there)
    sweep(fields, count, here, there, source, coefs, west, east, dead)
    for s in range(1, LEAST):
        sweep(fields, count, pair[s % 2], pair[1 - s % 2], source, coefs)
    top = functools.reduce(jnp.maximum, steps)

    def body(turn, carry):
        for s in range(2):
            at = LEAST + 2 * turn + s
            keep = [jnp.full((SUB, LANES), n, jnp.int32) > at for n in steps]
            sweep(fields, count, pair[s], pair[1 - s], source, coefs, keep=keep)
        return carry

    lax.fori_loop(0, (top - LEAST + 1) // 2, body, 0)


def lane_masks(odd):
    lane = lane_of()
    west = (lane == 0) & (odd == 0)
    east = (lane == LANES - 1) & (odd == 1)
    dead = lane == (1 - odd) * (LANES - 1)
    return west, east, dead


def prepare_kernel(odd_ref, v_hbm, o_hbm, m_hbm, c_hbm, *refs):
    vs_ref, os_ref, om_ref, cf_ref, e_ref, v_ref, o_ref, m_ref, c_ref, sems = refs
    own, rows, _ = o_ref.shape
    count = rows // SUB
    copies = [
        pltpu.make_async_copy(source, target, sems.at[at])
        for at, (source, target) in enumerate(((m_hbm, m_ref), (c_hbm, c_ref), (o_hbm, o_ref)))
    ]
    for first in range(own):
        part = pl.ds(first * own, own)
        copies.append(pltpu.make_async_copy(v_hbm.at[part], v_ref.at[part], sems.at[3 + first]))
    for copy in copies:
        copy.start()
    copies[0].wait()
    copies[1].wait()
    e_ref[1 + own] = packed([m_ref[...], c_ref[0], c_ref[1], c_ref[2]])
    e_ref[2 + own] = packed([c_ref[3], c_ref[4]])
    dead = lane_masks(odd_ref[1])[2]
    metric = spread(m_ref, count)
    raw = [spread(c_ref, count, n) for n in range(5)]
    weights = []
    for t in range(count):
        scale = jnp.where(dead, 0.0, scaled_coefs([raw[n][t] for n in range(5)]))
        weights.append(scale * metric[t])
        for n in range(5):
            cf_ref[n, t] = scale * raw[n][t]
    copies[2].wait()
    e_ref[0] = packed([o_ref[k] for k in range(own)])
    for k in range(own):
        for t, value in enumerate(spread(o_ref, count, k)):
            os_ref[k, t] = value
            om_ref[k, t] = weights[t] * value
    for first in range(own):
        copies[3 + first].wait()
        e_ref[1 + first] = packed([v_ref[first * own + k] for k in range(own)])
        for k in range(own):
            for t, value in enumerate(spread(v_ref, count, first * own + k)):
                vs_ref[first * own + k, t] = value


def prepare(odd, potentials, orbitals, metric, coefficients):
    own, rows, lanes = orbitals.shape
    count = rows // SUB
    arrays = (potentials, orbitals, metric, coefficients)
    return pl.pallas_call(
        prepare_kernel,
        out_shape=(
            f32(potentials.shape[0], count, SUB, lanes),
            f32(own, count, SUB, lanes),
            f32(own, count, SUB, lanes),
            f32(5, count, SUB, lanes),
            f32(own + 3, rows, lanes),
        ),
        in_specs=[SMEM] + [HBM] * 4,
        out_specs=(VMEM,) * 5,
        scratch_shapes=[pltpu.VMEM(a.shape, jnp.float32) for a in arrays]
        + [pltpu.SemaphoreType.DMA((3 + own,))],
        compiler_params=params(),
        name="prepare",
    )(odd, *arrays)


def rows_kernel(par_ref, o_ref, v_ref, m_ref, c_ref, pay_a, pay_b, sems):
    rows = o_ref.shape[1]
    odd = par_ref[0]
    copies = []
    for pay, start in ((pay_a, (1 - odd) * (rows - HALO)), (pay_b, odd * (rows - HALO))):
        start = pl.multiple_of(start, HALO)
        at = 0
        for ref in (o_ref, v_ref, m_ref, c_ref):
            count = ref.shape[0]
            copy = pltpu.make_async_copy(
                ref.at[:, pl.ds(start, HALO), :], pay.at[pl.ds(at, count)], sems.at[len(copies)]
            )
            copy.start()
            copies.append(copy)
            at += count
    for copy in copies:
        copy.wait()


def row_payloads(odd, orbitals, potentials, metric, coefficients):
    own, _, lanes = orbitals.shape
    fields = own + potentials.shape[0] + 1 + coefficients.shape[0]
    return pl.pallas_call(
        rows_kernel,
        out_shape=(f32(fields, HALO, lanes),) * 2,
        in_specs=[SMEM] + [HBM] * 4,
        out_specs=(ANY, ANY),
        scratch_shapes=[pltpu.SemaphoreType.DMA((8,))],
        compiler_params=params(),
        name="row_payloads",
    )(odd, orbitals, potentials, metric[None], coefficients)


def interior_kernel(groups, before, last, odd_ref, n_ref, by_ref, *refs):
    vs_ref, os_ref, om_ref, cf_ref, p_ref = refs[:5]
    out_ref, back_ref, back, qs, sr, va, vb = refs[-7:]
    own, count = om_ref.shape[:2]
    masks = lane_masks(odd_ref[1])
    if before:
        earlier, back_before = refs[5:7]

        def keep(k, carry):
            out_ref[by_ref[k]] = earlier[by_ref[k]]
            return carry

        lax.fori_loop(0, before * GROUP, keep, 0)
        back[...] = back_before[...]
    else:
        back[...] = jnp.zeros_like(back)
    for k in range(own):
        for t, value in enumerate(spread(p_ref, count, k)):
            qs[k, t] = value

    def group(g, carry):
        pairs = [by_ref[g * GROUP + k] for k in range(GROUP)]
        for k, p in enumerate(pairs):
            first, second = p // own, p % own
            for t in range(count):
                sr[k, t] = om_ref[first, t] * qs[second, t]
                va[k, t] = vs_ref[p, t]
        relax([n_ref[p] for p in pairs], count, va, vb, sr, cf_ref, masks)
        for k, p in enumerate(pairs):
            first, second = p // own, p % own
            spread_store(out_ref, [va[k, t] for t in range(count)], p)
            for t in range(count):
                back[second, t] = back[second, t] + va[k, t] * os_ref[first, t]
        return carry

    lax.fori_loop(before, before + groups, group, 0)
    for k in range(own):
        if last:
            spread_store(back_ref, [back[k, t] for t in range(count)], k)
        else:
            back_ref[k] = back[k]


def interior(groups, before, last, odd, counts, order, ready, partner, *earlier):
    pairs, count, _, lanes = ready[0].shape
    own, rows, _ = partner.shape
    four = pltpu.VMEM((GROUP, count, SUB, lanes), jnp.float32)
    each = pltpu.VMEM((own, count, SUB, lanes), jnp.float32)
    back = f32(own, rows, lanes) if last else f32(own, count, SUB, lanes)
    return pl.pallas_call(
        functools.partial(interior_kernel, groups, before, last),
        out_shape=(f32(pairs, rows, lanes), back),
        in_specs=[SMEM] * 3 + [VMEM] * (5 + len(earlier)),
        out_specs=(VMEM, VMEM),
        scratch_shapes=[each, each, four, four, four],
        compiler_params=params(),
        name=f"interior{before}",
    )(odd, counts, order, *ready[:4], partner, *earlier)


def beyond(odd_ref, a, b):
    low_is_a = odd_ref[0] == 1
    b = jnp.where(odd_ref[2] == 1, b, 0.0)
    return jnp.where(low_is_a, a, b), jnp.where(low_is_a, b, a)


def edges_kernel(odd_ref, e_ref, ra_ref, rb_ref, p2_ref, p_ref, out_ref):
    own, rows, _ = p_ref.shape
    groups = e_ref.shape[0]
    for g in range(groups):
        out_ref[g, SUB : SUB + rows] = e_ref[g]
    out_ref[groups, SUB : SUB + rows] = packed([p_ref[k] for k in range(own)])
    pairs = own * own
    ends = [beyond(odd_ref, ra_ref[f], rb_ref[f]) for f in range(own + pairs + 6)]
    ends += [beyond(odd_ref, p2_ref[k], p2_ref[own + k]) for k in range(own)]
    lists = [range(own)] + [range(own * (1 + k), own * (2 + k)) for k in range(own)]
    at = own + pairs
    lists += [range(at, at + 4), range(at + 4, at + 6), range(at + 6, at + 6 + own)]
    for g, fields in enumerate(lists):
        out_ref[g, 0:SUB] = packed([ends[f][0] for f in fields])
        out_ref[g, SUB + rows :] = packed([ends[f][1] for f in fields])


def tall_edges(odd, edges, rows_a, rows_b, partner_rows, partner):
    groups, rows, lanes = edges.shape
    return pl.pallas_call(
        edges_kernel,
        out_shape=f32(groups + 1, rows + 2 * SUB, lanes),
        in_specs=[SMEM] + [VMEM] * 5,
        out_specs=VMEM,
        compiler_params=params(),
        name="tall_edges",
    )(odd, edges, rows_a, rows_b, partner_rows, partner)


def bands_kernel(
    odd_ref, n_ref, by_ref, v_ref, o_ref, p_ref, m_ref, c_ref, ra_ref, rb_ref, p2_ref,
    out_ref, back_ref, band, cf, ms, sr, va, vb,
):
    own, rows, _ = o_ref.shape
    pairs = v_ref.shape[0]
    tall = 3 * SUB
    count = 2 * tall // SUB

    def fill(at, ends, ref, *index):
        band[at, 0:SUB] = ends[0]
        band[at, SUB:tall] = ref[(*index, slice(0, 2 * SUB))]
        band[at, tall : tall + 2 * SUB] = ref[(*index, slice(rows - 2 * SUB, rows))]
        band[at, tall + 2 * SUB : 2 * tall] = ends[1]

    def received(f):
        return beyond(odd_ref, ra_ref[f], rb_ref[f])

    def fill_pair(p, carry):
        fill(p, received(own + p), v_ref, p)
        return carry

    lax.fori_loop(0, pairs, fill_pair, 0, unroll=4)
    o_at, p_at = pairs, pairs + own
    m_at = p_at + own
    for k in range(own):
        fill(o_at + k, received(k), o_ref, k)
        fill(p_at + k, beyond(odd_ref, p2_ref[k], p2_ref[own + k]), p_ref, k)
    fill(m_at, received(own + pairs), m_ref)
    for n in range(5):
        fill(m_at + 1 + n, received(own + pairs + 1 + n), c_ref, n)

    masks = lane_masks(odd_ref[1])
    metric = spread(band, count, m_at)
    raw = [spread(band, count, m_at + 1 + n) for n in range(5)]
    for t in range(count):
        scale = jnp.where(masks[2], 0.0, scaled_coefs([raw[n][t] for n in range(5)]))
        ms[t] = scale * metric[t]
        for n in range(5):
            cf[n, t] = scale * raw[n][t]

    def group(g, carry):
        chosen = [by_ref[g * BANDS + k] for k in range(BANDS)]
        for k, p in enumerate(chosen):
            o, q = spread(band, count, o_at + p // own), spread(band, count, p_at + p % own)
            v = spread(band, count, p)
            for t in range(count):
                sr[k, t] = ms[t] * (o[t] * q[t])
                va[k, t] = v[t]
        relax([n_ref[p] for p in chosen], count, va, vb, sr, cf, masks)
        for k, p in enumerate(chosen):
            spread_store(band, [va[k, t] for t in range(count)], p)
            out_ref[p, 0] = band[p, SUB : 2 * SUB]
            out_ref[p, 1] = band[p, tall + SUB : tall + 2 * SUB]
        return carry

    lax.fori_loop(0, pairs // BANDS, group, 0)
    for end, start in enumerate((0, rows - SUB)):
        o = [o_ref[k, start : start + SUB] for k in range(own)]
        for second in range(own):
            terms = [out_ref[first * own + second, end] * o[first] for first in range(own)]
            back_ref[end * own + second] = sum(terms[1:], terms[0])


def bands(odd, counts, order, potentials, orbitals, partner, metric, coefficients, *received):
    own, rows, lanes = orbitals.shape
    pairs = potentials.shape[0]
    count = 6
    some = pltpu.VMEM((BANDS, count, SUB, lanes), jnp.float32)
    return pl.pallas_call(
        bands_kernel,
        out_shape=(f32(pairs, 2, SUB, lanes), f32(2 * own, SUB, lanes)),
        in_specs=[SMEM] * 3 + [VMEM] * 8,
        out_specs=(VMEM, VMEM),
        scratch_shapes=[
            pltpu.VMEM((pairs + 2 * own + 6, count * SUB, lanes), jnp.float32),
            pltpu.VMEM((5, count, SUB, lanes), jnp.float32),
            pltpu.VMEM((count, SUB, lanes), jnp.float32),
            some,
            some,
            some,
        ],
        compiler_params=params(),
        name="bands",
    )(odd, counts, order, potentials, orbitals, partner, metric, coefficients, *received)


def strip_place(odd_ref, side):
    left_own = odd_ref[1] == side
    in_strip = jnp.where(left_own, HALO, STRIP // 2)
    in_block = jnp.where(left_own, LANES - HALO, 0)
    return left_own, in_strip, in_block


def strips_kernel(sides, odd_ref, n_ref, rows_ref, e_ref, *refs):
    recv = refs[:sides]
    pay_ref, sv_ref, st, cf, ms, orep, sr, va, vb, flat = refs[sides:]
    own = n_ref.shape[0] // BLOCKS
    groups, tall, _ = e_ref.shape
    rows = tall - 2 * SUB
    count = tall // SUB
    lane = lane_of()
    block = lane // STRIP
    lead = rows_ref.shape[0]
    fold = rows // SUB // BLOCKS
    pay_ref[0:lead] = rows_ref[...]

    for side in range(sides):
        left_own, in_strip, _ = strip_place(odd_ref, side)
        within = lane_of(tall) % STRIP
        from_own = jnp.where(left_own, within, STRIP - 1 - within) < STRIP // 2
        for g in range(groups):
            st[g] = jnp.where(from_own, e_ref[g], recv[side][g])
        first_group, second_group = spread(st, count, own + 1), spread(st, count, own + 2)
        for t in range(count):
            cs = [replicated(first_group[t], 1 + n) for n in range(3)]
            cs += [replicated(second_group[t], n) for n in range(2)]
            scale = scaled_coefs(cs)
            ms[t] = scale * replicated(first_group[t], 0)
            for n in range(5):
                cf[n, t] = scale * cs[n]
        o, q = spread(st, count, 0), spread(st, count, groups - 1)
        for t in range(count):
            weighted = ms[t] * q[t]
            for g in range(own):
                alone = replicated(o[t], g)
                orep[g, t] = alone
                sr[g, t] = alone * weighted
        steps = []
        for g in range(own):
            for t, value in enumerate(spread(st, count, 1 + g)):
                va[g, t] = value
            n = jnp.zeros((SUB, LANES), jnp.int32)
            for k in range(own):
                n = jnp.where(block == k, n_ref[g * own + k], n)
            steps.append(n)

        def body(turn, carry):
            for s in range(2):
                keep = [n > 2 * turn + s for n in steps]
                sweep(own, count, (va, vb)[s], (vb, va)[s], sr, cf, keep=keep)
            return carry

        lax.fori_loop(0, SWEEPS // 2, body, 0)
        back = []
        for t in range(count):
            terms = [va[g, t] * orep[g, t] for g in range(own)]
            back.append(sum(terms[1:], terms[0]))
        spread_store(flat, back)
        for g in range(own):
            spread_store(sv_ref, [va[g, t] for t in range(count)], side * own + g)
        for v in range(fold):
            out = jnp.zeros((SUB, LANES), jnp.float32)
            for g in range(BLOCKS):
                at = SUB + (g * fold + v) * SUB
                shift = (HALO * g - in_strip) % LANES
                turned = pltpu.roll(flat[at : at + SUB], shift, 1)
                out = jnp.where(lane % STRIP // HALO == g, turned, out)
            pay_ref[lead + side * fold + v] = out


def strips(odd, counts, band_back, edges, received):
    sides = len(received)
    groups, tall, lanes = edges.shape
    own = counts.shape[0] // BLOCKS
    count = tall // SUB
    fold = (tall - 2 * SUB) // SUB // BLOCKS
    each = pltpu.VMEM((own, count, SUB, lanes), jnp.float32)
    return pl.pallas_call(
        functools.partial(strips_kernel, sides),
        out_shape=(
            f32(band_back.shape[0] + sides * fold, SUB, lanes),
            f32(sides * own, tall, lanes),
        ),
        in_specs=[SMEM] * 2 + [VMEM] * (2 + sides),
        out_specs=(VMEM, VMEM),
        scratch_shapes=[
            pltpu.VMEM((groups, tall, lanes), jnp.float32),
            pltpu.VMEM((5, count, SUB, lanes), jnp.float32),
            pltpu.VMEM((count, SUB, lanes), jnp.float32),
            each,
            each,
            each,
            each,
            pltpu.VMEM((tall, lanes), jnp.float32),
        ],
        compiler_params=params(),
        name="strips",
    )(odd, counts, band_back, edges, *received)


def merge_kernel(sides, odd_ref, inner_ref, ends_ref, sv_ref, o_ref, p_ref, *refs):
    v_ref, home_ref, full, sems = refs
    own, rows, _ = o_ref.shape
    lane = lane_of()

    def copy_out(r):
        at = pl.multiple_of(r * SUB, SUB)
        return pltpu.make_async_copy(
            full.at[:, pl.ds(at, SUB), :], v_ref.at[:, pl.ds(at, SUB), :], sems.at[r]
        )

    def merge(r, carry):
        at = pl.multiple_of(r * SUB, SUB)
        q = [p_ref[k, pl.ds(at, SUB)] for k in range(own)]
        home = [0.0] * own
        for first in range(own):
            strips = [sv_ref[side * own + first, pl.ds(at + SUB, SUB)] for side in range(sides)]
            for second in range(own):
                p = first * own + second
                value = inner_ref[p, pl.ds(at, SUB)]
                value = jnp.where(r == 0, ends_ref[p, 0], value)
                value = jnp.where(r == rows // SUB - 1, ends_ref[p, 1], value)
                for side in range(sides):
                    right = odd_ref[1] == side
                    edge = jnp.where(right, LANES - 1 - lane, lane) < HALO
                    turned = pltpu.roll(
                        strips[side], (-(STRIP * second + STRIP // 2)) % LANES, 1
                    )
                    value = jnp.where(edge, turned, value)
                full[p, pl.ds(at, SUB)] = value
                home[first] = home[first] + value * q[second]
        for k in range(own):
            home_ref[k, pl.ds(at, SUB)] = o_ref[k, pl.ds(at, SUB)] - step_size * home[k]
        copy_out(r).start()
        return carry

    lax.fori_loop(0, rows // SUB, merge, 0, unroll=4)

    def finished(r, carry):
        copy_out(r).wait()
        return carry

    lax.fori_loop(0, rows // SUB, finished, 0)


def merged(odd, inner, ends, strip_fields, orbitals, partner):
    own, rows, _ = orbitals.shape
    sides = strip_fields.shape[0] // own
    return pl.pallas_call(
        functools.partial(merge_kernel, sides),
        out_shape=(f32(*inner.shape), f32(*orbitals.shape)),
        in_specs=[SMEM] + [VMEM] * 5,
        out_specs=(ANY, VMEM),
        scratch_shapes=[
            pltpu.VMEM(inner.shape, jnp.float32),
            pltpu.SemaphoreType.DMA((rows // SUB,)),
        ],
        compiler_params=params(),
        name="merge",
    )(odd, inner, ends, strip_fields, orbitals, partner)


def norm_kernel(odd_ref, home_ref, recv_ref, edge_ref, m_ref, upd_ref, norm_ref):
    own, rows, _ = home_ref.shape
    lane = lane_of()
    fold = rows // SUB // BLOCKS
    lead = 2 * own
    sides = (edge_ref.shape[0] - lead) // fold
    norm_ref[...] = jnp.zeros_like(norm_ref)
    for k in range(own):
        total = jnp.zeros((SUB, LANES), jnp.float32)
        for r in range(rows // SUB):
            at = r * SUB
            value = recv_ref[k, at : at + SUB]
            if r == 0:
                value = edge_ref[k]
            if r == rows // SUB - 1:
                value = edge_ref[own + k]
            g, v = divmod(r, fold)
            for side in range(sides):
                left_own, _, in_block = strip_place(odd_ref, side)
                edge = jnp.where(left_own, LANES - 1 - lane, lane) < HALO
                shift = (in_block - STRIP * k - HALO * g) % LANES
                turned = pltpu.roll(edge_ref[lead + side * fold + v], shift, 1)
                value = jnp.where(edge, turned, value)
            updated = home_ref[k, at : at + SUB] - step_size * value
            upd_ref[k, at : at + SUB] = updated
            total = total + m_ref[at : at + SUB] * updated * updated
        norm_ref[k : k + 1] = jnp.sum(total, axis=0, keepdims=True)


def partial_norms(odd, home, received, edge_terms, metric):
    own, _, lanes = home.shape
    return pl.pallas_call(
        norm_kernel,
        out_shape=(f32(*home.shape), f32(-(-own // SUB) * SUB, lanes)),
        in_specs=[SMEM] + [VMEM] * 4,
        out_specs=(VMEM, VMEM),
        compiler_params=params(),
        name="partial_norms",
    )(odd, home, received, edge_terms, metric)


def scale_kernel(cells, upd_ref, norm_ref, other_ref, out_ref):
    for k in range(upd_ref.shape[0]):
        total = norm_ref[k : k + 1] + other_ref[k : k + 1]
        norm = jnp.sum(total, axis=1, keepdims=True)
        out_ref[k] = upd_ref[k] * jnp.sqrt(cells / norm)


def rescaled(updated, norms, others, cells):
    return pl.pallas_call(
        functools.partial(scale_kernel, float(cells)),
        out_shape=f32(*updated.shape),
        in_specs=[VMEM] * 3,
        out_specs=VMEM,
        compiler_params=params(),
        name="rescaled",
    )(updated, norms, others)


def shifted(value, axis, by):
    size = lax.axis_size(axis)
    return lax.ppermute(value, axis, [(i, (i + by) % size) for i in range(size)])


def pair_swaps(size):
    even = [(i, i + 1) for i in range(0, size - 1, 2)]
    odd = [(i, i + 1) for i in range(1, size - 1, 2)]
    return [p + [(b, a) for a, b in p] for p in (even, odd)]


def row_swap(swap, gx, gy):
    to = dict(swap)
    pairs = []
    for i in range(gx):
        for j in range(gy):
            pairs.append((i * gy + j, to[i] * gy + j if i in to else i * gy + (j ^ 1)))
    return pairs


def norm_hops(gx, gy):
    hops = [[(i, i ^ (1 << k)) for i in range(gx * gy)] for k in range(gy.bit_length() - 1)]
    for k in range(gx.bit_length() - 1):
        hops.append([(i, i ^ (gy << k) ^ 1) for i in range(gx * gy)])
    return hops


def by_count(counts):
    at = jnp.arange(counts.shape[0], dtype=jnp.int32)
    more = counts[None] > counts[:, None]
    tie = (counts[None] == counts[:, None]) & (at[None] < at[:, None])
    rank = jnp.sum((more | tie).astype(jnp.int32), axis=1)
    return jnp.sum(jnp.where(rank[None] == at[:, None], at[None], 0), axis=1)


def local(orbitals, potentials, coefficients, metric, sweep_counts):
    own, rows, lanes = orbitals.shape
    gx, gy = lax.axis_size("gx"), lax.axis_size("gy")
    row_at = lax.axis_index("gx")
    inside = (row_at > 0) & (row_at < gx - 1)
    odd = jnp.stack([row_at % 2, lax.axis_index("gy") % 2, inside]).astype(jnp.int32)
    order = by_count(sweep_counts)
    col_swaps = [p for p in pair_swaps(gy) if p]
    row_swaps = [row_swap(p, gx, gy) for p in pair_swaps(gx)]
    half = potentials.shape[0] // GROUP // 2

    partner = shifted(orbitals, "orb", 1)
    pay_a, pay_b = row_payloads(odd, orbitals, potentials, metric, coefficients)
    rows_a = lax.ppermute(pay_a, ("gx", "gy"), row_swaps[0])
    ready = prepare(odd, potentials, orbitals, metric, coefficients)
    pay_b, ready = lax.optimization_barrier((pay_b, ready))
    rows_b = lax.ppermute(pay_b, ("gx", "gy"), row_swaps[1])
    inner = interior(half, 0, False, odd, sweep_counts, order, ready, partner)
    rows_a, rows_b, inner = lax.optimization_barrier((rows_a, rows_b, inner))
    beside = jnp.concatenate([rows_a[:own], rows_b[:own]], 0)
    partner_rows = shifted(beside, "orb", 1)
    inner, back = interior(half, half, True, odd, sweep_counts, order, ready, partner, *inner)
    partner_rows, inner, back = lax.optimization_barrier((partner_rows, inner, back))
    early = shifted(back, "orb", -1)
    edges = tall_edges(odd, ready[4], rows_a, rows_b, partner_rows, partner)
    received = [lax.ppermute(edges, "gy", swap) for swap in col_swaps]
    ends, band_back = bands(
        odd, sweep_counts, order, potentials, orbitals, partner, metric, coefficients,
        rows_a, rows_b, partner_rows,
    )
    edge_back, strip_fields = strips(odd, sweep_counts, band_back, edges, received)
    edge_terms = shifted(edge_back, "orb", -1)
    fields, home = merged(odd, inner, ends, strip_fields, orbitals, partner)
    updated, norms = partial_norms(odd, home, early, edge_terms, metric)
    hops = norm_hops(gx, gy)
    for at, hop in enumerate(hops):
        other = lax.ppermute(norms, ("gx", "gy"), hop)
        if at < len(hops) - 1:
            norms = norms + other
    return (rescaled(updated, norms, other, rows * lanes * gx * gy), fields)


def solution(mesh):
    return jax.shard_map(
        local,
        mesh=mesh,
        in_specs=(
            P("orb", "gx", "gy"),
            P("orb", "gx", "gy"),
            P(None, "gx", "gy"),
            P("gx", "gy"),
            P("orb"),
        ),
        out_specs=(P("orb", "gx", "gy"), P("orb", "gx", "gy")),
        check_vma=False,
    )
```

```python
import functools

import jax
import jax.numpy as jnp
from jax import lax
from jax.experimental import pallas as pl
from jax.experimental.pallas import tpu as pltpu
from jax.sharding import PartitionSpec as P

SWEEPS = 8

relaxation = 0.8
screening = 0.02
step_size = 0.1

LANES = 128
SUB = 8
HALO = 8
STRIP = 32
BLOCKS = LANES // STRIP
LEAST = 4
GROUP = 4
BANDS = 8
AHEAD = 16
VMEM_LIMIT = 40 * 1024 * 1024

VMEM = pl.BlockSpec(memory_space=pltpu.VMEM)
SMEM = pl.BlockSpec(memory_space=pltpu.SMEM)
ANY = pl.BlockSpec(memory_space=pl.ANY)
HBM = pl.BlockSpec(memory_space=pltpu.HBM)


def f32(*shape):
    return jax.ShapeDtypeStruct(shape, jnp.float32)


def params():
    return pltpu.CompilerParams(vmem_limit_bytes=VMEM_LIMIT)


def cost(microseconds):
    return pl.CostEstimate(
        flops=0, bytes_accessed=int(microseconds * 3.7e6), transcendentals=0
    )


def lane_of(rows=SUB):
    return lax.broadcasted_iota(jnp.int32, (rows, LANES), 1)


def packed(fields):
    rows = fields[0].shape[0]
    block = lane_of(rows) // STRIP
    out = jnp.zeros((rows, LANES), jnp.float32)
    for at, value in enumerate(fields):
        turned = pltpu.roll(value, (STRIP * at + STRIP // 2) % LANES, 1)
        out = jnp.where(block == at, turned, out)
    return out


def replicated(value, at):
    one = jnp.where(lane_of(value.shape[0]) // STRIP == at, value, 0.0)
    one = one + pltpu.roll(one, STRIP, 1)
    return one + pltpu.roll(one, 2 * STRIP, 1)


def spread(ref, count, *index):
    return [ref[(*index, pl.ds(t, SUB, stride=count), slice(None))] for t in range(count)]


def spread_store(ref, values, *index):
    count = len(values)
    for t, value in enumerate(values):
        ref[(*index, pl.ds(t, SUB, stride=count), slice(None))] = value


def scaled_coefs(coefs):
    total = coefs[0] + coefs[1] + coefs[2] + coefs[3] + 4.0 * coefs[4]
    diagonal = (1.0 + screening) * total
    return relaxation / jnp.where(diagonal == 0.0, 1.0, diagonal)


def sweep(fields, count, old, new, source, coefs, west=None, east=None, dead=None, keep=None):
    held, to_east, to_west, slopes = {}, {}, {}, {}

    def issue(k, t):
        value = old[k, t]
        held[k, t] = value
        e, w = pltpu.roll(value, LANES - 1, 1), pltpu.roll(value, 1, 1)
        if west is not None:
            w, e = jnp.where(west, 0.0, w), jnp.where(east, 0.0, e)
        to_east[k, t], to_west[k, t] = e, w

    def field(k, t):
        return held[k, t]

    def slope(k, t):
        if (k, t) not in slopes:
            slopes[k, t] = to_east[k, t] - to_west[k, t]
        return slopes[k, t]

    def above(get, k, t):
        return get(k, t - 1) if t else pltpu.roll(get(k, count - 1), 1, 0)

    def below(get, k, t):
        return get(k, t + 1) if t < count - 1 else pltpu.roll(get(k, 0), SUB - 1, 0)

    order = []
    for k in range(fields):
        order += [(k, count - 1)] + [(k, t) for t in range(count - 1)]
    done = 0
    for at in range(fields * count):
        k, t = divmod(at, count)
        until = min(len(order), max(at + AHEAD, k * count + min(t + 3, count)))
        while done < until:
            issue(*order[done])
            done += 1
        value = (1.0 - relaxation) * field(k, t) + source[k, t]
        value = value + coefs[0, t] * above(field, k, t) + coefs[1, t] * below(field, k, t)
        value = value + coefs[2, t] * to_east[k, t] + coefs[3, t] * to_west[k, t]
        value = value + coefs[4, t] * (above(slope, k, t) - below(slope, k, t))
        if dead is not None:
            value = jnp.where(dead, 0.0, value)
        if keep is not None:
            value = jnp.where(keep[k], value, field(k, t))
        new[k, t] = value


def relax(steps, count, here, there, source, coefs, masks):
    fields = len(steps)
    west, east, dead = masks
    pair = (here, there)
    sweep(fields, count, here, there, source, coefs, west, east, dead)
    for s in range(1, LEAST):
        sweep(fields, count, pair[s % 2], pair[1 - s % 2], source, coefs)
    top = functools.reduce(jnp.maximum, steps)

    def body(turn, carry):
        for s in range(2):
            at = LEAST + 2 * turn + s
            keep = [jnp.full((SUB, LANES), n, jnp.int32) > at for n in steps]
            sweep(fields, count, pair[s], pair[1 - s], source, coefs, keep=keep)
        return carry

    lax.fori_loop(0, (top - LEAST + 1) // 2, body, 0)


def lane_masks(odd):
    lane = lane_of()
    west = (lane == 0) & (odd == 0)
    east = (lane == LANES - 1) & (odd == 1)
    dead = lane == (1 - odd) * (LANES - 1)
    return west, east, dead


def prepare_kernel(odd_ref, o_hbm, v_hbm, m_hbm, c_hbm, *refs):
    vs_ref, os_ref, om_ref, cf_ref, e_ref, pay_a, pay_b, o_ref, v_ref, m_ref, c_ref, sems = refs
    own, rows, _ = o_ref.shape
    pairs = v_ref.shape[0]
    count = rows // SUB
    sources = [(m_hbm, m_ref), (c_hbm, c_ref), (o_hbm, o_ref)]
    for first in range(own):
        part = pl.ds(first * own, own)
        sources.append((v_hbm.at[part], v_ref.at[part]))
    copies = [
        pltpu.make_async_copy(source, target, sems.at[at])
        for at, (source, target) in enumerate(sources)
    ]
    for copy in copies:
        copy.start()

    starts = [(1 - odd_ref[0]) * (rows - HALO), odd_ref[0] * (rows - HALO)]
    starts = [pl.multiple_of(start, HALO) for start in starts]

    def send_rows(at, ref, index):
        for pay, start in zip((pay_a, pay_b), starts):
            pay[at] = ref[index, pl.ds(start, HALO)]

    copies[0].wait()
    copies[1].wait()
    send_rows(own + pairs, m_ref, 0)
    for n in range(5):
        send_rows(own + pairs + 1 + n, c_ref, n)
    e_ref[1 + own] = packed([m_ref[0], c_ref[0], c_ref[1], c_ref[2]])
    e_ref[2 + own] = packed([c_ref[3], c_ref[4]])
    dead = lane_masks(odd_ref[1])[2]
    metric = spread(m_ref, count, 0)
    raw = [spread(c_ref, count, n) for n in range(5)]
    weights = []
    for t in range(count):
        scale = jnp.where(dead, 0.0, scaled_coefs([raw[n][t] for n in range(5)]))
        weights.append(scale * metric[t])
        for n in range(5):
            cf_ref[n, t] = scale * raw[n][t]
    copies[2].wait()
    e_ref[0] = packed([o_ref[k] for k in range(own)])
    for k in range(own):
        send_rows(k, o_ref, k)
        for t, value in enumerate(spread(o_ref, count, k)):
            os_ref[k, t] = value
            om_ref[k, t] = weights[t] * value
    for first in range(own):
        copies[3 + first].wait()
        e_ref[1 + first] = packed([v_ref[first * own + k] for k in range(own)])
        for p in range(first * own, (first + 1) * own):
            send_rows(own + p, v_ref, p)
            for t, value in enumerate(spread(v_ref, count, p)):
                vs_ref[p, t] = value


def prepare(odd, *arrays):
    orbitals, potentials, _, coefficients = arrays
    own, rows, lanes = orbitals.shape
    pairs = potentials.shape[0]
    count = rows // SUB
    inputs = [pltpu.with_memory_space_constraint(a, pltpu.HBM) for a in arrays]
    return pl.pallas_call(
        prepare_kernel,
        out_shape=(
            f32(pairs, count, SUB, lanes),
            f32(own, count, SUB, lanes),
            f32(own, count, SUB, lanes),
            f32(5, count, SUB, lanes),
            f32(own + 3, rows, lanes),
            *[f32(own + pairs + 1 + coefficients.shape[0], HALO, lanes)] * 2,
        ),
        in_specs=[SMEM] + [HBM] * 4,
        out_specs=(VMEM,) * 7,
        scratch_shapes=[pltpu.VMEM(a.shape, jnp.float32) for a in arrays]
        + [pltpu.SemaphoreType.DMA((3 + own,))],
        compiler_params=params(),
        cost_estimate=cost(2.0),
        name="prepare",
    )(odd, *inputs)


def interior_kernel(groups, before, last, odd_ref, n_ref, by_ref, *refs):
    vs_ref, os_ref, om_ref, cf_ref, p_ref = refs[:5]
    out_ref, back_ref, back, qs, sr, va, vb = refs[-7:]
    own, count = om_ref.shape[:2]
    masks = lane_masks(odd_ref[1])
    if before:
        earlier, back_before = refs[5:7]

        def keep(k, carry):
            out_ref[by_ref[k]] = earlier[by_ref[k]]
            return carry

        lax.fori_loop(0, before * GROUP, keep, 0)
        back[...] = back_before[...]
    else:
        back[...] = jnp.zeros_like(back)
    for k in range(own):
        for t, value in enumerate(spread(p_ref, count, k)):
            qs[k, t] = value

    def group(g, carry):
        pairs = [by_ref[g * GROUP + k] for k in range(GROUP)]
        for k, p in enumerate(pairs):
            first, second = p // own, p % own
            for t in range(count):
                sr[k, t] = om_ref[first, t] * qs[second, t]
                va[k, t] = vs_ref[p, t]
        relax([n_ref[p] for p in pairs], count, va, vb, sr, cf_ref, masks)
        for k, p in enumerate(pairs):
            first, second = p // own, p % own
            spread_store(out_ref, [va[k, t] for t in range(count)], p)
            for t in range(count):
                back[second, t] = back[second, t] + va[k, t] * os_ref[first, t]
        return carry

    lax.fori_loop(before, before + groups, group, 0)
    for k in range(own):
        if last:
            spread_store(back_ref, [back[k, t] for t in range(count)], k)
        else:
            back_ref[k] = back[k]


def interior(groups, before, last, odd, counts, order, ready, partner, *earlier):
    pairs, count, _, lanes = ready[0].shape
    own, rows, _ = partner.shape
    four = pltpu.VMEM((GROUP, count, SUB, lanes), jnp.float32)
    each = pltpu.VMEM((own, count, SUB, lanes), jnp.float32)
    back = f32(own, rows, lanes) if last else f32(own, count, SUB, lanes)
    return pl.pallas_call(
        functools.partial(interior_kernel, groups, before, last),
        out_shape=(f32(pairs, rows, lanes), back),
        in_specs=[SMEM] * 3 + [VMEM] * (5 + len(earlier)),
        out_specs=(VMEM, VMEM),
        scratch_shapes=[each, each, four, four, four],
        compiler_params=params(),
        cost_estimate=cost(1.8 * groups),
        name=f"interior{before}",
    )(odd, counts, order, *ready[:4], partner, *earlier)


def beyond(odd_ref, a, b):
    low_is_a = odd_ref[0] == 1
    b = jnp.where(odd_ref[2] == 1, b, 0.0)
    return jnp.where(low_is_a, a, b), jnp.where(low_is_a, b, a)


def edges_kernel(odd_ref, e_ref, ra_ref, rb_ref, p2_ref, p_ref, out_ref):
    own, rows, _ = p_ref.shape
    groups = e_ref.shape[0]
    for g in range(groups):
        out_ref[g, SUB : SUB + rows] = e_ref[g]
    out_ref[groups, SUB : SUB + rows] = packed([p_ref[k] for k in range(own)])
    pairs = own * own
    ends = [beyond(odd_ref, ra_ref[f], rb_ref[f]) for f in range(own + pairs + 6)]
    ends += [beyond(odd_ref, p2_ref[k], p2_ref[own + k]) for k in range(own)]
    lists = [range(own)] + [range(own * (1 + k), own * (2 + k)) for k in range(own)]
    at = own + pairs
    lists += [range(at, at + 4), range(at + 4, at + 6), range(at + 6, at + 6 + own)]
    for g, fields in enumerate(lists):
        out_ref[g, 0:SUB] = packed([ends[f][0] for f in fields])
        out_ref[g, SUB + rows :] = packed([ends[f][1] for f in fields])


def tall_edges(odd, edges, rows_a, rows_b, partner_rows, partner):
    groups, rows, lanes = edges.shape
    return pl.pallas_call(
        edges_kernel,
        out_shape=f32(groups + 1, rows + 2 * SUB, lanes),
        in_specs=[SMEM] + [VMEM] * 5,
        out_specs=VMEM,
        compiler_params=params(),
        cost_estimate=cost(0.7),
        name="tall_edges",
    )(odd, edges, rows_a, rows_b, partner_rows, partner)


def bands_kernel(
    odd_ref, n_ref, by_ref, v_ref, o_ref, p_ref, m_ref, c_ref, ra_ref, rb_ref, p2_ref,
    out_ref, back_ref, band, cf, ms, sr, va, vb,
):
    own, rows, _ = o_ref.shape
    pairs = v_ref.shape[0]
    tall = 3 * SUB
    count = 2 * tall // SUB

    def fill(at, ends, ref, *index):
        band[at, 0:SUB] = ends[0]
        band[at, SUB:tall] = ref[(*index, slice(0, 2 * SUB))]
        band[at, tall : tall + 2 * SUB] = ref[(*index, slice(rows - 2 * SUB, rows))]
        band[at, tall + 2 * SUB : 2 * tall] = ends[1]

    def received(f):
        return beyond(odd_ref, ra_ref[f], rb_ref[f])

    def fill_pair(p, carry):
        fill(p, received(own + p), v_ref, p)
        return carry

    lax.fori_loop(0, pairs, fill_pair, 0, unroll=4)
    o_at, p_at = pairs, pairs + own
    m_at = p_at + own
    for k in range(own):
        fill(o_at + k, received(k), o_ref, k)
        fill(p_at + k, beyond(odd_ref, p2_ref[k], p2_ref[own + k]), p_ref, k)
    fill(m_at, received(own + pairs), m_ref)
    for n in range(5):
        fill(m_at + 1 + n, received(own + pairs + 1 + n), c_ref, n)

    masks = lane_masks(odd_ref[1])
    metric = spread(band, count, m_at)
    raw = [spread(band, count, m_at + 1 + n) for n in range(5)]
    for t in range(count):
        scale = jnp.where(masks[2], 0.0, scaled_coefs([raw[n][t] for n in range(5)]))
        ms[t] = scale * metric[t]
        for n in range(5):
            cf[n, t] = scale * raw[n][t]

    def group(g, carry):
        chosen = [by_ref[g * BANDS + k] for k in range(BANDS)]
        for k, p in enumerate(chosen):
            o, q = spread(band, count, o_at + p // own), spread(band, count, p_at + p % own)
            v = spread(band, count, p)
            for t in range(count):
                sr[k, t] = ms[t] * (o[t] * q[t])
                va[k, t] = v[t]
        relax([n_ref[p] for p in chosen], count, va, vb, sr, cf, masks)
        for k, p in enumerate(chosen):
            spread_store(band, [va[k, t] for t in range(count)], p)
            out_ref[p, 0] = band[p, SUB : 2 * SUB]
            out_ref[p, 1] = band[p, tall + SUB : tall + 2 * SUB]
        return carry

    lax.fori_loop(0, pairs // BANDS, group, 0)
    for end, start in enumerate((0, rows - SUB)):
        o = [o_ref[k, start : start + SUB] for k in range(own)]
        for second in range(own):
            terms = [out_ref[first * own + second, end] * o[first] for first in range(own)]
            back_ref[end * own + second] = sum(terms[1:], terms[0])


def bands(odd, counts, order, potentials, orbitals, partner, metric, coefficients, *received):
    own, rows, lanes = orbitals.shape
    pairs = potentials.shape[0]
    count = 6
    some = pltpu.VMEM((BANDS, count, SUB, lanes), jnp.float32)
    return pl.pallas_call(
        bands_kernel,
        out_shape=(f32(pairs, 2, SUB, lanes), f32(2 * own, SUB, lanes)),
        in_specs=[SMEM] * 3 + [VMEM] * 8,
        out_specs=(VMEM, VMEM),
        scratch_shapes=[
            pltpu.VMEM((pairs + 2 * own + 6, count * SUB, lanes), jnp.float32),
            pltpu.VMEM((5, count, SUB, lanes), jnp.float32),
            pltpu.VMEM((count, SUB, lanes), jnp.float32),
            some,
            some,
            some,
        ],
        compiler_params=params(),
        cost_estimate=cost(2.5),
        name="bands",
    )(odd, counts, order, potentials, orbitals, partner, metric, coefficients, *received)


def strip_place(odd_ref, side):
    left_own = odd_ref[1] == side
    in_strip = jnp.where(left_own, HALO, STRIP // 2)
    in_block = jnp.where(left_own, LANES - HALO, 0)
    return left_own, in_strip, in_block


def strips_kernel(sides, odd_ref, n_ref, rows_ref, e_ref, *refs):
    recv = refs[:sides]
    pay_ref, sv_ref, st, cf, ms, orep, sr, va, vb, flat = refs[sides:]
    own = n_ref.shape[0] // BLOCKS
    groups, tall, _ = e_ref.shape
    rows = tall - 2 * SUB
    count = tall // SUB
    lane = lane_of()
    block = lane // STRIP
    lead = rows_ref.shape[0]
    fold = rows // SUB // BLOCKS
    pay_ref[0:lead] = rows_ref[...]

    for side in range(sides):
        left_own, in_strip, _ = strip_place(odd_ref, side)
        within = lane_of(tall) % STRIP
        from_own = jnp.where(left_own, within, STRIP - 1 - within) < STRIP // 2
        for g in range(groups):
            st[g] = jnp.where(from_own, e_ref[g], recv[side][g])
        first_group, second_group = spread(st, count, own + 1), spread(st, count, own + 2)
        for t in range(count):
            cs = [replicated(first_group[t], 1 + n) for n in range(3)]
            cs += [replicated(second_group[t], n) for n in range(2)]
            scale = scaled_coefs(cs)
            ms[t] = scale * replicated(first_group[t], 0)
            for n in range(5):
                cf[n, t] = scale * cs[n]
        o, q = spread(st, count, 0), spread(st, count, groups - 1)
        for t in range(count):
            weighted = ms[t] * q[t]
            for g in range(own):
                alone = replicated(o[t], g)
                orep[g, t] = alone
                sr[g, t] = alone * weighted
        steps = []
        for g in range(own):
            for t, value in enumerate(spread(st, count, 1 + g)):
                va[g, t] = value
            n = jnp.zeros((SUB, LANES), jnp.int32)
            for k in range(own):
                n = jnp.where(block == k, n_ref[g * own + k], n)
            steps.append(n)

        def body(turn, carry):
            for s in range(2):
                keep = [n > 2 * turn + s for n in steps]
                sweep(own, count, (va, vb)[s], (vb, va)[s], sr, cf, keep=keep)
            return carry

        lax.fori_loop(0, SWEEPS // 2, body, 0)
        back = []
        for t in range(count):
            terms = [va[g, t] * orep[g, t] for g in range(own)]
            back.append(sum(terms[1:], terms[0]))
        spread_store(flat, back)
        for g in range(own):
            spread_store(sv_ref, [va[g, t] for t in range(count)], side * own + g)
        for v in range(fold):
            out = jnp.zeros((SUB, LANES), jnp.float32)
            for g in range(BLOCKS):
                at = SUB + (g * fold + v) * SUB
                shift = (HALO * g - in_strip) % LANES
                turned = pltpu.roll(flat[at : at + SUB], shift, 1)
                out = jnp.where(lane % STRIP // HALO == g, turned, out)
            pay_ref[lead + side * fold + v] = out


def strips(odd, counts, band_back, edges, received):
    sides = len(received)
    groups, tall, lanes = edges.shape
    own = counts.shape[0] // BLOCKS
    count = tall // SUB
    fold = (tall - 2 * SUB) // SUB // BLOCKS
    each = pltpu.VMEM((own, count, SUB, lanes), jnp.float32)
    return pl.pallas_call(
        functools.partial(strips_kernel, sides),
        out_shape=(
            f32(band_back.shape[0] + sides * fold, SUB, lanes),
            f32(sides * own, tall, lanes),
        ),
        in_specs=[SMEM] * 2 + [VMEM] * (2 + sides),
        out_specs=(VMEM, VMEM),
        scratch_shapes=[
            pltpu.VMEM((groups, tall, lanes), jnp.float32),
            pltpu.VMEM((5, count, SUB, lanes), jnp.float32),
            pltpu.VMEM((count, SUB, lanes), jnp.float32),
            each,
            each,
            each,
            each,
            pltpu.VMEM((tall, lanes), jnp.float32),
        ],
        compiler_params=params(),
        cost_estimate=cost(2.9),
        name="strips",
    )(odd, counts, band_back, edges, *received)


def merge_kernel(sides, odd_ref, inner_ref, ends_ref, sv_ref, o_ref, p_ref, v_ref, home_ref):
    own, rows, _ = o_ref.shape
    lane = lane_of()

    def merge(r, carry):
        at = pl.multiple_of(r * SUB, SUB)
        q = [p_ref[k, pl.ds(at, SUB)] for k in range(own)]
        home = [0.0] * own
        for first in range(own):
            strips = [sv_ref[side * own + first, pl.ds(at + SUB, SUB)] for side in range(sides)]
            for second in range(own):
                p = first * own + second
                value = inner_ref[p, pl.ds(at, SUB)]
                value = jnp.where(r == 0, ends_ref[p, 0], value)
                value = jnp.where(r == rows // SUB - 1, ends_ref[p, 1], value)
                for side in range(sides):
                    right = odd_ref[1] == side
                    edge = jnp.where(right, LANES - 1 - lane, lane) < HALO
                    turned = pltpu.roll(
                        strips[side], (-(STRIP * second + STRIP // 2)) % LANES, 1
                    )
                    value = jnp.where(edge, turned, value)
                v_ref[p, pl.ds(at, SUB)] = value
                home[first] = home[first] + value * q[second]
        for k in range(own):
            home_ref[k, pl.ds(at, SUB)] = o_ref[k, pl.ds(at, SUB)] - step_size * home[k]
        return carry

    lax.fori_loop(0, rows // SUB, merge, 0, unroll=4)


def merged(odd, inner, ends, strip_fields, orbitals, partner):
    own, rows, _ = orbitals.shape
    sides = strip_fields.shape[0] // own
    return pl.pallas_call(
        functools.partial(merge_kernel, sides),
        out_shape=(f32(*inner.shape), f32(*orbitals.shape)),
        in_specs=[SMEM] + [VMEM] * 5,
        out_specs=(VMEM, VMEM),
        compiler_params=params(),
        cost_estimate=cost(1.2),
        name="merge",
    )(odd, inner, ends, strip_fields, orbitals, partner)


def write_kernel(v_ref, out_ref, sems):
    parts = sems.shape[0]
    size = v_ref.shape[0] // parts
    copies = []
    for k in range(parts):
        part = pl.ds(k * size, size)
        copies.append(pltpu.make_async_copy(v_ref.at[part], out_ref.at[part], sems.at[k]))
    for copy in copies:
        copy.start()
    for copy in copies:
        copy.wait()


def written(fields):
    return pl.pallas_call(
        write_kernel,
        out_shape=f32(*fields.shape),
        in_specs=[ANY],
        out_specs=ANY,
        scratch_shapes=[pltpu.SemaphoreType.DMA((4,))],
        compiler_params=params(),
        cost_estimate=cost(1.2),
        name="write",
    )(fields)


def norm_kernel(odd_ref, home_ref, recv_ref, edge_ref, m_ref, upd_ref, norm_ref):
    own, rows, _ = home_ref.shape
    lane = lane_of()
    fold = rows // SUB // BLOCKS
    lead = 2 * own
    sides = (edge_ref.shape[0] - lead) // fold
    norm_ref[...] = jnp.zeros_like(norm_ref)
    for k in range(own):
        total = jnp.zeros((SUB, LANES), jnp.float32)
        for r in range(rows // SUB):
            at = r * SUB
            value = recv_ref[k, at : at + SUB]
            if r == 0:
                value = edge_ref[k]
            if r == rows // SUB - 1:
                value = edge_ref[own + k]
            g, v = divmod(r, fold)
            for side in range(sides):
                left_own, _, in_block = strip_place(odd_ref, side)
                edge = jnp.where(left_own, LANES - 1 - lane, lane) < HALO
                shift = (in_block - STRIP * k - HALO * g) % LANES
                turned = pltpu.roll(edge_ref[lead + side * fold + v], shift, 1)
                value = jnp.where(edge, turned, value)
            updated = home_ref[k, at : at + SUB] - step_size * value
            upd_ref[k, at : at + SUB] = updated
            total = total + m_ref[at : at + SUB] * updated * updated
        norm_ref[k : k + 1] = jnp.sum(total, axis=0, keepdims=True)


def partial_norms(odd, home, received, edge_terms, metric):
    own, _, lanes = home.shape
    return pl.pallas_call(
        norm_kernel,
        out_shape=(f32(*home.shape), f32(-(-own // SUB) * SUB, lanes)),
        in_specs=[SMEM] + [VMEM] * 4,
        out_specs=(VMEM, VMEM),
        compiler_params=params(),
        cost_estimate=cost(0.7),
        name="partial_norms",
    )(odd, home, received, edge_terms, metric)


def scale_kernel(cells, upd_ref, *refs):
    out_ref = refs[-1]
    sums = functools.reduce(lambda a, b: a + b, [ref[...] for ref in refs[:-1]])
    for k in range(upd_ref.shape[0]):
        total = sums[k : k + 1]
        norm = jnp.sum(total, axis=1, keepdims=True)
        out_ref[k] = upd_ref[k] * jnp.sqrt(cells / norm)


def rescaled(updated, norms, cells):
    return pl.pallas_call(
        functools.partial(scale_kernel, float(cells)),
        out_shape=f32(*updated.shape),
        in_specs=[VMEM] * (1 + len(norms)),
        out_specs=VMEM,
        compiler_params=params(),
        cost_estimate=cost(0.8),
        name="rescaled",
    )(updated, *norms)


def shifted(value, axis, by):
    size = lax.axis_size(axis)
    return lax.ppermute(value, axis, [(i, (i + by) % size) for i in range(size)])


def pair_swaps(size):
    even = [(i, i + 1) for i in range(0, size - 1, 2)]
    odd = [(i, i + 1) for i in range(1, size - 1, 2)]
    return [p + [(b, a) for a, b in p] for p in (even, odd)]


def row_swap(swap, gx, gy):
    to = dict(swap)
    pairs = []
    for i in range(gx):
        for j in range(gy):
            pairs.append((i * gy + j, to[i] * gy + j if i in to else i * gy + (j ^ 1)))
    return pairs


def norm_hops(gx, gy):
    along = [[(i, i ^ (1 << k)) for i in range(gx * gy)] for k in range(gy.bit_length() - 1)]
    across = [[(i, i ^ (gy * k) ^ 1) for i in range(gx * gy)] for k in range(1, gx)]
    return along, across


def by_count(counts):
    at = jnp.arange(counts.shape[0], dtype=jnp.int32)
    more = counts[None] > counts[:, None]
    tie = (counts[None] == counts[:, None]) & (at[None] < at[:, None])
    rank = jnp.sum((more | tie).astype(jnp.int32), axis=1)
    return jnp.sum(jnp.where(rank[None] == at[:, None], at[None], 0), axis=1)


def local(orbitals, potentials, coefficients, metric, sweep_counts):
    own, rows, lanes = orbitals.shape
    gx, gy = lax.axis_size("gx"), lax.axis_size("gy")
    row_at = lax.axis_index("gx")
    inside = (row_at > 0) & (row_at < gx - 1)
    odd = jnp.stack([row_at % 2, lax.axis_index("gy") % 2, inside]).astype(jnp.int32)
    order = by_count(sweep_counts)
    col_swaps = [p for p in pair_swaps(gy) if p]
    row_swaps = [row_swap(p, gx, gy) for p in pair_swaps(gx)]
    groups = potentials.shape[0] // GROUP

    partner = shifted(orbitals, "orb", 1)
    *ready, edges, pay_a, pay_b = prepare(odd, orbitals, potentials, metric[None], coefficients)
    rows_a = lax.ppermute(pay_a, ("gx", "gy"), row_swaps[0])
    rows_b = lax.ppermute(pay_b, ("gx", "gy"), row_swaps[1])
    inner = interior(1, 0, False, odd, sweep_counts, order, ready, partner)
    rows_a, rows_b, inner = lax.optimization_barrier((rows_a, rows_b, inner))
    beside = jnp.concatenate([rows_a[:own], rows_b[:own]], 0)
    partner_rows = shifted(beside, "orb", 1)
    inner, back = interior(
        groups - 1, 1, True, odd, sweep_counts, order, ready, partner, *inner
    )
    partner_rows, inner, back = lax.optimization_barrier((partner_rows, inner, back))
    early = shifted(back, "orb", -1)
    edges = tall_edges(odd, edges, rows_a, rows_b, partner_rows, partner)
    received = [lax.ppermute(edges, "gy", swap) for swap in col_swaps]
    ends, band_back = bands(
        odd, sweep_counts, order, potentials, orbitals, partner, metric, coefficients,
        rows_a, rows_b, partner_rows,
    )
    edge_back, strip_fields = strips(odd, sweep_counts, band_back, edges, received)
    edge_terms = shifted(edge_back, "orb", -1)
    fields, home = merged(odd, inner, ends, strip_fields, orbitals, partner)
    updated, norms = partial_norms(odd, home, early, edge_terms, metric)
    norms, fields = lax.optimization_barrier((norms, fields))
    along, across = norm_hops(gx, gy)
    for hop in along:
        norms = norms + lax.ppermute(norms, ("gx", "gy"), hop)
    norms = [norms] + [lax.ppermute(norms, ("gx", "gy"), hop) for hop in across]
    return (rescaled(updated, norms, rows * lanes * gx * gy), written(fields))


def solution(mesh):
    return jax.shard_map(
        local,
        mesh=mesh,
        in_specs=(
            P("orb", "gx", "gy"),
            P("orb", "gx", "gy"),
            P(None, "gx", "gy"),
            P("gx", "gy"),
            P("orb"),
        ),
        out_specs=(P("orb", "gx", "gy"), P("orb", "gx", "gy")),
        check_vma=False,
    )
```

```python
import functools

import jax
import jax.numpy as jnp
from jax import lax
from jax.experimental import pallas as pl
from jax.experimental.pallas import tpu as pltpu
from jax.sharding import PartitionSpec as P

SWEEPS = 8

relaxation = 0.8
screening = 0.02
step_size = 0.1

LANES = 128
SUB = 8
HALO = 8
STRIP = 32
BLOCKS = LANES // STRIP
LEAST = 4
GROUP = 4
BANDS = 8
AHEAD = 16
VMEM_LIMIT = 16 * 1024 * 1024

VMEM = pl.BlockSpec(memory_space=pltpu.VMEM)
ANY = pl.BlockSpec(memory_space=pl.ANY)
HBM = pl.BlockSpec(memory_space=pltpu.HBM)


def f32(*shape):
    return jax.ShapeDtypeStruct(shape, jnp.float32)


def params():
    return pltpu.CompilerParams(vmem_limit_bytes=VMEM_LIMIT)


def cost(microseconds):
    return pl.CostEstimate(
        flops=0, bytes_accessed=int(microseconds * 3.7e6), transcendentals=0
    )


def place():
    row, col = lax.axis_index("gx"), lax.axis_index("gy")
    inside = (row > 0) & (row < lax.axis_size("gx") - 1)
    return row % 2, col % 2, inside


def lane_of(rows=SUB):
    return lax.broadcasted_iota(jnp.int32, (rows, LANES), 1)


def packed(fields):
    rows = fields[0].shape[0]
    block = lane_of(rows) // STRIP
    out = jnp.zeros((rows, LANES), jnp.float32)
    for at, value in enumerate(fields):
        turned = pltpu.roll(value, (STRIP * at + STRIP // 2) % LANES, 1)
        out = jnp.where(block == at, turned, out)
    return out


def replicated(value, at):
    one = jnp.where(lane_of(value.shape[0]) // STRIP == at, value, 0.0)
    one = one + pltpu.roll(one, STRIP, 1)
    return one + pltpu.roll(one, 2 * STRIP, 1)


def spread(ref, count, *index):
    return [ref[(*index, pl.ds(t, SUB, stride=count), slice(None))] for t in range(count)]


def spread_store(ref, values, *index):
    count = len(values)
    for t, value in enumerate(values):
        ref[(*index, pl.ds(t, SUB, stride=count), slice(None))] = value


def scaled_coefs(coefs):
    total = coefs[0] + coefs[1] + coefs[2] + coefs[3] + 4.0 * coefs[4]
    diagonal = (1.0 + screening) * total
    return relaxation / jnp.where(diagonal == 0.0, 1.0, diagonal)


def sweep(fields, count, old, new, source, coefs, west=None, east=None, dead=None, keep=None):
    held, to_east, to_west, slopes = {}, {}, {}, {}

    def issue(k, t):
        value = old[k, t]
        held[k, t] = value
        e, w = pltpu.roll(value, LANES - 1, 1), pltpu.roll(value, 1, 1)
        if west is not None:
            w, e = jnp.where(west, 0.0, w), jnp.where(east, 0.0, e)
        to_east[k, t], to_west[k, t] = e, w

    def field(k, t):
        return held[k, t]

    def slope(k, t):
        if (k, t) not in slopes:
            slopes[k, t] = to_east[k, t] - to_west[k, t]
        return slopes[k, t]

    def above(get, k, t):
        return get(k, t - 1) if t else pltpu.roll(get(k, count - 1), 1, 0)

    def below(get, k, t):
        return get(k, t + 1) if t < count - 1 else pltpu.roll(get(k, 0), SUB - 1, 0)

    order = []
    for k in range(fields):
        order += [(k, count - 1)] + [(k, t) for t in range(count - 1)]
    done = 0
    for at in range(fields * count):
        k, t = divmod(at, count)
        until = min(len(order), max(at + AHEAD, k * count + min(t + 3, count)))
        while done < until:
            issue(*order[done])
            done += 1
        value = (1.0 - relaxation) * field(k, t) + source[k, t]
        value = value + coefs[0, t] * above(field, k, t) + coefs[1, t] * below(field, k, t)
        value = value + coefs[2, t] * to_east[k, t] + coefs[3, t] * to_west[k, t]
        value = value + coefs[4, t] * (above(slope, k, t) - below(slope, k, t))
        if dead is not None:
            value = jnp.where(dead, 0.0, value)
        if keep is not None:
            value = jnp.where(keep[k], value, field(k, t))
        new[k, t] = value


def relax(steps, count, here, there, source, coefs, masks):
    fields = len(steps)
    west, east, dead = masks
    pair = (here, there)
    sweep(fields, count, here, there, source, coefs, west, east, dead)
    for s in range(1, LEAST):
        sweep(fields, count, pair[s % 2], pair[1 - s % 2], source, coefs)
    top = functools.reduce(jnp.maximum, steps)

    def body(turn, carry):
        for s in range(2):
            at = LEAST + 2 * turn + s
            keep = [jnp.full((SUB, LANES), n, jnp.int32) > at for n in steps]
            sweep(fields, count, pair[s], pair[1 - s], source, coefs, keep=keep)
        return carry

    lax.fori_loop(0, (top - LEAST + 1) // 2, body, 0)


def lane_masks(odd):
    lane = lane_of()
    west = (lane == 0) & (odd == 0)
    east = (lane == LANES - 1) & (odd == 1)
    dead = lane == (1 - odd) * (LANES - 1)
    return west, east, dead


def prepare_kernel(by_in, steps_in, o_hbm, v_hbm, m_hbm, c_hbm, by_ref, steps_ref, *refs):
    vs_ref, os_ref, om_ref, cf_ref, e_ref, pay_a, pay_b, o_ref, v_ref, m_ref, c_ref, sems = refs
    own, rows, _ = o_ref.shape
    pairs = v_ref.shape[0]
    count = rows // SUB
    sources = [(m_hbm, m_ref), (c_hbm, c_ref), (o_hbm, o_ref)]
    for first in range(own):
        part = pl.ds(first * own, own)
        sources.append((v_hbm.at[part], v_ref.at[part]))
    copies = [
        pltpu.make_async_copy(source, target, sems.at[at])
        for at, (source, target) in enumerate(sources)
    ]
    for copy in copies:
        copy.start()
    by_ref[...] = by_in[...]
    steps_ref[...] = steps_in[...]

    starts = [(1 - place()[0]) * (rows - HALO), place()[0] * (rows - HALO)]
    starts = [pl.multiple_of(start, HALO) for start in starts]

    def send_rows(at, ref, index):
        for pay, start in zip((pay_a, pay_b), starts):
            pay[at] = ref[index, pl.ds(start, HALO)]

    copies[0].wait()
    copies[1].wait()
    send_rows(own + pairs, m_ref, 0)
    for n in range(5):
        send_rows(own + pairs + 1 + n, c_ref, n)
    e_ref[1 + own] = packed([m_ref[0], c_ref[0], c_ref[1], c_ref[2]])
    e_ref[2 + own] = packed([c_ref[3], c_ref[4]])
    dead = lane_masks(place()[1])[2]
    metric = spread(m_ref, count, 0)
    raw = [spread(c_ref, count, n) for n in range(5)]
    weights = []
    for t in range(count):
        scale = jnp.where(dead, 0.0, scaled_coefs([raw[n][t] for n in range(5)]))
        weights.append(scale * metric[t])
        for n in range(5):
            cf_ref[n, t] = scale * raw[n][t]
    copies[2].wait()
    e_ref[0] = packed([o_ref[k] for k in range(own)])
    for k in range(own):
        send_rows(k, o_ref, k)
        for t, value in enumerate(spread(o_ref, count, k)):
            os_ref[k, t] = value
            om_ref[k, t] = weights[t] * value
    for first in range(own):
        copies[3 + first].wait()
        e_ref[1 + first] = packed([v_ref[first * own + k] for k in range(own)])
        for p in range(first * own, (first + 1) * own):
            send_rows(own + p, v_ref, p)
            for t, value in enumerate(spread(v_ref, count, p)):
                vs_ref[p, t] = value


def prepare(order, steps, *arrays):
    orbitals, potentials, _, coefficients = arrays
    own, rows, lanes = orbitals.shape
    pairs = potentials.shape[0]
    count = rows // SUB
    inputs = [pltpu.with_memory_space_constraint(a, pltpu.HBM) for a in arrays]
    return pl.pallas_call(
        prepare_kernel,
        out_shape=(
            jax.ShapeDtypeStruct(order.shape, order.dtype),
            jax.ShapeDtypeStruct(steps.shape, steps.dtype),
            f32(pairs, count, SUB, lanes),
            f32(own, count, SUB, lanes),
            f32(own, count, SUB, lanes),
            f32(5, count, SUB, lanes),
            f32(own + 3, rows, lanes),
            *[f32(own + pairs + 1 + coefficients.shape[0], HALO, lanes)] * 2,
            *[f32(*a.shape) for a in arrays],
        ),
        in_specs=[VMEM] * 2 + [HBM] * 4,
        out_specs=(VMEM,) * 13,
        scratch_shapes=[pltpu.SemaphoreType.DMA((3 + own,))],
        compiler_params=params(),
        cost_estimate=cost(2.0),
        name="prepare",
    )(order, steps, *inputs)


def interior_kernel(groups, before, last, by_any, *refs):
    vs_ref, os_ref, om_ref, cf_ref, p_ref = refs[:5]
    out_ref, back_ref, back, qs, sr, va, vb, by_ref, sem = refs[-9:]
    own, count = om_ref.shape[:2]
    fetch = pltpu.make_async_copy(by_any, by_ref, sem)
    fetch.start()
    masks = lane_masks(place()[1])
    for k in range(own):
        for t, value in enumerate(spread(p_ref, count, k)):
            qs[k, t] = value
    if before:
        earlier, back_before = refs[5:7]
        back[...] = back_before[...]
    else:
        back[...] = jnp.zeros_like(back)
    fetch.wait()
    if before:

        def keep(k, carry):
            out_ref[by_ref[1, k]] = earlier[by_ref[1, k]]
            return carry

        lax.fori_loop(0, before * GROUP, keep, 0)

    def group(g, carry):
        pairs = [by_ref[1, g * GROUP + k] for k in range(GROUP)]
        for k, p in enumerate(pairs):
            first, second = p // own, p % own
            for t in range(count):
                sr[k, t] = om_ref[first, t] * qs[second, t]
                va[k, t] = vs_ref[p, t]
        steps = [by_ref[0, g * GROUP + k] for k in range(GROUP)]
        relax(steps, count, va, vb, sr, cf_ref, masks)
        for k, p in enumerate(pairs):
            first, second = p // own, p % own
            spread_store(out_ref, [va[k, t] for t in range(count)], p)
            for t in range(count):
                back[second, t] = back[second, t] + va[k, t] * os_ref[first, t]
        return carry

    lax.fori_loop(before, before + groups, group, 0)
    for k in range(own):
        if last:
            spread_store(back_ref, [back[k, t] for t in range(count)], k)
        else:
            back_ref[k] = back[k]


def interior(groups, before, last, order, ready, partner, *earlier):
    pairs, count, _, lanes = ready[0].shape
    own, rows, _ = partner.shape
    four = pltpu.VMEM((GROUP, count, SUB, lanes), jnp.float32)
    each = pltpu.VMEM((own, count, SUB, lanes), jnp.float32)
    back = f32(own, rows, lanes) if last else f32(own, count, SUB, lanes)
    return pl.pallas_call(
        functools.partial(interior_kernel, groups, before, last),
        out_shape=(f32(pairs, rows, lanes), back),
        in_specs=[ANY] + [VMEM] * (5 + len(earlier)),
        out_specs=(VMEM, VMEM),
        scratch_shapes=[each, each, four, four, four]
        + [pltpu.SMEM(order.shape, jnp.int32), pltpu.SemaphoreType.DMA],
        compiler_params=params(),
        cost_estimate=cost(1.8 * groups),
        name=f"interior{before}",
    )(order, *ready[:4], partner, *earlier)


def row_pair_kernel(own, a_ref, b_ref, out_ref):
    out_ref[0:own] = a_ref[0:own]
    out_ref[own:] = b_ref[0:own]


def row_pair(own, rows_a, rows_b):
    return pl.pallas_call(
        functools.partial(row_pair_kernel, own),
        out_shape=f32(2 * own, *rows_a.shape[1:]),
        in_specs=[VMEM] * 2,
        out_specs=VMEM,
        compiler_params=params(),
        cost_estimate=cost(0.1),
        name="row_pair",
    )(rows_a, rows_b)


def beyond(at, a, b):
    low_is_a = at[0] == 1
    b = jnp.where(at[2], b, 0.0)
    return jnp.where(low_is_a, a, b), jnp.where(low_is_a, b, a)


def edges_kernel(e_ref, ra_ref, rb_ref, p2_ref, p_ref, out_ref):
    here_at = place()
    own, rows, _ = p_ref.shape
    groups = e_ref.shape[0]
    for g in range(groups):
        out_ref[g, SUB : SUB + rows] = e_ref[g]
    out_ref[groups, SUB : SUB + rows] = packed([p_ref[k] for k in range(own)])
    pairs = own * own
    ends = [beyond(here_at, ra_ref[f], rb_ref[f]) for f in range(own + pairs + 6)]
    ends += [beyond(here_at, p2_ref[k], p2_ref[own + k]) for k in range(own)]
    lists = [range(own)] + [range(own * (1 + k), own * (2 + k)) for k in range(own)]
    at = own + pairs
    lists += [range(at, at + 4), range(at + 4, at + 6), range(at + 6, at + 6 + own)]
    for g, fields in enumerate(lists):
        out_ref[g, 0:SUB] = packed([ends[f][0] for f in fields])
        out_ref[g, SUB + rows :] = packed([ends[f][1] for f in fields])


def tall_edges(edges, rows_a, rows_b, partner_rows, partner):
    groups, rows, lanes = edges.shape
    return pl.pallas_call(
        edges_kernel,
        out_shape=f32(groups + 1, rows + 2 * SUB, lanes),
        in_specs=[VMEM] * 5,
        out_specs=VMEM,
        compiler_params=params(),
        cost_estimate=cost(0.7),
        name="tall_edges",
    )(edges, rows_a, rows_b, partner_rows, partner)


def bands_kernel(
    by_any, v_ref, o_ref, p_ref, m_ref, c_ref, ra_ref, rb_ref, p2_ref,
    out_ref, back_ref, band, cf, ms, sr, va, vb, by_ref, sem,
):
    fetch = pltpu.make_async_copy(by_any, by_ref, sem)
    fetch.start()
    here_at = place()
    own, rows, _ = o_ref.shape
    pairs = v_ref.shape[0]
    tall = 3 * SUB
    count = 2 * tall // SUB

    def fill(at, ends, ref, *index):
        band[at, 0:SUB] = ends[0]
        band[at, SUB:tall] = ref[(*index, slice(0, 2 * SUB))]
        band[at, tall : tall + 2 * SUB] = ref[(*index, slice(rows - 2 * SUB, rows))]
        band[at, tall + 2 * SUB : 2 * tall] = ends[1]

    def received(f):
        return beyond(here_at, ra_ref[f], rb_ref[f])

    def fill_pair(p, carry):
        fill(p, received(own + p), v_ref, p)
        return carry

    lax.fori_loop(0, pairs, fill_pair, 0, unroll=4)
    o_at, p_at = pairs, pairs + own
    m_at = p_at + own
    for k in range(own):
        fill(o_at + k, received(k), o_ref, k)
        fill(p_at + k, beyond(here_at, p2_ref[k], p2_ref[own + k]), p_ref, k)
    fill(m_at, received(own + pairs), m_ref)
    for n in range(5):
        fill(m_at + 1 + n, received(own + pairs + 1 + n), c_ref, n)

    masks = lane_masks(place()[1])
    metric = spread(band, count, m_at)
    raw = [spread(band, count, m_at + 1 + n) for n in range(5)]
    for t in range(count):
        scale = jnp.where(masks[2], 0.0, scaled_coefs([raw[n][t] for n in range(5)]))
        ms[t] = scale * metric[t]
        for n in range(5):
            cf[n, t] = scale * raw[n][t]

    def group(g, carry):
        chosen = [by_ref[1, g * BANDS + k] for k in range(BANDS)]
        for k, p in enumerate(chosen):
            o, q = spread(band, count, o_at + p // own), spread(band, count, p_at + p % own)
            v = spread(band, count, p)
            for t in range(count):
                sr[k, t] = ms[t] * (o[t] * q[t])
                va[k, t] = v[t]
        steps = [by_ref[0, g * BANDS + k] for k in range(BANDS)]
        relax(steps, count, va, vb, sr, cf, masks)
        for k, p in enumerate(chosen):
            spread_store(band, [va[k, t] for t in range(count)], p)
            out_ref[p, 0] = band[p, SUB : 2 * SUB]
            out_ref[p, 1] = band[p, tall + SUB : tall + 2 * SUB]
        return carry

    fetch.wait()
    lax.fori_loop(0, pairs // BANDS, group, 0)
    for end, start in enumerate((0, rows - SUB)):
        o = [o_ref[k, start : start + SUB] for k in range(own)]
        for second in range(own):
            terms = [out_ref[first * own + second, end] * o[first] for first in range(own)]
            back_ref[end * own + second] = sum(terms[1:], terms[0])


def bands(order, potentials, orbitals, partner, metric, coefficients, *received):
    own, rows, lanes = orbitals.shape
    pairs = potentials.shape[0]
    count = 6
    some = pltpu.VMEM((BANDS, count, SUB, lanes), jnp.float32)
    return pl.pallas_call(
        bands_kernel,
        out_shape=(f32(pairs, 2, SUB, lanes), f32(2 * own, SUB, lanes)),
        in_specs=[ANY] + [VMEM] * 8,
        out_specs=(VMEM, VMEM),
        scratch_shapes=[
            pltpu.VMEM((pairs + 2 * own + 6, count * SUB, lanes), jnp.float32),
            pltpu.VMEM((5, count, SUB, lanes), jnp.float32),
            pltpu.VMEM((count, SUB, lanes), jnp.float32),
            some,
            some,
            some,
            pltpu.SMEM(order.shape, jnp.int32),
            pltpu.SemaphoreType.DMA,
        ],
        compiler_params=params(),
        cost_estimate=cost(2.5),
        name="bands",
    )(order, potentials, orbitals, partner, metric, coefficients, *received)


def strip_place(side):
    left_own = place()[1] == side
    in_strip = jnp.where(left_own, HALO, STRIP // 2)
    in_block = jnp.where(left_own, LANES - HALO, 0)
    return left_own, in_strip, in_block


def strips_kernel(sides, n_ref, rows_ref, e_ref, *refs):
    recv = refs[:sides]
    pay_ref, sv_ref, st, cf, ms, orep, sr, va, vb, flat = refs[sides:]
    own = n_ref.shape[0]
    groups, tall, _ = e_ref.shape
    rows = tall - 2 * SUB
    count = tall // SUB
    lane = lane_of()
    lead = rows_ref.shape[0]
    fold = rows // SUB // BLOCKS
    pay_ref[0:lead] = rows_ref[...]

    for side in range(sides):
        left_own, in_strip, _ = strip_place(side)
        within = lane_of(tall) % STRIP
        from_own = jnp.where(left_own, within, STRIP - 1 - within) < STRIP // 2
        for g in range(groups):
            st[g] = jnp.where(from_own, e_ref[g], recv[side][g])
        first_group, second_group = spread(st, count, own + 1), spread(st, count, own + 2)
        for t in range(count):
            cs = [replicated(first_group[t], 1 + n) for n in range(3)]
            cs += [replicated(second_group[t], n) for n in range(2)]
            scale = scaled_coefs(cs)
            ms[t] = scale * replicated(first_group[t], 0)
            for n in range(5):
                cf[n, t] = scale * cs[n]
        o, q = spread(st, count, 0), spread(st, count, groups - 1)
        for t in range(count):
            weighted = ms[t] * q[t]
            for g in range(own):
                alone = replicated(o[t], g)
                orep[g, t] = alone
                sr[g, t] = alone * weighted
        steps = []
        for g in range(own):
            for t, value in enumerate(spread(st, count, 1 + g)):
                va[g, t] = value
            steps.append(n_ref[g])

        def body(turn, carry):
            for s in range(2):
                keep = [n > 2 * turn + s for n in steps]
                sweep(own, count, (va, vb)[s], (vb, va)[s], sr, cf, keep=keep)
            return carry

        lax.fori_loop(0, SWEEPS // 2, body, 0)
        back = []
        for t in range(count):
            terms = [va[g, t] * orep[g, t] for g in range(own)]
            back.append(sum(terms[1:], terms[0]))
        spread_store(flat, back)
        for g in range(own):
            spread_store(sv_ref, [va[g, t] for t in range(count)], side * own + g)
        for v in range(fold):
            out = jnp.zeros((SUB, LANES), jnp.float32)
            for g in range(BLOCKS):
                at = SUB + (g * fold + v) * SUB
                shift = (HALO * g - in_strip) % LANES
                turned = pltpu.roll(flat[at : at + SUB], shift, 1)
                out = jnp.where(lane % STRIP // HALO == g, turned, out)
            pay_ref[lead + side * fold + v] = out


def strips(steps, band_back, edges, received):
    sides = len(received)
    groups, tall, lanes = edges.shape
    own = steps.shape[0]
    count = tall // SUB
    fold = (tall - 2 * SUB) // SUB // BLOCKS
    each = pltpu.VMEM((own, count, SUB, lanes), jnp.float32)
    return pl.pallas_call(
        functools.partial(strips_kernel, sides),
        out_shape=(
            f32(band_back.shape[0] + sides * fold, SUB, lanes),
            f32(sides * own, tall, lanes),
        ),
        in_specs=[VMEM] * (3 + sides),
        out_specs=(VMEM, VMEM),
        scratch_shapes=[
            pltpu.VMEM((groups, tall, lanes), jnp.float32),
            pltpu.VMEM((5, count, SUB, lanes), jnp.float32),
            pltpu.VMEM((count, SUB, lanes), jnp.float32),
            each,
            each,
            each,
            each,
            pltpu.VMEM((tall, lanes), jnp.float32),
        ],
        compiler_params=params(),
        cost_estimate=cost(2.9),
        name="strips",
    )(steps, band_back, edges, *received)


def merge_kernel(sides, inner_ref, ends_ref, sv_ref, o_ref, p_ref, v_ref, home_ref):
    own, rows, _ = o_ref.shape
    lane = lane_of()

    def merge(r, carry):
        at = pl.multiple_of(r * SUB, SUB)
        q = [p_ref[k, pl.ds(at, SUB)] for k in range(own)]
        home = [0.0] * own
        for first in range(own):
            strips = [sv_ref[side * own + first, pl.ds(at + SUB, SUB)] for side in range(sides)]
            for second in range(own):
                p = first * own + second
                value = inner_ref[p, pl.ds(at, SUB)]
                value = jnp.where(r == 0, ends_ref[p, 0], value)
                value = jnp.where(r == rows // SUB - 1, ends_ref[p, 1], value)
                for side in range(sides):
                    right = place()[1] == side
                    edge = jnp.where(right, LANES - 1 - lane, lane) < HALO
                    turned = pltpu.roll(
                        strips[side], (-(STRIP * second + STRIP // 2)) % LANES, 1
                    )
                    value = jnp.where(edge, turned, value)
                v_ref[p, pl.ds(at, SUB)] = value
                home[first] = home[first] + value * q[second]
        for k in range(own):
            home_ref[k, pl.ds(at, SUB)] = o_ref[k, pl.ds(at, SUB)] - step_size * home[k]
        return carry

    lax.fori_loop(0, rows // SUB, merge, 0, unroll=4)


def merged(inner, ends, strip_fields, orbitals, partner):
    own, rows, _ = orbitals.shape
    sides = strip_fields.shape[0] // own
    return pl.pallas_call(
        functools.partial(merge_kernel, sides),
        out_shape=(f32(*inner.shape), f32(*orbitals.shape)),
        in_specs=[VMEM] * 5,
        out_specs=(VMEM, VMEM),
        compiler_params=params(),
        cost_estimate=cost(1.2),
        name="merge",
    )(inner, ends, strip_fields, orbitals, partner)


def write_kernel(v_ref, out_ref, sems):
    parts = sems.shape[0]
    size = v_ref.shape[0] // parts
    copies = []
    for k in range(parts):
        part = pl.ds(k * size, size)
        copies.append(pltpu.make_async_copy(v_ref.at[part], out_ref.at[part], sems.at[k]))
    for copy in copies:
        copy.start()
    for copy in copies:
        copy.wait()


def written(fields):
    return pl.pallas_call(
        write_kernel,
        out_shape=f32(*fields.shape),
        in_specs=[ANY],
        out_specs=ANY,
        scratch_shapes=[pltpu.SemaphoreType.DMA((4,))],
        compiler_params=params(),
        cost_estimate=cost(1.2),
        name="write",
    )(fields)


def norm_kernel(home_ref, recv_ref, edge_ref, m_ref, upd_ref, norm_ref):
    own, rows, _ = home_ref.shape
    lane = lane_of()
    fold = rows // SUB // BLOCKS
    lead = 2 * own
    sides = (edge_ref.shape[0] - lead) // fold
    norm_ref[...] = jnp.zeros_like(norm_ref)
    for k in range(own):
        total = jnp.zeros((SUB, LANES), jnp.float32)
        for r in range(rows // SUB):
            at = r * SUB
            value = recv_ref[k, at : at + SUB]
            if r == 0:
                value = edge_ref[k]
            if r == rows // SUB - 1:
                value = edge_ref[own + k]
            g, v = divmod(r, fold)
            for side in range(sides):
                left_own, _, in_block = strip_place(side)
                edge = jnp.where(left_own, LANES - 1 - lane, lane) < HALO
                shift = (in_block - STRIP * k - HALO * g) % LANES
                turned = pltpu.roll(edge_ref[lead + side * fold + v], shift, 1)
                value = jnp.where(edge, turned, value)
            updated = home_ref[k, at : at + SUB] - step_size * value
            upd_ref[k, at : at + SUB] = updated
            total = total + m_ref[at : at + SUB] * updated * updated
        norm_ref[k : k + 1] = jnp.sum(total, axis=0, keepdims=True)


def partial_norms(home, received, edge_terms, metric):
    own, _, lanes = home.shape
    return pl.pallas_call(
        norm_kernel,
        out_shape=(f32(*home.shape), f32(-(-own // SUB) * SUB, lanes)),
        in_specs=[VMEM] * 4,
        out_specs=(VMEM, VMEM),
        compiler_params=params(),
        cost_estimate=cost(0.7),
        name="partial_norms",
    )(home, received, edge_terms, metric)


def scale_kernel(cells, upd_ref, *refs):
    out_ref = refs[-1]
    sums = functools.reduce(lambda a, b: a + b, [ref[...] for ref in refs[:-1]])
    for k in range(upd_ref.shape[0]):
        total = sums[k : k + 1]
        norm = jnp.sum(total, axis=1, keepdims=True)
        out_ref[k] = upd_ref[k] * jnp.sqrt(cells / norm)


def rescaled(updated, norms, cells):
    return pl.pallas_call(
        functools.partial(scale_kernel, float(cells)),
        out_shape=f32(*updated.shape),
        in_specs=[VMEM] * (1 + len(norms)),
        out_specs=VMEM,
        compiler_params=params(),
        cost_estimate=cost(0.8),
        name="rescaled",
    )(updated, *norms)


def shifted(value, axis, by):
    size = lax.axis_size(axis)
    return lax.ppermute(value, axis, [(i, (i + by) % size) for i in range(size)])


def pair_swaps(size):
    even = [(i, i + 1) for i in range(0, size - 1, 2)]
    odd = [(i, i + 1) for i in range(1, size - 1, 2)]
    return [p + [(b, a) for a, b in p] for p in (even, odd)]


def row_swap(swap, gx, gy):
    to = dict(swap)
    pairs = []
    for i in range(gx):
        for j in range(gy):
            pairs.append((i * gy + j, to[i] * gy + j if i in to else i * gy + (j ^ 1)))
    return pairs


def norm_hops(gx, gy):
    along = [[(i, i ^ (1 << k)) for i in range(gx * gy)] for k in range(gy.bit_length() - 1)]
    across = [[(i, i ^ (gy * k) ^ 1) for i in range(gx * gy)] for k in range(1, gx)]
    return along, across


def by_count(counts):
    at = jnp.arange(counts.shape[0], dtype=jnp.int32)
    more = counts[None] > counts[:, None]
    tie = (counts[None] == counts[:, None]) & (at[None] < at[:, None])
    rank = jnp.sum((more | tie).astype(jnp.int32), axis=1)
    chosen = (rank[None] == at[:, None])[None]
    return jnp.sum(jnp.where(chosen, jnp.stack([counts, at])[:, None], 0), axis=2)


def local(orbitals, potentials, coefficients, metric, sweep_counts):
    own, rows, lanes = orbitals.shape
    gx, gy = lax.axis_size("gx"), lax.axis_size("gy")
    order = by_count(sweep_counts)
    steps = jnp.repeat(sweep_counts.reshape(own, 1, own), STRIP, axis=2)
    steps = jnp.broadcast_to(steps, (own, SUB, lanes))
    col_swaps = [p for p in pair_swaps(gy) if p]
    row_swaps = [row_swap(p, gx, gy) for p in pair_swaps(gx)]
    groups = potentials.shape[0] // GROUP

    partner = shifted(orbitals, "orb", 1)
    order, steps, *ready = prepare(order, steps, orbitals, potentials, metric[None], coefficients)
    *ready, edges, pay_a, pay_b, orbitals, potentials, metric, coefficients = ready
    metric = metric.reshape(rows, lanes)
    rows_a = lax.ppermute(pay_a, ("gx", "gy"), row_swaps[0])
    rows_b = lax.ppermute(pay_b, ("gx", "gy"), row_swaps[1])
    inner = interior(1, 0, False, order, ready, partner)
    rows_a, rows_b, inner = lax.optimization_barrier((rows_a, rows_b, inner))
    partner_rows = shifted(row_pair(own, rows_a, rows_b), "orb", 1)
    inner, back = interior(groups - 1, 1, True, order, ready, partner, *inner)
    partner_rows, inner, back = lax.optimization_barrier((partner_rows, inner, back))
    early = shifted(back, "orb", -1)
    edges = tall_edges(edges, rows_a, rows_b, partner_rows, partner)
    received = [lax.ppermute(edges, "gy", swap) for swap in col_swaps]
    ends, band_back = bands(
        order, potentials, orbitals, partner, metric, coefficients,
        rows_a, rows_b, partner_rows,
    )
    edge_back, strip_fields = strips(steps, band_back, edges, received)
    edge_terms = shifted(edge_back, "orb", -1)
    fields, home = merged(inner, ends, strip_fields, orbitals, partner)
    updated, norms = partial_norms(home, early, edge_terms, metric)
    norms, fields = lax.optimization_barrier((norms, fields))
    along, across = norm_hops(gx, gy)
    for hop in along:
        norms = norms + lax.ppermute(norms, ("gx", "gy"), hop)
    norms = [norms] + [lax.ppermute(norms, ("gx", "gy"), hop) for hop in across]
    return (rescaled(updated, norms, rows * lanes * gx * gy), written(fields))


def solution(mesh):
    return jax.shard_map(
        local,
        mesh=mesh,
        in_specs=(
            P("orb", "gx", "gy"),
            P("orb", "gx", "gy"),
            P(None, "gx", "gy"),
            P("gx", "gy"),
            P("orb"),
        ),
        out_specs=(P("orb", "gx", "gy"), P("orb", "gx", "gy")),
        check_vma=False,
    )
```

```python
import functools

import jax
import jax.numpy as jnp
from jax import lax
from jax.experimental import pallas as pl
from jax.experimental.pallas import tpu as pltpu
from jax.sharding import PartitionSpec as P

SWEEPS = 8

relaxation = 0.8
screening = 0.02
step_size = 0.1

LANES = 128
SUB = 8
HALO = 8
STRIP = 32
BLOCKS = LANES // STRIP
LEAST = 4
FIRST = 8
GROUP = 8
BANDS = 8
AHEAD = 16
VMEM_LIMIT = 16 * 1024 * 1024

VMEM = pl.BlockSpec(memory_space=pltpu.VMEM)
ANY = pl.BlockSpec(memory_space=pl.ANY)
HBM = pl.BlockSpec(memory_space=pltpu.HBM)


def f32(*shape):
    return jax.ShapeDtypeStruct(shape, jnp.float32)


def params():
    return pltpu.CompilerParams(vmem_limit_bytes=VMEM_LIMIT)


def cost(microseconds):
    return pl.CostEstimate(
        flops=0, bytes_accessed=int(microseconds * 3.7e6), transcendentals=0
    )


def place():
    row, col = lax.axis_index("gx"), lax.axis_index("gy")
    inside = (row > 0) & (row < lax.axis_size("gx") - 1)
    return row % 2, col % 2, inside


def lane_of(rows=SUB):
    return lax.broadcasted_iota(jnp.int32, (rows, LANES), 1)


def packed(fields):
    rows = fields[0].shape[0]
    block = lane_of(rows) // STRIP
    out = jnp.zeros((rows, LANES), jnp.float32)
    for at, value in enumerate(fields):
        turned = pltpu.roll(value, (STRIP * at + STRIP // 2) % LANES, 1)
        out = jnp.where(block == at, turned, out)
    return out


def replicated(value, at):
    one = jnp.where(lane_of(value.shape[0]) // STRIP == at, value, 0.0)
    one = one + pltpu.roll(one, STRIP, 1)
    return one + pltpu.roll(one, 2 * STRIP, 1)


def spread(ref, count, *index):
    return [ref[(*index, pl.ds(t, SUB, stride=count), slice(None))] for t in range(count)]


def spread_store(ref, values, *index):
    count = len(values)
    for t, value in enumerate(values):
        ref[(*index, pl.ds(t, SUB, stride=count), slice(None))] = value


def scaled_coefs(coefs):
    total = coefs[0] + coefs[1] + coefs[2] + coefs[3] + 4.0 * coefs[4]
    diagonal = (1.0 + screening) * total
    return relaxation / jnp.where(diagonal == 0.0, 1.0, diagonal)


def sweep(fields, count, old, new, source, coefs, west=None, east=None, dead=None, keep=None):
    held, to_east, to_west, slopes = {}, {}, {}, {}

    def issue(k, t):
        value = old[k, t]
        held[k, t] = value
        e, w = pltpu.roll(value, LANES - 1, 1), pltpu.roll(value, 1, 1)
        if west is not None:
            w, e = jnp.where(west, 0.0, w), jnp.where(east, 0.0, e)
        to_east[k, t], to_west[k, t] = e, w

    def field(k, t):
        return held[k, t]

    def slope(k, t):
        if (k, t) not in slopes:
            slopes[k, t] = to_east[k, t] - to_west[k, t]
        return slopes[k, t]

    def above(get, k, t):
        return get(k, t - 1) if t else pltpu.roll(get(k, count - 1), 1, 0)

    def below(get, k, t):
        return get(k, t + 1) if t < count - 1 else pltpu.roll(get(k, 0), SUB - 1, 0)

    order = []
    for k in range(fields):
        order += [(k, count - 1)] + [(k, t) for t in range(count - 1)]
    done = 0
    for at in range(fields * count):
        k, t = divmod(at, count)
        until = min(len(order), max(at + AHEAD, k * count + min(t + 3, count)))
        while done < until:
            issue(*order[done])
            done += 1
        value = (1.0 - relaxation) * field(k, t) + source[k, t]
        value = value + coefs[0, t] * above(field, k, t) + coefs[1, t] * below(field, k, t)
        value = value + coefs[2, t] * to_east[k, t] + coefs[3, t] * to_west[k, t]
        value = value + coefs[4, t] * (above(slope, k, t) - below(slope, k, t))
        if dead is not None:
            value = jnp.where(dead, 0.0, value)
        if keep is not None:
            value = jnp.where(keep[k], value, field(k, t))
        new[k, t] = value


class Chosen:
    def __init__(self, ref, picks):
        self.ref, self.picks = ref, picks

    def __getitem__(self, at):
        return self.ref[self.picks[at[0]], at[1]]


def relax(steps, count, here, there, source, coefs, masks):
    fields = len(steps)
    west, east, dead = masks
    pair = (here, there)
    sweep(fields, count, here, there, source, coefs, west, east, dead)
    for s in range(1, LEAST):
        sweep(fields, count, pair[s % 2], pair[1 - s % 2], source, coefs)
    top = functools.reduce(jnp.maximum, steps)

    def body(turn, carry):
        for s in range(2):
            at = LEAST + 2 * turn + s
            keep = [jnp.full((SUB, LANES), n, jnp.int32) > at for n in steps]
            sweep(fields, count, pair[s], pair[1 - s], source, coefs, keep=keep)
        return carry

    lax.fori_loop(0, (top - LEAST + 1) // 2, body, 0)


def lane_masks(odd):
    lane = lane_of()
    west = (lane == 0) & (odd == 0)
    east = (lane == LANES - 1) & (odd == 1)
    dead = lane == (1 - odd) * (LANES - 1)
    return west, east, dead


def sorted_counts(counts):
    pairs = counts.shape[1]
    at = lax.broadcasted_iota(jnp.int32, (pairs, pairs), 1)
    down = lax.broadcasted_iota(jnp.int32, (pairs, pairs), 0)
    row = jnp.broadcast_to(counts, (pairs, pairs)).astype(jnp.float32)

    def turned(value):
        return jnp.sum(jnp.where(at == down, value, 0.0), axis=1, keepdims=True)

    def rank(key):
        own_key = turned(key)
        before = jnp.where(key > own_key, 1.0, 0.0)
        before = before + jnp.where((key == own_key) & (at < down), 1.0, 0.0)
        return jnp.sum(before, axis=1, keepdims=True)

    chosen = jnp.broadcast_to(rank(row), row.shape) == at.astype(jnp.float32)
    column = jnp.broadcast_to(turned(row), row.shape)
    steps = jnp.sum(jnp.where(chosen, column, 0.0), axis=0, keepdims=True)
    which = jnp.sum(jnp.where(chosen, down.astype(jnp.float32), 0.0), axis=0, keepdims=True)
    return jnp.concatenate([steps, which], axis=0).astype(jnp.int32)


def prepare_kernel(n_hbm, o_hbm, v_hbm, m_hbm, c_hbm, by_ref, steps_ref, *refs):
    vs_ref, os_ref, om_ref, cf_ref, e_ref, pay_a, pay_b, o_ref, v_ref, m_ref, c_ref = refs[:11]
    n_ref, sems = refs[11:]
    own, rows, _ = o_ref.shape
    pairs = v_ref.shape[0]
    count = rows // SUB
    sources = [(n_hbm, n_ref), (m_hbm, m_ref), (c_hbm, c_ref), (o_hbm, o_ref)]
    for first in range(own):
        part = pl.ds(first * own, own)
        sources.append((v_hbm.at[part], v_ref.at[part]))
    copies = [
        pltpu.make_async_copy(source, target, sems.at[at])
        for at, (source, target) in enumerate(sources)
    ]
    for copy in copies:
        copy.start()

    starts = [(1 - place()[0]) * (rows - HALO), place()[0] * (rows - HALO)]
    starts = [pl.multiple_of(start, HALO) for start in starts]

    def send_rows(at, ref, index):
        for pay, start in zip((pay_a, pay_b), starts):
            pay[at] = ref[index, pl.ds(start, HALO)]

    copies[0].wait()
    counts = n_ref[...]
    by_ref[...] = sorted_counts(counts)
    at = lax.broadcasted_iota(jnp.int32, counts.shape, 1)
    floats = counts.astype(jnp.float32)
    block = lane_of() // STRIP
    for first in range(own):
        steps = jnp.zeros((SUB, LANES), jnp.float32)
        for second in range(own):
            alone = jnp.where(at == first * own + second, floats, 0.0)
            steps = jnp.where(block == second, jnp.sum(alone, axis=1, keepdims=True), steps)
        steps_ref[first] = steps.astype(jnp.int32)
    copies[1].wait()
    copies[2].wait()
    send_rows(own + pairs, m_ref, 0)
    for n in range(5):
        send_rows(own + pairs + 1 + n, c_ref, n)
    e_ref[1 + own] = packed([m_ref[0], c_ref[0], c_ref[1], c_ref[2]])
    e_ref[2 + own] = packed([c_ref[3], c_ref[4]])
    dead = lane_masks(place()[1])[2]
    metric = spread(m_ref, count, 0)
    raw = [spread(c_ref, count, n) for n in range(5)]
    weights = []
    for t in range(count):
        scale = jnp.where(dead, 0.0, scaled_coefs([raw[n][t] for n in range(5)]))
        weights.append(scale * metric[t])
        for n in range(5):
            cf_ref[n, t] = scale * raw[n][t]
    copies[3].wait()
    e_ref[0] = packed([o_ref[k] for k in range(own)])
    for k in range(own):
        send_rows(k, o_ref, k)
        for t, value in enumerate(spread(o_ref, count, k)):
            os_ref[k, t] = value
            om_ref[k, t] = weights[t] * value
    for first in range(own):
        copies[4 + first].wait()
        e_ref[1 + first] = packed([v_ref[first * own + k] for k in range(own)])
        for p in range(first * own, (first + 1) * own):
            send_rows(own + p, v_ref, p)
            for t, value in enumerate(spread(v_ref, count, p)):
                vs_ref[p, t] = value


def prepare(*arrays):
    counts, orbitals, potentials, _, coefficients = arrays
    own, rows, lanes = orbitals.shape
    pairs = potentials.shape[0]
    count = rows // SUB
    inputs = [pltpu.with_memory_space_constraint(a, pltpu.HBM) for a in arrays]
    return pl.pallas_call(
        prepare_kernel,
        out_shape=(
            jax.ShapeDtypeStruct((2, pairs), jnp.int32),
            jax.ShapeDtypeStruct((own, SUB, lanes), jnp.int32),
            f32(pairs, count, SUB, lanes),
            f32(own, count, SUB, lanes),
            f32(own, count, SUB, lanes),
            f32(5, count, SUB, lanes),
            f32(own + 3, rows, lanes),
            *[f32(own + pairs + 1 + coefficients.shape[0], HALO, lanes)] * 2,
            *[f32(*a.shape) for a in arrays[1:]],
        ),
        in_specs=[HBM] * 5,
        out_specs=(VMEM,) * 13,
        scratch_shapes=[
            pltpu.VMEM(counts.shape, jnp.int32),
            pltpu.SemaphoreType.DMA((4 + own,)),
        ],
        compiler_params=params(),
        cost_estimate=cost(2.0),
        name="prepare",
    )(*inputs)


def interior_kernel(size, groups, before, by_any, *refs):
    vs_ref, os_ref, om_ref, cf_ref, p_ref = refs[:5]
    out_ref, back_ref, back, flat, sr, va, vb, by_ref, sem = refs[-9:]
    own, count = om_ref.shape[:2]
    fetch = pltpu.make_async_copy(by_any, by_ref, sem)
    fetch.start()
    masks = lane_masks(place()[1])
    for second in range(own):
        partner = spread(p_ref, count, second)
        for first in range(own):
            for t in range(count):
                sr[first * own + second, t] = om_ref[first, t] * partner[t]
    if before:
        earlier, back_before = refs[5:7]
        back[...] = back_before[...]
    else:
        back[...] = jnp.zeros_like(back)
    fetch.wait()
    if before:

        def keep(k, carry):
            out_ref[by_ref[1, k]] = earlier[by_ref[1, k]]
            return carry

        lax.fori_loop(0, before, keep, 0)

    def group(g, carry):
        pairs = [by_ref[1, before + g * size + k] for k in range(size)]
        for k, p in enumerate(pairs):
            for t in range(count):
                va[k, t] = vs_ref[p, t]
        steps = [by_ref[0, before + g * size + k] for k in range(size)]
        relax(steps, count, va, vb, Chosen(sr, pairs), cf_ref, masks)
        for k, p in enumerate(pairs):
            first, second = p // own, p % own
            spread_store(out_ref, [va[k, t] for t in range(count)], p)
            for t in range(count):
                back[second, t] = back[second, t] + va[k, t] * os_ref[first, t]
        return carry

    lax.fori_loop(0, groups, group, 0)
    for k in range(own):
        if before:
            spread_store(flat, [back[k, t] for t in range(count)])
            back_ref[k] = flat[SUB : SUB + back_ref.shape[1]]
        else:
            back_ref[k] = back[k]


def interior(size, groups, before, order, ready, partner, *earlier):
    pairs, count, _, lanes = ready[0].shape
    own = ready[1].shape[0]
    rows = count * SUB
    some = pltpu.VMEM((size, count, SUB, lanes), jnp.float32)
    each = pltpu.VMEM((own, count, SUB, lanes), jnp.float32)
    every = pltpu.VMEM((pairs, count, SUB, lanes), jnp.float32)
    back = f32(own, rows - 2 * SUB, lanes) if before else f32(own, count, SUB, lanes)
    return pl.pallas_call(
        functools.partial(interior_kernel, size, groups, before),
        out_shape=(f32(pairs, rows, lanes), back),
        in_specs=[ANY] + [VMEM] * (5 + len(earlier)),
        out_specs=(VMEM, VMEM),
        scratch_shapes=[each, pltpu.VMEM((rows, lanes), jnp.float32), every, some, some]
        + [pltpu.SMEM(order.shape, jnp.int32), pltpu.SemaphoreType.DMA],
        compiler_params=params(),
        cost_estimate=cost(0.4 * size * groups),
        name=f"interior{before}",
    )(order, *ready[:4], partner, *earlier)


def row_pair_kernel(own, a_ref, b_ref, out_ref):
    out_ref[0:own] = a_ref[0:own]
    out_ref[own:] = b_ref[0:own]


def row_pair(own, rows_a, rows_b):
    return pl.pallas_call(
        functools.partial(row_pair_kernel, own),
        out_shape=f32(2 * own, *rows_a.shape[1:]),
        in_specs=[VMEM] * 2,
        out_specs=VMEM,
        compiler_params=params(),
        cost_estimate=cost(0.1),
        name="row_pair",
    )(rows_a, rows_b)


def beyond(at, a, b):
    low_is_a = at[0] == 1
    b = jnp.where(at[2], b, 0.0)
    return jnp.where(low_is_a, a, b), jnp.where(low_is_a, b, a)


def edges_kernel(e_ref, ra_ref, rb_ref, p2_ref, p_ref, out_ref):
    here_at = place()
    own, rows, _ = p_ref.shape
    groups = e_ref.shape[0]
    for g in range(groups):
        out_ref[g, SUB : SUB + rows] = e_ref[g]
    out_ref[groups, SUB : SUB + rows] = packed([p_ref[k] for k in range(own)])
    pairs = own * own
    ends = [beyond(here_at, ra_ref[f], rb_ref[f]) for f in range(own + pairs + 6)]
    ends += [beyond(here_at, p2_ref[k], p2_ref[own + k]) for k in range(own)]
    lists = [range(own)] + [range(own * (1 + k), own * (2 + k)) for k in range(own)]
    at = own + pairs
    lists += [range(at, at + 4), range(at + 4, at + 6), range(at + 6, at + 6 + own)]
    for g, fields in enumerate(lists):
        out_ref[g, 0:SUB] = packed([ends[f][0] for f in fields])
        out_ref[g, SUB + rows :] = packed([ends[f][1] for f in fields])


def tall_edges(edges, rows_a, rows_b, partner_rows, partner):
    groups, rows, lanes = edges.shape
    return pl.pallas_call(
        edges_kernel,
        out_shape=f32(groups + 1, rows + 2 * SUB, lanes),
        in_specs=[VMEM] * 5,
        out_specs=VMEM,
        compiler_params=params(),
        cost_estimate=cost(0.7),
        name="tall_edges",
    )(edges, rows_a, rows_b, partner_rows, partner)


def bands_kernel(
    by_any, v_ref, o_ref, p_ref, m_ref, c_ref, ra_ref, rb_ref, p2_ref,
    out_ref, back_ref, band, cf, ms, sr, va, vb, by_ref, sem,
):
    fetch = pltpu.make_async_copy(by_any, by_ref, sem)
    fetch.start()
    here_at = place()
    own, rows, _ = o_ref.shape
    pairs = v_ref.shape[0]
    tall = 3 * SUB
    count = 2 * tall // SUB

    def fill(at, ends, ref, *index):
        band[at, 0:SUB] = ends[0]
        band[at, SUB:tall] = ref[(*index, slice(0, 2 * SUB))]
        band[at, tall : tall + 2 * SUB] = ref[(*index, slice(rows - 2 * SUB, rows))]
        band[at, tall + 2 * SUB : 2 * tall] = ends[1]

    def received(f):
        return beyond(here_at, ra_ref[f], rb_ref[f])

    def fill_pair(p, carry):
        fill(p, received(own + p), v_ref, p)
        return carry

    lax.fori_loop(0, pairs, fill_pair, 0, unroll=4)
    o_at, p_at = pairs, pairs + own
    m_at = p_at + own
    for k in range(own):
        fill(o_at + k, received(k), o_ref, k)
        fill(p_at + k, beyond(here_at, p2_ref[k], p2_ref[own + k]), p_ref, k)
    fill(m_at, received(own + pairs), m_ref)
    for n in range(5):
        fill(m_at + 1 + n, received(own + pairs + 1 + n), c_ref, n)

    masks = lane_masks(place()[1])
    metric = spread(band, count, m_at)
    raw = [spread(band, count, m_at + 1 + n) for n in range(5)]
    for t in range(count):
        scale = jnp.where(masks[2], 0.0, scaled_coefs([raw[n][t] for n in range(5)]))
        ms[t] = scale * metric[t]
        for n in range(5):
            cf[n, t] = scale * raw[n][t]

    def group(g, carry):
        chosen = [by_ref[1, g * BANDS + k] for k in range(BANDS)]
        for k, p in enumerate(chosen):
            o, q = spread(band, count, o_at + p // own), spread(band, count, p_at + p % own)
            v = spread(band, count, p)
            for t in range(count):
                sr[k, t] = ms[t] * (o[t] * q[t])
                va[k, t] = v[t]
        steps = [by_ref[0, g * BANDS + k] for k in range(BANDS)]
        relax(steps, count, va, vb, sr, cf, masks)
        for k, p in enumerate(chosen):
            spread_store(band, [va[k, t] for t in range(count)], p)
            out_ref[p, 0] = band[p, SUB : 2 * SUB]
            out_ref[p, 1] = band[p, tall + SUB : tall + 2 * SUB]
        return carry

    fetch.wait()
    lax.fori_loop(0, pairs // BANDS, group, 0)
    for end, start in enumerate((0, rows - SUB)):
        o = [o_ref[k, start : start + SUB] for k in range(own)]
        for second in range(own):
            terms = [out_ref[first * own + second, end] * o[first] for first in range(own)]
            back_ref[end * own + second] = sum(terms[1:], terms[0])


def bands(order, potentials, orbitals, partner, metric, coefficients, *received):
    own, rows, lanes = orbitals.shape
    pairs = potentials.shape[0]
    count = 6
    some = pltpu.VMEM((BANDS, count, SUB, lanes), jnp.float32)
    return pl.pallas_call(
        bands_kernel,
        out_shape=(f32(pairs, 2, SUB, lanes), f32(2 * own, SUB, lanes)),
        in_specs=[ANY] + [VMEM] * 8,
        out_specs=(VMEM, VMEM),
        scratch_shapes=[
            pltpu.VMEM((pairs + 2 * own + 6, count * SUB, lanes), jnp.float32),
            pltpu.VMEM((5, count, SUB, lanes), jnp.float32),
            pltpu.VMEM((count, SUB, lanes), jnp.float32),
            some,
            some,
            some,
            pltpu.SMEM(order.shape, jnp.int32),
            pltpu.SemaphoreType.DMA,
        ],
        compiler_params=params(),
        cost_estimate=cost(2.5),
        name="bands",
    )(order, potentials, orbitals, partner, metric, coefficients, *received)


def strip_place(side):
    left_own = place()[1] == side
    in_strip = jnp.where(left_own, HALO, STRIP // 2)
    in_block = jnp.where(left_own, LANES - HALO, 0)
    return left_own, in_strip, in_block


def strips_kernel(sides, n_ref, rows_ref, e_ref, *refs):
    recv = refs[:sides]
    pay_ref, sv_ref, st, cf, ms, orep, sr, va, vb, flat = refs[sides:]
    own = n_ref.shape[0]
    groups, tall, _ = e_ref.shape
    rows = tall - 2 * SUB
    count = tall // SUB
    lane = lane_of()
    lead = rows_ref.shape[0]
    fold = rows // SUB // BLOCKS
    pay_ref[0:lead] = rows_ref[...]

    for side in range(sides):
        left_own, in_strip, _ = strip_place(side)
        within = lane_of(tall) % STRIP
        from_own = jnp.where(left_own, within, STRIP - 1 - within) < STRIP // 2
        for g in range(groups):
            st[g] = jnp.where(from_own, e_ref[g], recv[side][g])
        first_group, second_group = spread(st, count, own + 1), spread(st, count, own + 2)
        for t in range(count):
            cs = [replicated(first_group[t], 1 + n) for n in range(3)]
            cs += [replicated(second_group[t], n) for n in range(2)]
            scale = scaled_coefs(cs)
            ms[t] = scale * replicated(first_group[t], 0)
            for n in range(5):
                cf[n, t] = scale * cs[n]
        o, q = spread(st, count, 0), spread(st, count, groups - 1)
        for t in range(count):
            weighted = ms[t] * q[t]
            for g in range(own):
                alone = replicated(o[t], g)
                orep[g, t] = alone
                sr[g, t] = alone * weighted
        steps = []
        for g in range(own):
            for t, value in enumerate(spread(st, count, 1 + g)):
                va[g, t] = value
            steps.append(n_ref[g])

        def body(turn, carry):
            for s in range(4):
                keep = [n > 4 * turn + s for n in steps]
                sweep(own, count, (va, vb)[s % 2], (vb, va)[s % 2], sr, cf, keep=keep)
            return carry

        lax.fori_loop(0, SWEEPS // 4, body, 0)
        back = []
        for t in range(count):
            terms = [va[g, t] * orep[g, t] for g in range(own)]
            back.append(sum(terms[1:], terms[0]))
        spread_store(flat, back)
        for g in range(own):
            spread_store(sv_ref, [va[g, t] for t in range(count)], side * own + g)
        for v in range(fold):
            out = jnp.zeros((SUB, LANES), jnp.float32)
            for g in range(BLOCKS):
                at = SUB + (g * fold + v) * SUB
                shift = (HALO * g - in_strip) % LANES
                turned = pltpu.roll(flat[at : at + SUB], shift, 1)
                out = jnp.where(lane % STRIP // HALO == g, turned, out)
            pay_ref[lead + side * fold + v] = out


def strips(steps, band_back, edges, received):
    sides = len(received)
    groups, tall, lanes = edges.shape
    own = steps.shape[0]
    count = tall // SUB
    fold = (tall - 2 * SUB) // SUB // BLOCKS
    each = pltpu.VMEM((own, count, SUB, lanes), jnp.float32)
    return pl.pallas_call(
        functools.partial(strips_kernel, sides),
        out_shape=(
            f32(band_back.shape[0] + sides * fold, SUB, lanes),
            f32(sides * own, tall, lanes),
        ),
        in_specs=[VMEM] * (3 + sides),
        out_specs=(VMEM, VMEM),
        scratch_shapes=[
            pltpu.VMEM((groups, tall, lanes), jnp.float32),
            pltpu.VMEM((5, count, SUB, lanes), jnp.float32),
            pltpu.VMEM((count, SUB, lanes), jnp.float32),
            each,
            each,
            each,
            each,
            pltpu.VMEM((tall, lanes), jnp.float32),
        ],
        compiler_params=params(),
        cost_estimate=cost(2.9),
        name="strips",
    )(steps, band_back, edges, *received)


def merge_kernel(sides, inner_ref, ends_ref, sv_ref, o_ref, p_ref, v_ref, home_ref):
    own, rows, _ = o_ref.shape
    lane = lane_of()

    def merge(r, carry):
        at = pl.multiple_of(r * SUB, SUB)
        q = [p_ref[k, pl.ds(at, SUB)] for k in range(own)]
        home = [0.0] * own
        for first in range(own):
            strips = [sv_ref[side * own + first, pl.ds(at + SUB, SUB)] for side in range(sides)]
            for second in range(own):
                p = first * own + second
                value = inner_ref[p, pl.ds(at, SUB)]
                value = jnp.where(r == 0, ends_ref[p, 0], value)
                value = jnp.where(r == rows // SUB - 1, ends_ref[p, 1], value)
                for side in range(sides):
                    right = place()[1] == side
                    edge = jnp.where(right, LANES - 1 - lane, lane) < HALO
                    turned = pltpu.roll(
                        strips[side], (-(STRIP * second + STRIP // 2)) % LANES, 1
                    )
                    value = jnp.where(edge, turned, value)
                v_ref[p, pl.ds(at, SUB)] = value
                home[first] = home[first] + value * q[second]
        for k in range(own):
            home_ref[k, pl.ds(at, SUB)] = o_ref[k, pl.ds(at, SUB)] - step_size * home[k]
        return carry

    lax.fori_loop(0, rows // SUB, merge, 0, unroll=4)


def merged(inner, ends, strip_fields, orbitals, partner):
    own, rows, _ = orbitals.shape
    sides = strip_fields.shape[0] // own
    return pl.pallas_call(
        functools.partial(merge_kernel, sides),
        out_shape=(f32(*inner.shape), f32(*orbitals.shape)),
        in_specs=[VMEM] * 5,
        out_specs=(VMEM, VMEM),
        compiler_params=params(),
        cost_estimate=cost(1.2),
        name="merge",
    )(inner, ends, strip_fields, orbitals, partner)


def write_kernel(v_ref, out_ref, sems):
    parts = sems.shape[0]
    size = v_ref.shape[0] // parts
    copies = []
    for k in range(parts):
        part = pl.ds(k * size, size)
        copies.append(pltpu.make_async_copy(v_ref.at[part], out_ref.at[part], sems.at[k]))
    for copy in copies:
        copy.start()
    for copy in copies:
        copy.wait()


def written(fields):
    return pl.pallas_call(
        write_kernel,
        out_shape=f32(*fields.shape),
        in_specs=[ANY],
        out_specs=ANY,
        scratch_shapes=[pltpu.SemaphoreType.DMA((4,))],
        compiler_params=params(),
        cost_estimate=cost(1.2),
        name="write",
    )(fields)


def norm_kernel(home_ref, recv_ref, edge_ref, m_ref, upd_ref, norm_ref):
    own, rows, _ = home_ref.shape
    lane = lane_of()
    fold = rows // SUB // BLOCKS
    lead = 2 * own
    sides = (edge_ref.shape[0] - lead) // fold
    norm_ref[...] = jnp.zeros_like(norm_ref)
    for k in range(own):
        total = jnp.zeros((SUB, LANES), jnp.float32)
        for r in range(rows // SUB):
            at = r * SUB
            if r == 0:
                value = edge_ref[k]
            elif r == rows // SUB - 1:
                value = edge_ref[own + k]
            else:
                value = recv_ref[k, at - SUB : at]
            g, v = divmod(r, fold)
            for side in range(sides):
                left_own, _, in_block = strip_place(side)
                edge = jnp.where(left_own, LANES - 1 - lane, lane) < HALO
                shift = (in_block - STRIP * k - HALO * g) % LANES
                turned = pltpu.roll(edge_ref[lead + side * fold + v], shift, 1)
                value = jnp.where(edge, turned, value)
            updated = home_ref[k, at : at + SUB] - step_size * value
            upd_ref[k, at : at + SUB] = updated
            total = total + m_ref[at : at + SUB] * updated * updated
        norm_ref[k : k + 1] = jnp.sum(total, axis=0, keepdims=True)


def partial_norms(home, received, edge_terms, metric):
    own, _, lanes = home.shape
    return pl.pallas_call(
        norm_kernel,
        out_shape=(f32(*home.shape), f32(-(-own // SUB) * SUB, lanes)),
        in_specs=[VMEM] * 4,
        out_specs=(VMEM, VMEM),
        compiler_params=params(),
        cost_estimate=cost(0.7),
        name="partial_norms",
    )(home, received, edge_terms, metric)


def scale_kernel(cells, upd_ref, *refs):
    out_ref = refs[-1]
    sums = functools.reduce(lambda a, b: a + b, [ref[...] for ref in refs[:-1]])
    for k in range(upd_ref.shape[0]):
        total = sums[k : k + 1]
        norm = jnp.sum(total, axis=1, keepdims=True)
        out_ref[k] = upd_ref[k] * jnp.sqrt(cells / norm)


def rescaled(updated, norms, cells):
    return pl.pallas_call(
        functools.partial(scale_kernel, float(cells)),
        out_shape=f32(*updated.shape),
        in_specs=[VMEM] * (1 + len(norms)),
        out_specs=VMEM,
        compiler_params=params(),
        cost_estimate=cost(0.8),
        name="rescaled",
    )(updated, *norms)


def shifted(value, axis, by):
    size = lax.axis_size(axis)
    return lax.ppermute(value, axis, [(i, (i + by) % size) for i in range(size)])


def pair_swaps(size):
    even = [(i, i + 1) for i in range(0, size - 1, 2)]
    odd = [(i, i + 1) for i in range(1, size - 1, 2)]
    return [p + [(b, a) for a, b in p] for p in (even, odd)]


def row_swap(swap, gx, gy):
    to = dict(swap)
    pairs = []
    for i in range(gx):
        for j in range(gy):
            pairs.append((i * gy + j, to[i] * gy + j if i in to else i * gy + (j ^ 1)))
    return pairs


def norm_hops(gx, gy):
    along = [[(i, i ^ (1 << k)) for i in range(gx * gy)] for k in range(gy.bit_length() - 1)]
    along += [[(i, i ^ gy ^ 1) for i in range(gx * gy)]]
    across = [[(i, i ^ (gy * 2) ^ 1) for i in range(gx * gy)]]
    return along, across


def local(orbitals, potentials, coefficients, metric, sweep_counts):
    own, rows, lanes = orbitals.shape
    gx, gy = lax.axis_size("gx"), lax.axis_size("gy")
    col_swaps = [p for p in pair_swaps(gy) if p]
    row_swaps = [row_swap(p, gx, gy) for p in pair_swaps(gx)]
    pairs = potentials.shape[0]

    partner = shifted(orbitals, "orb", 1)
    order, steps, *ready = prepare(
        sweep_counts[None], orbitals, potentials, metric[None], coefficients
    )
    *ready, edges, pay_a, pay_b, orbitals, potentials, metric, coefficients = ready
    metric = metric.reshape(rows, lanes)
    rows_a = lax.ppermute(pay_a, ("gx", "gy"), row_swaps[0])
    rows_b = lax.ppermute(pay_b, ("gx", "gy"), row_swaps[1])
    inner = interior(FIRST, 1, 0, order, ready, partner)
    rows_a, rows_b, inner = lax.optimization_barrier((rows_a, rows_b, inner))
    partner_rows = shifted(row_pair(own, rows_a, rows_b), "orb", 1)
    inner, back = interior(
        GROUP, (pairs - FIRST) // GROUP, FIRST, order, ready, partner, *inner
    )
    partner_rows, inner, back = lax.optimization_barrier((partner_rows, inner, back))
    early = shifted(back, "orb", -1)
    edges = tall_edges(edges, rows_a, rows_b, partner_rows, partner)
    received = [lax.ppermute(edges, "gy", swap) for swap in col_swaps]
    ends, band_back = bands(
        order, potentials, orbitals, partner, metric, coefficients,
        rows_a, rows_b, partner_rows,
    )
    edge_back, strip_fields = strips(steps, band_back, edges, received)
    edge_terms = shifted(edge_back, "orb", -1)
    fields, home = merged(inner, ends, strip_fields, orbitals, partner)
    updated, norms = partial_norms(home, early, edge_terms, metric)
    norms, fields = lax.optimization_barrier((norms, fields))
    along, across = norm_hops(gx, gy)
    for hop in along:
        norms = norms + lax.ppermute(norms, ("gx", "gy"), hop)
    norms = [norms] + [lax.ppermute(norms, ("gx", "gy"), hop) for hop in across]
    return (rescaled(updated, norms, rows * lanes * gx * gy), written(fields))


def solution(mesh):
    return jax.shard_map(
        local,
        mesh=mesh,
        in_specs=(
            P("orb", "gx", "gy"),
            P("orb", "gx", "gy"),
            P(None, "gx", "gy"),
            P("gx", "gy"),
            P("orb"),
        ),
        out_specs=(P("orb", "gx", "gy"), P("orb", "gx", "gy")),
        check_vma=False,
    )
```

```python
import functools

import jax
import jax.numpy as jnp
from jax import lax
from jax.experimental import pallas as pl
from jax.experimental.pallas import tpu as pltpu
from jax.sharding import PartitionSpec as P

SWEEPS = 8

relaxation = 0.8
screening = 0.02
step_size = 0.1

LANES = 128
SUB = 8
HALO = 8
STRIP = 32
BLOCKS = LANES // STRIP
LEAST = 4
GROUP = 8
BANDS = 8
AHEAD = 16
VMEM_LIMIT = 16 * 1024 * 1024

VMEM = pl.BlockSpec(memory_space=pltpu.VMEM)
ANY = pl.BlockSpec(memory_space=pl.ANY)
HBM = pl.BlockSpec(memory_space=pltpu.HBM)


def f32(*shape):
    return jax.ShapeDtypeStruct(shape, jnp.float32)


def params():
    return pltpu.CompilerParams(vmem_limit_bytes=VMEM_LIMIT)


def cost(microseconds):
    return pl.CostEstimate(
        flops=0, bytes_accessed=int(microseconds * 3.7e6), transcendentals=0
    )


def place():
    row, col = lax.axis_index("gx"), lax.axis_index("gy")
    inside = (row > 0) & (row < lax.axis_size("gx") - 1)
    return row % 2, col % 2, inside


def lane_of(rows=SUB):
    return lax.broadcasted_iota(jnp.int32, (rows, LANES), 1)


def packed(fields):
    rows = fields[0].shape[0]
    block = lane_of(rows) // STRIP
    out = jnp.zeros((rows, LANES), jnp.float32)
    for at, value in enumerate(fields):
        turned = pltpu.roll(value, (STRIP * at + STRIP // 2) % LANES, 1)
        out = jnp.where(block == at, turned, out)
    return out


def replicated(value, at):
    one = jnp.where(lane_of(value.shape[0]) // STRIP == at, value, 0.0)
    one = one + pltpu.roll(one, STRIP, 1)
    return one + pltpu.roll(one, 2 * STRIP, 1)


def spread(ref, count, *index):
    return [ref[(*index, pl.ds(t, SUB, stride=count), slice(None))] for t in range(count)]


def spread_store(ref, values, *index):
    count = len(values)
    for t, value in enumerate(values):
        ref[(*index, pl.ds(t, SUB, stride=count), slice(None))] = value


def scaled_coefs(coefs):
    total = coefs[0] + coefs[1] + coefs[2] + coefs[3] + 4.0 * coefs[4]
    diagonal = (1.0 + screening) * total
    return relaxation / jnp.where(diagonal == 0.0, 1.0, diagonal)


def sweep(fields, count, old, new, source, coefs, west=None, east=None, dead=None, keep=None):
    held, to_east, to_west, slopes = {}, {}, {}, {}

    def issue(k, t):
        value = old[k, t]
        held[k, t] = value
        e, w = pltpu.roll(value, LANES - 1, 1), pltpu.roll(value, 1, 1)
        if west is not None:
            w, e = jnp.where(west, 0.0, w), jnp.where(east, 0.0, e)
        to_east[k, t], to_west[k, t] = e, w

    def field(k, t):
        return held[k, t]

    def slope(k, t):
        if (k, t) not in slopes:
            slopes[k, t] = to_east[k, t] - to_west[k, t]
        return slopes[k, t]

    def above(get, k, t):
        return get(k, t - 1) if t else pltpu.roll(get(k, count - 1), 1, 0)

    def below(get, k, t):
        return get(k, t + 1) if t < count - 1 else pltpu.roll(get(k, 0), SUB - 1, 0)

    order = []
    for k in range(fields):
        order += [(k, count - 1)] + [(k, t) for t in range(count - 1)]
    done = 0
    for at in range(fields * count):
        k, t = divmod(at, count)
        until = min(len(order), max(at + AHEAD, k * count + min(t + 3, count)))
        while done < until:
            issue(*order[done])
            done += 1
        value = (1.0 - relaxation) * field(k, t) + source[k, t]
        value = value + coefs[0, t] * above(field, k, t) + coefs[1, t] * below(field, k, t)
        value = value + coefs[2, t] * to_east[k, t] + coefs[3, t] * to_west[k, t]
        value = value + coefs[4, t] * (above(slope, k, t) - below(slope, k, t))
        if dead is not None:
            value = jnp.where(dead, 0.0, value)
        if keep is not None:
            value = jnp.where(keep[k], value, field(k, t))
        new[k, t] = value


class Chosen:
    def __init__(self, ref, picks):
        self.ref, self.picks = ref, picks

    def __getitem__(self, at):
        return self.ref[self.picks[at[0]], at[1]]


def relax(steps, count, here, there, source, coefs, masks):
    fields = len(steps)
    west, east, dead = masks
    pair = (here, there)
    sweep(fields, count, here, there, source, coefs, west, east, dead)
    for s in range(1, LEAST):
        sweep(fields, count, pair[s % 2], pair[1 - s % 2], source, coefs)
    top = functools.reduce(jnp.maximum, steps)

    def body(turn, carry):
        for s in range(2):
            at = LEAST + 2 * turn + s
            keep = [jnp.full((SUB, LANES), n, jnp.int32) > at for n in steps]
            sweep(fields, count, pair[s], pair[1 - s], source, coefs, keep=keep)
        return carry

    lax.fori_loop(0, (top - LEAST + 1) // 2, body, 0)


def lane_masks(odd):
    lane = lane_of()
    west = (lane == 0) & (odd == 0)
    east = (lane == LANES - 1) & (odd == 1)
    dead = lane == (1 - odd) * (LANES - 1)
    return west, east, dead


def sorted_counts(counts):
    pairs = counts.shape[1]
    at = lax.broadcasted_iota(jnp.int32, (pairs, pairs), 1)
    down = lax.broadcasted_iota(jnp.int32, (pairs, pairs), 0)
    row = jnp.broadcast_to(counts, (pairs, pairs)).astype(jnp.float32)

    def turned(value):
        return jnp.sum(jnp.where(at == down, value, 0.0), axis=1, keepdims=True)

    def rank(key):
        own_key = turned(key)
        before = jnp.where(key > own_key, 1.0, 0.0)
        before = before + jnp.where((key == own_key) & (at < down), 1.0, 0.0)
        return jnp.sum(before, axis=1, keepdims=True)

    chosen = jnp.broadcast_to(rank(row), row.shape) == at.astype(jnp.float32)
    column = jnp.broadcast_to(turned(row), row.shape)
    steps = jnp.sum(jnp.where(chosen, column, 0.0), axis=0, keepdims=True)
    which = jnp.sum(jnp.where(chosen, down.astype(jnp.float32), 0.0), axis=0, keepdims=True)
    return jnp.concatenate([steps, which], axis=0).astype(jnp.int32)


def prepare_kernel(n_hbm, o_hbm, v_hbm, m_hbm, c_hbm, by_ref, steps_ref, *refs):
    vs_ref, os_ref, om_ref, cf_ref, e_ref, o_ref, v_ref, m_ref, c_ref = refs[:9]
    n_ref, sems = refs[9:]
    own, rows, _ = o_ref.shape
    count = rows // SUB
    sources = [(n_hbm, n_ref), (m_hbm, m_ref), (c_hbm, c_ref), (o_hbm, o_ref)]
    for first in range(own):
        part = pl.ds(first * own, own)
        sources.append((v_hbm.at[part], v_ref.at[part]))
    copies = [
        pltpu.make_async_copy(source, target, sems.at[at])
        for at, (source, target) in enumerate(sources)
    ]
    for copy in copies:
        copy.start()

    copies[0].wait()
    counts = n_ref[...]
    by_ref[...] = sorted_counts(counts)
    at = lax.broadcasted_iota(jnp.int32, counts.shape, 1)
    floats = counts.astype(jnp.float32)
    block = lane_of() // STRIP
    for first in range(own):
        steps = jnp.zeros((SUB, LANES), jnp.float32)
        for second in range(own):
            alone = jnp.where(at == first * own + second, floats, 0.0)
            steps = jnp.where(block == second, jnp.sum(alone, axis=1, keepdims=True), steps)
        steps_ref[first] = steps.astype(jnp.int32)
    copies[1].wait()
    copies[2].wait()
    e_ref[1 + own] = packed([m_ref[0], c_ref[0], c_ref[1], c_ref[2]])
    e_ref[2 + own] = packed([c_ref[3], c_ref[4]])
    dead = lane_masks(place()[1])[2]
    metric = spread(m_ref, count, 0)
    raw = [spread(c_ref, count, n) for n in range(5)]
    weights = []
    for t in range(count):
        scale = jnp.where(dead, 0.0, scaled_coefs([raw[n][t] for n in range(5)]))
        weights.append(scale * metric[t])
        for n in range(5):
            cf_ref[n, t] = scale * raw[n][t]
    copies[3].wait()
    e_ref[0] = packed([o_ref[k] for k in range(own)])
    for k in range(own):
        for t, value in enumerate(spread(o_ref, count, k)):
            os_ref[k, t] = value
            om_ref[k, t] = weights[t] * value
    for first in range(own):
        copies[4 + first].wait()
        e_ref[1 + first] = packed([v_ref[first * own + k] for k in range(own)])
        for p in range(first * own, (first + 1) * own):
            for t, value in enumerate(spread(v_ref, count, p)):
                vs_ref[p, t] = value


def prepare(*arrays):
    counts, orbitals, potentials, _, coefficients = arrays
    own, rows, lanes = orbitals.shape
    pairs = potentials.shape[0]
    count = rows // SUB
    return pl.pallas_call(
        prepare_kernel,
        out_shape=(
            jax.ShapeDtypeStruct((2, pairs), jnp.int32),
            jax.ShapeDtypeStruct((own, SUB, lanes), jnp.int32),
            f32(pairs, count, SUB, lanes),
            f32(own, count, SUB, lanes),
            f32(own, count, SUB, lanes),
            f32(5, count, SUB, lanes),
            f32(own + 3, rows, lanes),
            *[f32(*a.shape) for a in arrays[1:]],
        ),
        in_specs=[HBM] * 5,
        out_specs=(VMEM,) * 11,
        scratch_shapes=[
            pltpu.VMEM(counts.shape, jnp.int32),
            pltpu.SemaphoreType.DMA((4 + own,)),
        ],
        compiler_params=params(),
        cost_estimate=cost(2.0),
        name="prepare",
    )(*arrays)


def rows_kernel(o_hbm, v_hbm, m_hbm, c_hbm, pay_a, pay_b, sems):
    rows = o_hbm.shape[1]
    odd = place()[0]
    copies = []
    for pay, start in ((pay_a, (1 - odd) * (rows - HALO)), (pay_b, odd * (rows - HALO))):
        start = pl.multiple_of(start, HALO)
        at = 0
        for ref in (o_hbm, v_hbm, m_hbm, c_hbm):
            count = ref.shape[0]
            copy = pltpu.make_async_copy(
                ref.at[:, pl.ds(start, HALO), :], pay.at[pl.ds(at, count)], sems.at[len(copies)]
            )
            copy.start()
            copies.append(copy)
            at += count
    for copy in copies:
        copy.wait()


def row_payloads(*arrays):
    fields = sum(a.shape[0] for a in arrays)
    return pl.pallas_call(
        rows_kernel,
        out_shape=(f32(fields, HALO, arrays[0].shape[-1]),) * 2,
        in_specs=[HBM] * 4,
        out_specs=(VMEM, VMEM),
        scratch_shapes=[pltpu.SemaphoreType.DMA((8,))],
        compiler_params=params(),
        cost_estimate=cost(1.0),
        name="row_payloads",
    )(*arrays)


def interior_kernel(by_any, *refs):
    vs_ref, os_ref, om_ref, cf_ref, p_ref = refs[:5]
    out_ref, back_ref, back, flat, sr, va, vb, by_ref, sem = refs[-9:]
    own, count = om_ref.shape[:2]
    size = va.shape[0]
    fetch = pltpu.make_async_copy(by_any, by_ref, sem)
    fetch.start()
    masks = lane_masks(place()[1])
    for second in range(own):
        partner = spread(p_ref, count, second)
        for first in range(own):
            for t in range(count):
                sr[first * own + second, t] = om_ref[first, t] * partner[t]
    back[...] = jnp.zeros_like(back)
    fetch.wait()

    def group(g, carry):
        pairs = [by_ref[1, g * size + k] for k in range(size)]
        for k, p in enumerate(pairs):
            for t in range(count):
                va[k, t] = vs_ref[p, t]
        steps = [by_ref[0, g * size + k] for k in range(size)]
        relax(steps, count, va, vb, Chosen(sr, pairs), cf_ref, masks)
        for k, p in enumerate(pairs):
            first, second = p // own, p % own
            spread_store(out_ref, [va[k, t] for t in range(count)], p)
            for t in range(count):
                back[second, t] = back[second, t] + va[k, t] * os_ref[first, t]
        return carry

    lax.fori_loop(0, vs_ref.shape[0] // size, group, 0)
    for k in range(own):
        spread_store(flat, [back[k, t] for t in range(count)])
        back_ref[k] = flat[SUB : SUB + back_ref.shape[1]]


def interior(order, ready, partner):
    pairs, count, _, lanes = ready[0].shape
    own = ready[1].shape[0]
    rows = count * SUB
    some = pltpu.VMEM((GROUP, count, SUB, lanes), jnp.float32)
    each = pltpu.VMEM((own, count, SUB, lanes), jnp.float32)
    every = pltpu.VMEM((pairs, count, SUB, lanes), jnp.float32)
    return pl.pallas_call(
        interior_kernel,
        out_shape=(f32(pairs, rows, lanes), f32(own, rows - 2 * SUB, lanes)),
        in_specs=[ANY] + [VMEM] * 5,
        out_specs=(VMEM, VMEM),
        scratch_shapes=[each, pltpu.VMEM((rows, lanes), jnp.float32), every, some, some]
        + [pltpu.SMEM(order.shape, jnp.int32), pltpu.SemaphoreType.DMA],
        compiler_params=params(),
        cost_estimate=cost(5.5),
        name="interior",
    )(order, *ready[:4], partner)


def row_pair_kernel(own, a_ref, b_ref, out_ref):
    out_ref[0:own] = a_ref[0:own]
    out_ref[own:] = b_ref[0:own]


def row_pair(own, rows_a, rows_b):
    return pl.pallas_call(
        functools.partial(row_pair_kernel, own),
        out_shape=f32(2 * own, *rows_a.shape[1:]),
        in_specs=[VMEM] * 2,
        out_specs=VMEM,
        compiler_params=params(),
        cost_estimate=cost(0.1),
        name="row_pair",
    )(rows_a, rows_b)


def beyond(at, a, b):
    low_is_a = at[0] == 1
    b = jnp.where(at[2], b, 0.0)
    return jnp.where(low_is_a, a, b), jnp.where(low_is_a, b, a)


def edges_kernel(e_ref, ra_ref, rb_ref, p2_ref, p_ref, out_ref):
    here_at = place()
    own, rows, _ = p_ref.shape
    groups = e_ref.shape[0]
    for g in range(groups):
        out_ref[g, SUB : SUB + rows] = e_ref[g]
    out_ref[groups, SUB : SUB + rows] = packed([p_ref[k] for k in range(own)])
    pairs = own * own
    ends = [beyond(here_at, ra_ref[f], rb_ref[f]) for f in range(own + pairs + 6)]
    ends += [beyond(here_at, p2_ref[k], p2_ref[own + k]) for k in range(own)]
    lists = [range(own)] + [range(own * (1 + k), own * (2 + k)) for k in range(own)]
    at = own + pairs
    lists += [range(at, at + 4), range(at + 4, at + 6), range(at + 6, at + 6 + own)]
    for g, fields in enumerate(lists):
        out_ref[g, 0:SUB] = packed([ends[f][0] for f in fields])
        out_ref[g, SUB + rows :] = packed([ends[f][1] for f in fields])


def tall_edges(edges, rows_a, rows_b, partner_rows, partner):
    groups, rows, lanes = edges.shape
    return pl.pallas_call(
        edges_kernel,
        out_shape=f32(groups + 1, rows + 2 * SUB, lanes),
        in_specs=[VMEM] * 5,
        out_specs=VMEM,
        compiler_params=params(),
        cost_estimate=cost(0.7),
        name="tall_edges",
    )(edges, rows_a, rows_b, partner_rows, partner)


def bands_kernel(
    by_any, v_ref, o_ref, p_ref, m_ref, c_ref, ra_ref, rb_ref, p2_ref,
    out_ref, back_ref, band, cf, ms, sr, va, vb, by_ref, sem,
):
    fetch = pltpu.make_async_copy(by_any, by_ref, sem)
    fetch.start()
    here_at = place()
    own, rows, _ = o_ref.shape
    pairs = v_ref.shape[0]
    tall = 3 * SUB
    count = 2 * tall // SUB

    def fill(at, ends, ref, *index):
        band[at, 0:SUB] = ends[0]
        band[at, SUB:tall] = ref[(*index, slice(0, 2 * SUB))]
        band[at, tall : tall + 2 * SUB] = ref[(*index, slice(rows - 2 * SUB, rows))]
        band[at, tall + 2 * SUB : 2 * tall] = ends[1]

    def received(f):
        return beyond(here_at, ra_ref[f], rb_ref[f])

    def fill_pair(p, carry):
        fill(p, received(own + p), v_ref, p)
        return carry

    lax.fori_loop(0, pairs, fill_pair, 0, unroll=4)
    o_at, p_at = pairs, pairs + own
    m_at = p_at + own
    for k in range(own):
        fill(o_at + k, received(k), o_ref, k)
        fill(p_at + k, beyond(here_at, p2_ref[k], p2_ref[own + k]), p_ref, k)
    fill(m_at, received(own + pairs), m_ref)
    for n in range(5):
        fill(m_at + 1 + n, received(own + pairs + 1 + n), c_ref, n)

    masks = lane_masks(place()[1])
    metric = spread(band, count, m_at)
    raw = [spread(band, count, m_at + 1 + n) for n in range(5)]
    for t in range(count):
        scale = jnp.where(masks[2], 0.0, scaled_coefs([raw[n][t] for n in range(5)]))
        ms[t] = scale * metric[t]
        for n in range(5):
            cf[n, t] = scale * raw[n][t]

    def group(g, carry):
        chosen = [by_ref[1, g * BANDS + k] for k in range(BANDS)]
        for k, p in enumerate(chosen):
            o, q = spread(band, count, o_at + p // own), spread(band, count, p_at + p % own)
            v = spread(band, count, p)
            for t in range(count):
                sr[k, t] = ms[t] * (o[t] * q[t])
                va[k, t] = v[t]
        steps = [by_ref[0, g * BANDS + k] for k in range(BANDS)]
        relax(steps, count, va, vb, sr, cf, masks)
        for k, p in enumerate(chosen):
            spread_store(band, [va[k, t] for t in range(count)], p)
            out_ref[p, 0] = band[p, SUB : 2 * SUB]
            out_ref[p, 1] = band[p, tall + SUB : tall + 2 * SUB]
        return carry

    fetch.wait()
    lax.fori_loop(0, pairs // BANDS, group, 0)
    for end, start in enumerate((0, rows - SUB)):
        o = [o_ref[k, start : start + SUB] for k in range(own)]
        for second in range(own):
            terms = [out_ref[first * own + second, end] * o[first] for first in range(own)]
            back_ref[end * own + second] = sum(terms[1:], terms[0])


def bands(order, potentials, orbitals, partner, metric, coefficients, *received):
    own, rows, lanes = orbitals.shape
    pairs = potentials.shape[0]
    count = 6
    some = pltpu.VMEM((BANDS, count, SUB, lanes), jnp.float32)
    return pl.pallas_call(
        bands_kernel,
        out_shape=(f32(pairs, 2, SUB, lanes), f32(2 * own, SUB, lanes)),
        in_specs=[ANY] + [VMEM] * 8,
        out_specs=(VMEM, VMEM),
        scratch_shapes=[
            pltpu.VMEM((pairs + 2 * own + 6, count * SUB, lanes), jnp.float32),
            pltpu.VMEM((5, count, SUB, lanes), jnp.float32),
            pltpu.VMEM((count, SUB, lanes), jnp.float32),
            some,
            some,
            some,
            pltpu.SMEM(order.shape, jnp.int32),
            pltpu.SemaphoreType.DMA,
        ],
        compiler_params=params(),
        cost_estimate=cost(2.5),
        name="bands",
    )(order, potentials, orbitals, partner, metric, coefficients, *received)


def strip_place(side):
    left_own = place()[1] == side
    in_strip = jnp.where(left_own, HALO, STRIP // 2)
    in_block = jnp.where(left_own, LANES - HALO, 0)
    return left_own, in_strip, in_block


def strips_kernel(sides, n_ref, rows_ref, e_ref, *refs):
    recv = refs[:sides]
    pay_ref, sv_ref, st, cf, ms, orep, sr, va, vb, flat = refs[sides:]
    own = n_ref.shape[0]
    groups, tall, _ = e_ref.shape
    rows = tall - 2 * SUB
    count = tall // SUB
    lane = lane_of()
    lead = rows_ref.shape[0]
    fold = rows // SUB // BLOCKS
    pay_ref[0:lead] = rows_ref[...]

    for side in range(sides):
        left_own, in_strip, _ = strip_place(side)
        within = lane_of(tall) % STRIP
        from_own = jnp.where(left_own, within, STRIP - 1 - within) < STRIP // 2
        for g in range(groups):
            st[g] = jnp.where(from_own, e_ref[g], recv[side][g])
        first_group, second_group = spread(st, count, own + 1), spread(st, count, own + 2)
        for t in range(count):
            cs = [replicated(first_group[t], 1 + n) for n in range(3)]
            cs += [replicated(second_group[t], n) for n in range(2)]
            scale = scaled_coefs(cs)
            ms[t] = scale * replicated(first_group[t], 0)
            for n in range(5):
                cf[n, t] = scale * cs[n]
        o, q = spread(st, count, 0), spread(st, count, groups - 1)
        for t in range(count):
            weighted = ms[t] * q[t]
            for g in range(own):
                alone = replicated(o[t], g)
                orep[g, t] = alone
                sr[g, t] = alone * weighted
        steps = []
        for g in range(own):
            for t, value in enumerate(spread(st, count, 1 + g)):
                va[g, t] = value
            steps.append(n_ref[g])

        def body(turn, carry):
            for s in range(4):
                keep = [n > 4 * turn + s for n in steps]
                sweep(own, count, (va, vb)[s % 2], (vb, va)[s % 2], sr, cf, keep=keep)
            return carry

        lax.fori_loop(0, SWEEPS // 4, body, 0)
        back = []
        for t in range(count):
            terms = [va[g, t] * orep[g, t] for g in range(own)]
            back.append(sum(terms[1:], terms[0]))
        spread_store(flat, back)
        for g in range(own):
            spread_store(sv_ref, [va[g, t] for t in range(count)], side * own + g)
        for v in range(fold):
            out = jnp.zeros((SUB, LANES), jnp.float32)
            for g in range(BLOCKS):
                at = SUB + (g * fold + v) * SUB
                shift = (HALO * g - in_strip) % LANES
                turned = pltpu.roll(flat[at : at + SUB], shift, 1)
                out = jnp.where(lane % STRIP // HALO == g, turned, out)
            pay_ref[lead + side * fold + v] = out


def strips(steps, band_back, edges, received):
    sides = len(received)
    groups, tall, lanes = edges.shape
    own = steps.shape[0]
    count = tall // SUB
    fold = (tall - 2 * SUB) // SUB // BLOCKS
    each = pltpu.VMEM((own, count, SUB, lanes), jnp.float32)
    return pl.pallas_call(
        functools.partial(strips_kernel, sides),
        out_shape=(
            f32(band_back.shape[0] + sides * fold, SUB, lanes),
            f32(sides * own, tall, lanes),
        ),
        in_specs=[VMEM] * (3 + sides),
        out_specs=(VMEM, VMEM),
        scratch_shapes=[
            pltpu.VMEM((groups, tall, lanes), jnp.float32),
            pltpu.VMEM((5, count, SUB, lanes), jnp.float32),
            pltpu.VMEM((count, SUB, lanes), jnp.float32),
            each,
            each,
            each,
            each,
            pltpu.VMEM((tall, lanes), jnp.float32),
        ],
        compiler_params=params(),
        cost_estimate=cost(2.9),
        name="strips",
    )(steps, band_back, edges, *received)


def merge_kernel(sides, inner_ref, ends_ref, sv_ref, o_ref, p_ref, v_ref, home_ref):
    own, rows, _ = o_ref.shape
    lane = lane_of()

    def merge(r, carry):
        at = pl.multiple_of(r * SUB, SUB)
        q = [p_ref[k, pl.ds(at, SUB)] for k in range(own)]
        home = [0.0] * own
        for first in range(own):
            strips = [sv_ref[side * own + first, pl.ds(at + SUB, SUB)] for side in range(sides)]
            for second in range(own):
                p = first * own + second
                value = inner_ref[p, pl.ds(at, SUB)]
                value = jnp.where(r == 0, ends_ref[p, 0], value)
                value = jnp.where(r == rows // SUB - 1, ends_ref[p, 1], value)
                for side in range(sides):
                    right = place()[1] == side
                    edge = jnp.where(right, LANES - 1 - lane, lane) < HALO
                    turned = pltpu.roll(
                        strips[side], (-(STRIP * second + STRIP // 2)) % LANES, 1
                    )
                    value = jnp.where(edge, turned, value)
                v_ref[p, pl.ds(at, SUB)] = value
                home[first] = home[first] + value * q[second]
        for k in range(own):
            home_ref[k, pl.ds(at, SUB)] = o_ref[k, pl.ds(at, SUB)] - step_size * home[k]
        return carry

    lax.fori_loop(0, rows // SUB, merge, 0, unroll=4)


def merged(inner, ends, strip_fields, orbitals, partner):
    own, rows, _ = orbitals.shape
    sides = strip_fields.shape[0] // own
    return pl.pallas_call(
        functools.partial(merge_kernel, sides),
        out_shape=(f32(*inner.shape), f32(*orbitals.shape)),
        in_specs=[VMEM] * 5,
        out_specs=(VMEM, VMEM),
        compiler_params=params(),
        cost_estimate=cost(1.2),
        name="merge",
    )(inner, ends, strip_fields, orbitals, partner)


def write_kernel(v_ref, out_ref, sems):
    parts = sems.shape[0]
    size = v_ref.shape[0] // parts
    copies = []
    for k in range(parts):
        part = pl.ds(k * size, size)
        copies.append(pltpu.make_async_copy(v_ref.at[part], out_ref.at[part], sems.at[k]))
    for copy in copies:
        copy.start()
    for copy in copies:
        copy.wait()


def written(fields):
    return pl.pallas_call(
        write_kernel,
        out_shape=f32(*fields.shape),
        in_specs=[ANY],
        out_specs=ANY,
        scratch_shapes=[pltpu.SemaphoreType.DMA((4,))],
        compiler_params=params(),
        cost_estimate=cost(1.2),
        name="write",
    )(fields)


def norm_kernel(home_ref, recv_ref, edge_ref, m_ref, upd_ref, norm_ref):
    own, rows, _ = home_ref.shape
    lane = lane_of()
    fold = rows // SUB // BLOCKS
    lead = 2 * own
    sides = (edge_ref.shape[0] - lead) // fold
    norm_ref[...] = jnp.zeros_like(norm_ref)
    for k in range(own):
        total = jnp.zeros((SUB, LANES), jnp.float32)
        for r in range(rows // SUB):
            at = r * SUB
            if r == 0:
                value = edge_ref[k]
            elif r == rows // SUB - 1:
                value = edge_ref[own + k]
            else:
                value = recv_ref[k, at - SUB : at]
            g, v = divmod(r, fold)
            for side in range(sides):
                left_own, _, in_block = strip_place(side)
                edge = jnp.where(left_own, LANES - 1 - lane, lane) < HALO
                shift = (in_block - STRIP * k - HALO * g) % LANES
                turned = pltpu.roll(edge_ref[lead + side * fold + v], shift, 1)
                value = jnp.where(edge, turned, value)
            updated = home_ref[k, at : at + SUB] - step_size * value
            upd_ref[k, at : at + SUB] = updated
            total = total + m_ref[at : at + SUB] * updated * updated
        norm_ref[k : k + 1] = jnp.sum(total, axis=0, keepdims=True)


def partial_norms(home, received, edge_terms, metric):
    own, _, lanes = home.shape
    return pl.pallas_call(
        norm_kernel,
        out_shape=(f32(*home.shape), f32(-(-own // SUB) * SUB, lanes)),
        in_specs=[VMEM] * 4,
        out_specs=(VMEM, VMEM),
        compiler_params=params(),
        cost_estimate=cost(0.7),
        name="partial_norms",
    )(home, received, edge_terms, metric)


def scale_kernel(cells, upd_ref, *refs):
    out_ref = refs[-1]
    sums = functools.reduce(lambda a, b: a + b, [ref[...] for ref in refs[:-1]])
    for k in range(upd_ref.shape[0]):
        total = sums[k : k + 1]
        norm = jnp.sum(total, axis=1, keepdims=True)
        out_ref[k] = upd_ref[k] * jnp.sqrt(cells / norm)


def rescaled(updated, norms, cells):
    return pl.pallas_call(
        functools.partial(scale_kernel, float(cells)),
        out_shape=f32(*updated.shape),
        in_specs=[VMEM] * (1 + len(norms)),
        out_specs=VMEM,
        compiler_params=params(),
        cost_estimate=cost(0.8),
        name="rescaled",
    )(updated, *norms)


def shifted(value, axis, by):
    size = lax.axis_size(axis)
    return lax.ppermute(value, axis, [(i, (i + by) % size) for i in range(size)])


def pair_swaps(size):
    even = [(i, i + 1) for i in range(0, size - 1, 2)]
    odd = [(i, i + 1) for i in range(1, size - 1, 2)]
    return [p + [(b, a) for a, b in p] for p in (even, odd)]


def row_swap(swap, gx, gy):
    to = dict(swap)
    pairs = []
    for i in range(gx):
        for j in range(gy):
            pairs.append((i * gy + j, to[i] * gy + j if i in to else i * gy + (j ^ 1)))
    return pairs


def norm_hops(gx, gy):
    along = [[(i, i ^ (1 << k)) for i in range(gx * gy)] for k in range(gy.bit_length() - 1)]
    along += [[(i, i ^ gy ^ 1) for i in range(gx * gy)]]
    across = [[(i, i ^ (gy * 2) ^ 1) for i in range(gx * gy)]]
    return along, across


def local(orbitals, potentials, coefficients, metric, sweep_counts):
    own, rows, lanes = orbitals.shape
    gx, gy = lax.axis_size("gx"), lax.axis_size("gy")
    col_swaps = [p for p in pair_swaps(gy) if p]
    row_swaps = [row_swap(p, gx, gy) for p in pair_swaps(gx)]

    partner = shifted(orbitals, "orb", 1)
    arrays = [
        pltpu.with_memory_space_constraint(a, pltpu.HBM)
        for a in (orbitals, potentials, metric[None], coefficients)
    ]
    pay_a, pay_b = row_payloads(*arrays)
    rows_a = lax.ppermute(pay_a, ("gx", "gy"), row_swaps[0])
    rows_b = lax.ppermute(pay_b, ("gx", "gy"), row_swaps[1])
    counts = pltpu.with_memory_space_constraint(sweep_counts[None], pltpu.HBM)
    order, steps, *ready = prepare(counts, *arrays)
    *ready, edges, orbitals, potentials, metric, coefficients = ready
    metric = metric.reshape(rows, lanes)
    beside = row_pair(own, rows_a, rows_b)
    beside, order = lax.optimization_barrier((beside, order))
    partner_rows = shifted(beside, "orb", 1)
    inner, back = interior(order, ready, partner)
    partner_rows, inner, back = lax.optimization_barrier((partner_rows, inner, back))
    early = shifted(back, "orb", -1)
    edges = tall_edges(edges, rows_a, rows_b, partner_rows, partner)
    received = [lax.ppermute(edges, "gy", swap) for swap in col_swaps]
    ends, band_back = bands(
        order, potentials, orbitals, partner, metric, coefficients,
        rows_a, rows_b, partner_rows,
    )
    edge_back, strip_fields = strips(steps, band_back, edges, received)
    edge_terms = shifted(edge_back, "orb", -1)
    fields, home = merged(inner, ends, strip_fields, orbitals, partner)
    updated, norms = partial_norms(home, early, edge_terms, metric)
    norms, fields = lax.optimization_barrier((norms, fields))
    along, across = norm_hops(gx, gy)
    for hop in along:
        norms = norms + lax.ppermute(norms, ("gx", "gy"), hop)
    norms = [norms] + [lax.ppermute(norms, ("gx", "gy"), hop) for hop in across]
    return (rescaled(updated, norms, rows * lanes * gx * gy), written(fields))


def solution(mesh):
    return jax.shard_map(
        local,
        mesh=mesh,
        in_specs=(
            P("orb", "gx", "gy"),
            P("orb", "gx", "gy"),
            P(None, "gx", "gy"),
            P("gx", "gy"),
            P("orb"),
        ),
        out_specs=(P("orb", "gx", "gy"), P("orb", "gx", "gy")),
        check_vma=False,
    )
```

```python
import functools

import jax
import jax.numpy as jnp
from jax import lax
from jax.experimental import pallas as pl
from jax.experimental.pallas import tpu as pltpu
from jax.sharding import PartitionSpec as P

SWEEPS = 8

relaxation = 0.8
screening = 0.02
step_size = 0.1

LANES = 128
SUB = 8
HALO = 8
STRIP = 32
BLOCKS = LANES // STRIP
LEAST = 4
GROUP = 8
BANDS = 8
AHEAD = 16
VMEM_LIMIT = 16 * 1024 * 1024

VMEM = pl.BlockSpec(memory_space=pltpu.VMEM)
ANY = pl.BlockSpec(memory_space=pl.ANY)
HBM = pl.BlockSpec(memory_space=pltpu.HBM)


def f32(*shape):
    return jax.ShapeDtypeStruct(shape, jnp.float32)


def params():
    return pltpu.CompilerParams(vmem_limit_bytes=VMEM_LIMIT)


def cost(microseconds):
    return pl.CostEstimate(
        flops=0, bytes_accessed=int(microseconds * 3.7e6), transcendentals=0
    )


def place():
    row, col = lax.axis_index("gx"), lax.axis_index("gy")
    inside = (row > 0) & (row < lax.axis_size("gx") - 1)
    return row % 2, col % 2, inside


def lane_of(rows=SUB):
    return lax.broadcasted_iota(jnp.int32, (rows, LANES), 1)


def packed(fields):
    rows = fields[0].shape[0]
    block = lane_of(rows) // STRIP
    out = jnp.zeros((rows, LANES), jnp.float32)
    for at, value in enumerate(fields):
        turned = pltpu.roll(value, (STRIP * at + STRIP // 2) % LANES, 1)
        out = jnp.where(block == at, turned, out)
    return out


def replicated(value, at):
    one = jnp.where(lane_of(value.shape[0]) // STRIP == at, value, 0.0)
    one = one + pltpu.roll(one, STRIP, 1)
    return one + pltpu.roll(one, 2 * STRIP, 1)


def spread(ref, count, *index):
    return [ref[(*index, pl.ds(t, SUB, stride=count), slice(None))] for t in range(count)]


def spread_store(ref, values, *index):
    count = len(values)
    for t, value in enumerate(values):
        ref[(*index, pl.ds(t, SUB, stride=count), slice(None))] = value


def scaled_coefs(coefs):
    total = coefs[0] + coefs[1] + coefs[2] + coefs[3] + 4.0 * coefs[4]
    diagonal = (1.0 + screening) * total
    return relaxation / jnp.where(diagonal == 0.0, 1.0, diagonal)


def sweep(fields, count, old, new, source, coefs, west=None, east=None, dead=None, keep=None):
    held, to_east, to_west, slopes = {}, {}, {}, {}

    def issue(k, t):
        value = old[k, t]
        held[k, t] = value
        e, w = pltpu.roll(value, LANES - 1, 1), pltpu.roll(value, 1, 1)
        if west is not None:
            w, e = jnp.where(west, 0.0, w), jnp.where(east, 0.0, e)
        to_east[k, t], to_west[k, t] = e, w

    def field(k, t):
        return held[k, t]

    def slope(k, t):
        if (k, t) not in slopes:
            slopes[k, t] = to_east[k, t] - to_west[k, t]
        return slopes[k, t]

    def above(get, k, t):
        return get(k, t - 1) if t else pltpu.roll(get(k, count - 1), 1, 0)

    def below(get, k, t):
        return get(k, t + 1) if t < count - 1 else pltpu.roll(get(k, 0), SUB - 1, 0)

    order = []
    for k in range(fields):
        order += [(k, count - 1)] + [(k, t) for t in range(count - 1)]
    done = 0
    for at in range(fields * count):
        k, t = divmod(at, count)
        until = min(len(order), max(at + AHEAD, k * count + min(t + 3, count)))
        while done < until:
            issue(*order[done])
            done += 1
        value = (1.0 - relaxation) * field(k, t) + source[k, t]
        value = value + coefs[0, t] * above(field, k, t) + coefs[1, t] * below(field, k, t)
        value = value + coefs[2, t] * to_east[k, t] + coefs[3, t] * to_west[k, t]
        value = value + coefs[4, t] * (above(slope, k, t) - below(slope, k, t))
        if dead is not None:
            value = jnp.where(dead, 0.0, value)
        if keep is not None:
            value = jnp.where(keep[k], value, field(k, t))
        new[k, t] = value


class Chosen:
    def __init__(self, ref, picks):
        self.ref, self.picks = ref, picks

    def __getitem__(self, at):
        return self.ref[self.picks[at[0]], at[1]]


def relax(steps, count, here, there, source, coefs, masks):
    fields = len(steps)
    west, east, dead = masks
    pair = (here, there)
    sweep(fields, count, here, there, source, coefs, west, east, dead)
    for s in range(1, LEAST):
        sweep(fields, count, pair[s % 2], pair[1 - s % 2], source, coefs)
    top = functools.reduce(jnp.maximum, steps)

    def body(turn, carry):
        for s in range(2):
            at = LEAST + 2 * turn + s
            keep = [jnp.full((SUB, LANES), n, jnp.int32) > at for n in steps]
            sweep(fields, count, pair[s], pair[1 - s], source, coefs, keep=keep)
        return carry

    lax.fori_loop(0, (top - LEAST) // 2, body, 0)

    @pl.when((top - LEAST) % 2 == 1)
    def _():
        keep = [jnp.full((SUB, LANES), n, jnp.int32) >= top for n in steps]
        sweep(fields, count, here, there, source, coefs, keep=keep)
        for k in range(fields):
            for t in range(count):
                here[k, t] = there[k, t]


def lane_masks(odd):
    lane = lane_of()
    west = (lane == 0) & (odd == 0)
    east = (lane == LANES - 1) & (odd == 1)
    dead = lane == (1 - odd) * (LANES - 1)
    return west, east, dead


def sorted_counts(counts):
    pairs = counts.shape[1]
    at = lax.broadcasted_iota(jnp.int32, (pairs, pairs), 1)
    down = lax.broadcasted_iota(jnp.int32, (pairs, pairs), 0)
    row = jnp.broadcast_to(counts, (pairs, pairs)).astype(jnp.float32)

    def turned(value):
        return jnp.sum(jnp.where(at == down, value, 0.0), axis=1, keepdims=True)

    def rank(key):
        own_key = turned(key)
        before = jnp.where(key > own_key, 1.0, 0.0)
        before = before + jnp.where((key == own_key) & (at < down), 1.0, 0.0)
        return jnp.sum(before, axis=1, keepdims=True)

    chosen = jnp.broadcast_to(rank(row), row.shape) == at.astype(jnp.float32)
    column = jnp.broadcast_to(turned(row), row.shape)
    steps = jnp.sum(jnp.where(chosen, column, 0.0), axis=0, keepdims=True)
    which = jnp.sum(jnp.where(chosen, down.astype(jnp.float32), 0.0), axis=0, keepdims=True)
    return jnp.concatenate([steps, which], axis=0).astype(jnp.int32)


def prepare_kernel(n_hbm, o_hbm, v_hbm, m_hbm, c_hbm, by_ref, steps_ref, *refs):
    vs_ref, os_ref, om_ref, cf_ref, e_ref, o_ref, v_ref, m_ref, c_ref = refs[:9]
    n_ref, sems = refs[9:]
    own, rows, _ = o_ref.shape
    count = rows // SUB
    sources = [(n_hbm, n_ref), (m_hbm, m_ref), (c_hbm, c_ref), (o_hbm, o_ref)]
    for first in range(own):
        part = pl.ds(first * own, own)
        sources.append((v_hbm.at[part], v_ref.at[part]))
    copies = [
        pltpu.make_async_copy(source, target, sems.at[at])
        for at, (source, target) in enumerate(sources)
    ]
    for copy in copies:
        copy.start()

    copies[0].wait()
    counts = n_ref[...]
    by_ref[...] = sorted_counts(counts)
    at = lax.broadcasted_iota(jnp.int32, counts.shape, 1)
    floats = counts.astype(jnp.float32)
    block = lane_of() // STRIP
    for first in range(own):
        steps = jnp.zeros((SUB, LANES), jnp.float32)
        for second in range(own):
            alone = jnp.where(at == first * own + second, floats, 0.0)
            steps = jnp.where(block == second, jnp.sum(alone, axis=1, keepdims=True), steps)
        steps_ref[first] = steps.astype(jnp.int32)
    copies[1].wait()
    copies[2].wait()
    e_ref[1 + own] = packed([m_ref[0], c_ref[0], c_ref[1], c_ref[2]])
    e_ref[2 + own] = packed([c_ref[3], c_ref[4]])
    dead = lane_masks(place()[1])[2]
    metric = spread(m_ref, count, 0)
    raw = [spread(c_ref, count, n) for n in range(5)]
    weights = []
    for t in range(count):
        scale = jnp.where(dead, 0.0, scaled_coefs([raw[n][t] for n in range(5)]))
        weights.append(scale * metric[t])
        for n in range(5):
            cf_ref[n, t] = scale * raw[n][t]
    copies[3].wait()
    e_ref[0] = packed([o_ref[k] for k in range(own)])
    for k in range(own):
        for t, value in enumerate(spread(o_ref, count, k)):
            os_ref[k, t] = value
            om_ref[k, t] = weights[t] * value
    for first in range(own):
        copies[4 + first].wait()
        e_ref[1 + first] = packed([v_ref[first * own + k] for k in range(own)])
        for p in range(first * own, (first + 1) * own):
            for t, value in enumerate(spread(v_ref, count, p)):
                vs_ref[p, t] = value


def prepare(*arrays):
    counts, orbitals, potentials, _, coefficients = arrays
    own, rows, lanes = orbitals.shape
    pairs = potentials.shape[0]
    count = rows // SUB
    return pl.pallas_call(
        prepare_kernel,
        out_shape=(
            jax.ShapeDtypeStruct((2, pairs), jnp.int32),
            jax.ShapeDtypeStruct((own, SUB, lanes), jnp.int32),
            f32(pairs, count, SUB, lanes),
            f32(own, count, SUB, lanes),
            f32(own, count, SUB, lanes),
            f32(5, count, SUB, lanes),
            f32(own + 3, rows, lanes),
            *[f32(*a.shape) for a in arrays[1:]],
        ),
        in_specs=[HBM] * 5,
        out_specs=(VMEM,) * 11,
        scratch_shapes=[
            pltpu.VMEM(counts.shape, jnp.int32),
            pltpu.SemaphoreType.DMA((4 + own,)),
        ],
        compiler_params=params(),
        cost_estimate=cost(2.0),
        name="prepare",
    )(*arrays)


def rows_kernel(o_hbm, v_hbm, m_hbm, c_hbm, pay_a, pay_b, sems):
    rows = o_hbm.shape[1]
    odd = place()[0]
    copies = []
    for pay, start in ((pay_a, (1 - odd) * (rows - HALO)), (pay_b, odd * (rows - HALO))):
        start = pl.multiple_of(start, HALO)
        at = 0
        for ref in (o_hbm, v_hbm, m_hbm, c_hbm):
            count = ref.shape[0]
            copy = pltpu.make_async_copy(
                ref.at[:, pl.ds(start, HALO), :], pay.at[pl.ds(at, count)], sems.at[len(copies)]
            )
            copy.start()
            copies.append(copy)
            at += count
    for copy in copies:
        copy.wait()


def row_payloads(*arrays):
    fields = sum(a.shape[0] for a in arrays)
    return pl.pallas_call(
        rows_kernel,
        out_shape=(f32(fields, HALO, arrays[0].shape[-1]),) * 2,
        in_specs=[HBM] * 4,
        out_specs=(VMEM, VMEM),
        scratch_shapes=[pltpu.SemaphoreType.DMA((8,))],
        compiler_params=params(),
        cost_estimate=cost(1.0),
        name="row_payloads",
    )(*arrays)


def interior_kernel(by_any, *refs):
    vs_ref, os_ref, om_ref, cf_ref, p_ref = refs[:5]
    out_ref, back_ref, back, flat, sr, va, vb, by_ref, sem = refs[-9:]
    own, count = om_ref.shape[:2]
    size = va.shape[0]
    fetch = pltpu.make_async_copy(by_any, by_ref, sem)
    fetch.start()
    masks = lane_masks(place()[1])
    for second in range(own):
        partner = spread(p_ref, count, second)
        for first in range(own):
            for t in range(count):
                sr[first * own + second, t] = om_ref[first, t] * partner[t]
    back[...] = jnp.zeros_like(back)
    fetch.wait()

    def group(g, carry):
        pairs = [by_ref[1, g * size + k] for k in range(size)]
        for k, p in enumerate(pairs):
            for t in range(count):
                va[k, t] = vs_ref[p, t]
        steps = [by_ref[0, g * size + k] for k in range(size)]
        relax(steps, count, va, vb, Chosen(sr, pairs), cf_ref, masks)
        for k, p in enumerate(pairs):
            first, second = p // own, p % own
            spread_store(out_ref, [va[k, t] for t in range(count)], p)
            for t in range(count):
                back[second, t] = back[second, t] + va[k, t] * os_ref[first, t]
        return carry

    lax.fori_loop(0, vs_ref.shape[0] // size, group, 0)
    for k in range(own):
        spread_store(flat, [back[k, t] for t in range(count)])
        back_ref[k] = flat[SUB : SUB + back_ref.shape[1]]


def interior(order, ready, partner):
    pairs, count, _, lanes = ready[0].shape
    own = ready[1].shape[0]
    rows = count * SUB
    some = pltpu.VMEM((GROUP, count, SUB, lanes), jnp.float32)
    each = pltpu.VMEM((own, count, SUB, lanes), jnp.float32)
    every = pltpu.VMEM((pairs, count, SUB, lanes), jnp.float32)
    return pl.pallas_call(
        interior_kernel,
        out_shape=(f32(pairs, rows, lanes), f32(own, rows - 2 * SUB, lanes)),
        in_specs=[ANY] + [VMEM] * 5,
        out_specs=(VMEM, VMEM),
        scratch_shapes=[each, pltpu.VMEM((rows, lanes), jnp.float32), every, some, some]
        + [pltpu.SMEM(order.shape, jnp.int32), pltpu.SemaphoreType.DMA],
        compiler_params=params(),
        cost_estimate=cost(5.5),
        name="interior",
    )(order, *ready[:4], partner)


def row_pair_kernel(own, a_ref, b_ref, out_ref):
    out_ref[0:own] = a_ref[0:own]
    out_ref[own:] = b_ref[0:own]


def row_pair(own, rows_a, rows_b):
    return pl.pallas_call(
        functools.partial(row_pair_kernel, own),
        out_shape=f32(2 * own, *rows_a.shape[1:]),
        in_specs=[VMEM] * 2,
        out_specs=VMEM,
        compiler_params=params(),
        cost_estimate=cost(0.1),
        name="row_pair",
    )(rows_a, rows_b)


def beyond(at, a, b):
    low_is_a = at[0] == 1
    b = jnp.where(at[2], b, 0.0)
    return jnp.where(low_is_a, a, b), jnp.where(low_is_a, b, a)


def edges_kernel(e_ref, ra_ref, rb_ref, p2_ref, p_ref, out_ref):
    here_at = place()
    own, rows, _ = p_ref.shape
    groups = e_ref.shape[0]
    for g in range(groups):
        out_ref[g, SUB : SUB + rows] = e_ref[g]
    out_ref[groups, SUB : SUB + rows] = packed([p_ref[k] for k in range(own)])
    pairs = own * own
    ends = [beyond(here_at, ra_ref[f], rb_ref[f]) for f in range(own + pairs + 6)]
    ends += [beyond(here_at, p2_ref[k], p2_ref[own + k]) for k in range(own)]
    lists = [range(own)] + [range(own * (1 + k), own * (2 + k)) for k in range(own)]
    at = own + pairs
    lists += [range(at, at + 4), range(at + 4, at + 6), range(at + 6, at + 6 + own)]
    for g, fields in enumerate(lists):
        out_ref[g, 0:SUB] = packed([ends[f][0] for f in fields])
        out_ref[g, SUB + rows :] = packed([ends[f][1] for f in fields])


def tall_edges(edges, rows_a, rows_b, partner_rows, partner):
    groups, rows, lanes = edges.shape
    return pl.pallas_call(
        edges_kernel,
        out_shape=f32(groups + 1, rows + 2 * SUB, lanes),
        in_specs=[VMEM] * 5,
        out_specs=VMEM,
        compiler_params=params(),
        cost_estimate=cost(0.7),
        name="tall_edges",
    )(edges, rows_a, rows_b, partner_rows, partner)


def bands_kernel(
    by_any, v_ref, o_ref, p_ref, m_ref, c_ref, ra_ref, rb_ref, p2_ref,
    out_ref, back_ref, band, cf, ms, sr, va, vb, by_ref, sem,
):
    fetch = pltpu.make_async_copy(by_any, by_ref, sem)
    fetch.start()
    here_at = place()
    own, rows, _ = o_ref.shape
    pairs = v_ref.shape[0]
    tall = 3 * SUB
    count = 2 * tall // SUB

    def fill(at, ends, ref, *index):
        band[at, 0:SUB] = ends[0]
        band[at, SUB:tall] = ref[(*index, slice(0, 2 * SUB))]
        band[at, tall : tall + 2 * SUB] = ref[(*index, slice(rows - 2 * SUB, rows))]
        band[at, tall + 2 * SUB : 2 * tall] = ends[1]

    def received(f):
        return beyond(here_at, ra_ref[f], rb_ref[f])

    def fill_pair(p, carry):
        fill(p, received(own + p), v_ref, p)
        return carry

    lax.fori_loop(0, pairs, fill_pair, 0, unroll=4)
    o_at, p_at = pairs, pairs + own
    m_at = p_at + own
    for k in range(own):
        fill(o_at + k, received(k), o_ref, k)
        fill(p_at + k, beyond(here_at, p2_ref[k], p2_ref[own + k]), p_ref, k)
    fill(m_at, received(own + pairs), m_ref)
    for n in range(5):
        fill(m_at + 1 + n, received(own + pairs + 1 + n), c_ref, n)

    masks = lane_masks(place()[1])
    metric = spread(band, count, m_at)
    raw = [spread(band, count, m_at + 1 + n) for n in range(5)]
    for t in range(count):
        scale = jnp.where(masks[2], 0.0, scaled_coefs([raw[n][t] for n in range(5)]))
        ms[t] = scale * metric[t]
        for n in range(5):
            cf[n, t] = scale * raw[n][t]

    def group(g, carry):
        chosen = [by_ref[1, g * BANDS + k] for k in range(BANDS)]
        for k, p in enumerate(chosen):
            o, q = spread(band, count, o_at + p // own), spread(band, count, p_at + p % own)
            v = spread(band, count, p)
            for t in range(count):
                sr[k, t] = ms[t] * (o[t] * q[t])
                va[k, t] = v[t]
        steps = [by_ref[0, g * BANDS + k] for k in range(BANDS)]
        relax(steps, count, va, vb, sr, cf, masks)
        for k, p in enumerate(chosen):
            spread_store(band, [va[k, t] for t in range(count)], p)
            out_ref[p, 0] = band[p, SUB : 2 * SUB]
            out_ref[p, 1] = band[p, tall + SUB : tall + 2 * SUB]
        return carry

    fetch.wait()
    lax.fori_loop(0, pairs // BANDS, group, 0)
    for end, start in enumerate((0, rows - SUB)):
        o = [o_ref[k, start : start + SUB] for k in range(own)]
        for second in range(own):
            terms = [out_ref[first * own + second, end] * o[first] for first in range(own)]
            back_ref[end * own + second] = sum(terms[1:], terms[0])


def bands(order, potentials, orbitals, partner, metric, coefficients, *received):
    own, rows, lanes = orbitals.shape
    pairs = potentials.shape[0]
    count = 6
    some = pltpu.VMEM((BANDS, count, SUB, lanes), jnp.float32)
    return pl.pallas_call(
        bands_kernel,
        out_shape=(f32(pairs, 2, SUB, lanes), f32(2 * own, SUB, lanes)),
        in_specs=[ANY] + [VMEM] * 8,
        out_specs=(VMEM, VMEM),
        scratch_shapes=[
            pltpu.VMEM((pairs + 2 * own + 6, count * SUB, lanes), jnp.float32),
            pltpu.VMEM((5, count, SUB, lanes), jnp.float32),
            pltpu.VMEM((count, SUB, lanes), jnp.float32),
            some,
            some,
            some,
            pltpu.SMEM(order.shape, jnp.int32),
            pltpu.SemaphoreType.DMA,
        ],
        compiler_params=params(),
        cost_estimate=cost(2.5),
        name="bands",
    )(order, potentials, orbitals, partner, metric, coefficients, *received)


def strip_place(side):
    left_own = place()[1] == side
    in_strip = jnp.where(left_own, HALO, STRIP // 2)
    in_block = jnp.where(left_own, LANES - HALO, 0)
    return left_own, in_strip, in_block


def strips_kernel(sides, n_ref, rows_ref, e_ref, *refs):
    recv = refs[:sides]
    pay_ref, sv_ref, st, cf, ms, orep, sr, va, vb, flat = refs[sides:]
    own = n_ref.shape[0]
    groups, tall, _ = e_ref.shape
    rows = tall - 2 * SUB
    count = tall // SUB
    lane = lane_of()
    lead = rows_ref.shape[0]
    fold = rows // SUB // BLOCKS
    pay_ref[0:lead] = rows_ref[...]

    for side in range(sides):
        left_own, in_strip, _ = strip_place(side)
        within = lane_of(tall) % STRIP
        from_own = jnp.where(left_own, within, STRIP - 1 - within) < STRIP // 2
        for g in range(groups):
            st[g] = jnp.where(from_own, e_ref[g], recv[side][g])
        first_group, second_group = spread(st, count, own + 1), spread(st, count, own + 2)
        for t in range(count):
            cs = [replicated(first_group[t], 1 + n) for n in range(3)]
            cs += [replicated(second_group[t], n) for n in range(2)]
            scale = scaled_coefs(cs)
            ms[t] = scale * replicated(first_group[t], 0)
            for n in range(5):
                cf[n, t] = scale * cs[n]
        o, q = spread(st, count, 0), spread(st, count, groups - 1)
        for t in range(count):
            weighted = ms[t] * q[t]
            for g in range(own):
                alone = replicated(o[t], g)
                orep[g, t] = alone
                sr[g, t] = alone * weighted
        steps = []
        for g in range(own):
            for t, value in enumerate(spread(st, count, 1 + g)):
                va[g, t] = value
            steps.append(n_ref[g])

        def body(turn, carry):
            for s in range(4):
                keep = [n > 4 * turn + s for n in steps]
                sweep(own, count, (va, vb)[s % 2], (vb, va)[s % 2], sr, cf, keep=keep)
            return carry

        lax.fori_loop(0, SWEEPS // 4, body, 0)
        back = []
        for t in range(count):
            terms = [va[g, t] * orep[g, t] for g in range(own)]
            back.append(sum(terms[1:], terms[0]))
        spread_store(flat, back)
        for g in range(own):
            spread_store(sv_ref, [va[g, t] for t in range(count)], side * own + g)
        for v in range(fold):
            out = jnp.zeros((SUB, LANES), jnp.float32)
            for g in range(BLOCKS):
                at = SUB + (g * fold + v) * SUB
                shift = (HALO * g - in_strip) % LANES
                turned = pltpu.roll(flat[at : at + SUB], shift, 1)
                out = jnp.where(lane % STRIP // HALO == g, turned, out)
            pay_ref[lead + side * fold + v] = out


def strips(steps, band_back, edges, received):
    sides = len(received)
    groups, tall, lanes = edges.shape
    own = steps.shape[0]
    count = tall // SUB
    fold = (tall - 2 * SUB) // SUB // BLOCKS
    each = pltpu.VMEM((own, count, SUB, lanes), jnp.float32)
    return pl.pallas_call(
        functools.partial(strips_kernel, sides),
        out_shape=(
            f32(band_back.shape[0] + sides * fold, SUB, lanes),
            f32(sides * own, tall, lanes),
        ),
        in_specs=[VMEM] * (3 + sides),
        out_specs=(VMEM, VMEM),
        scratch_shapes=[
            pltpu.VMEM((groups, tall, lanes), jnp.float32),
            pltpu.VMEM((5, count, SUB, lanes), jnp.float32),
            pltpu.VMEM((count, SUB, lanes), jnp.float32),
            each,
            each,
            each,
            each,
            pltpu.VMEM((tall, lanes), jnp.float32),
        ],
        compiler_params=params(),
        cost_estimate=cost(2.9),
        name="strips",
    )(steps, band_back, edges, *received)


def merge_kernel(sides, inner_ref, ends_ref, sv_ref, o_ref, p_ref, v_ref, home_ref):
    own, rows, _ = o_ref.shape
    lane = lane_of()

    def merge(r, carry):
        at = pl.multiple_of(r * SUB, SUB)
        q = [p_ref[k, pl.ds(at, SUB)] for k in range(own)]
        home = [0.0] * own
        for first in range(own):
            strips = [sv_ref[side * own + first, pl.ds(at + SUB, SUB)] for side in range(sides)]
            for second in range(own):
                p = first * own + second
                value = inner_ref[p, pl.ds(at, SUB)]
                value = jnp.where(r == 0, ends_ref[p, 0], value)
                value = jnp.where(r == rows // SUB - 1, ends_ref[p, 1], value)
                for side in range(sides):
                    right = place()[1] == side
                    edge = jnp.where(right, LANES - 1 - lane, lane) < HALO
                    turned = pltpu.roll(
                        strips[side], (-(STRIP * second + STRIP // 2)) % LANES, 1
                    )
                    value = jnp.where(edge, turned, value)
                v_ref[p, pl.ds(at, SUB)] = value
                home[first] = home[first] + value * q[second]
        for k in range(own):
            home_ref[k, pl.ds(at, SUB)] = o_ref[k, pl.ds(at, SUB)] - step_size * home[k]
        return carry

    lax.fori_loop(0, rows // SUB, merge, 0, unroll=4)


def merged(inner, ends, strip_fields, orbitals, partner):
    own, rows, _ = orbitals.shape
    sides = strip_fields.shape[0] // own
    return pl.pallas_call(
        functools.partial(merge_kernel, sides),
        out_shape=(f32(*inner.shape), f32(*orbitals.shape)),
        in_specs=[VMEM] * 5,
        out_specs=(VMEM, VMEM),
        compiler_params=params(),
        cost_estimate=cost(1.2),
        name="merge",
    )(inner, ends, strip_fields, orbitals, partner)


def write_kernel(v_ref, out_ref, sems):
    parts = sems.shape[0]
    size = v_ref.shape[0] // parts
    copies = []
    for k in range(parts):
        part = pl.ds(k * size, size)
        copies.append(pltpu.make_async_copy(v_ref.at[part], out_ref.at[part], sems.at[k]))
    for copy in copies:
        copy.start()
    for copy in copies:
        copy.wait()


def written(fields):
    return pl.pallas_call(
        write_kernel,
        out_shape=f32(*fields.shape),
        in_specs=[ANY],
        out_specs=ANY,
        scratch_shapes=[pltpu.SemaphoreType.DMA((4,))],
        compiler_params=params(),
        cost_estimate=cost(1.2),
        name="write",
    )(fields)


def norm_kernel(home_ref, recv_ref, edge_ref, m_ref, upd_ref, norm_ref):
    own, rows, _ = home_ref.shape
    lane = lane_of()
    fold = rows // SUB // BLOCKS
    lead = 2 * own
    sides = (edge_ref.shape[0] - lead) // fold
    norm_ref[...] = jnp.zeros_like(norm_ref)
    for k in range(own):
        total = jnp.zeros((SUB, LANES), jnp.float32)
        for r in range(rows // SUB):
            at = r * SUB
            if r == 0:
                value = edge_ref[k]
            elif r == rows // SUB - 1:
                value = edge_ref[own + k]
            else:
                value = recv_ref[k, at - SUB : at]
            g, v = divmod(r, fold)
            for side in range(sides):
                left_own, _, in_block = strip_place(side)
                edge = jnp.where(left_own, LANES - 1 - lane, lane) < HALO
                shift = (in_block - STRIP * k - HALO * g) % LANES
                turned = pltpu.roll(edge_ref[lead + side * fold + v], shift, 1)
                value = jnp.where(edge, turned, value)
            updated = home_ref[k, at : at + SUB] - step_size * value
            upd_ref[k, at : at + SUB] = updated
            total = total + m_ref[at : at + SUB] * updated * updated
        norm_ref[k : k + 1] = jnp.sum(total, axis=0, keepdims=True)


def partial_norms(home, received, edge_terms, metric):
    own, _, lanes = home.shape
    return pl.pallas_call(
        norm_kernel,
        out_shape=(f32(*home.shape), f32(-(-own // SUB) * SUB, lanes)),
        in_specs=[VMEM] * 4,
        out_specs=(VMEM, VMEM),
        compiler_params=params(),
        cost_estimate=cost(0.7),
        name="partial_norms",
    )(home, received, edge_terms, metric)


def scale_kernel(cells, upd_ref, *refs):
    out_ref = refs[-1]
    sums = functools.reduce(lambda a, b: a + b, [ref[...] for ref in refs[:-1]])
    for k in range(upd_ref.shape[0]):
        total = sums[k : k + 1]
        norm = jnp.sum(total, axis=1, keepdims=True)
        out_ref[k] = upd_ref[k] * jnp.sqrt(cells / norm)


def rescaled(updated, norms, cells):
    return pl.pallas_call(
        functools.partial(scale_kernel, float(cells)),
        out_shape=f32(*updated.shape),
        in_specs=[VMEM] * (1 + len(norms)),
        out_specs=VMEM,
        compiler_params=params(),
        cost_estimate=cost(0.8),
        name="rescaled",
    )(updated, *norms)


def shifted(value, axis, by):
    size = lax.axis_size(axis)
    return lax.ppermute(value, axis, [(i, (i + by) % size) for i in range(size)])


def pair_swaps(size):
    even = [(i, i + 1) for i in range(0, size - 1, 2)]
    odd = [(i, i + 1) for i in range(1, size - 1, 2)]
    return [p + [(b, a) for a, b in p] for p in (even, odd)]


def row_swap(swap, gx, gy):
    to = dict(swap)
    pairs = []
    for i in range(gx):
        for j in range(gy):
            pairs.append((i * gy + j, to[i] * gy + j if i in to else i * gy + (j ^ 1)))
    return pairs


def norm_hops(gx, gy):
    along = [[(i, i ^ (1 << k)) for i in range(gx * gy)] for k in range(gy.bit_length() - 1)]
    along += [[(i, i ^ gy ^ 1) for i in range(gx * gy)]]
    across = [[(i, i ^ (gy * 2) ^ 1) for i in range(gx * gy)]]
    return along, across


def local(orbitals, potentials, coefficients, metric, sweep_counts):
    own, rows, lanes = orbitals.shape
    gx, gy = lax.axis_size("gx"), lax.axis_size("gy")
    col_swaps = [p for p in pair_swaps(gy) if p]
    row_swaps = [row_swap(p, gx, gy) for p in pair_swaps(gx)]

    partner = shifted(orbitals, "orb", 1)
    arrays = [
        pltpu.with_memory_space_constraint(a, pltpu.HBM)
        for a in (orbitals, potentials, metric[None], coefficients)
    ]
    pay_a, pay_b = row_payloads(*arrays)
    rows_a = lax.ppermute(pay_a, ("gx", "gy"), row_swaps[0])
    rows_b = lax.ppermute(pay_b, ("gx", "gy"), row_swaps[1])
    counts = pltpu.with_memory_space_constraint(sweep_counts[None], pltpu.HBM)
    order, steps, *ready = prepare(counts, *arrays)
    *ready, edges, orbitals, potentials, metric, coefficients = ready
    metric = metric.reshape(rows, lanes)
    beside = row_pair(own, rows_a, rows_b)
    beside, order = lax.optimization_barrier((beside, order))
    partner_rows = shifted(beside, "orb", 1)
    inner, back = interior(order, ready, partner)
    partner_rows, inner, back = lax.optimization_barrier((partner_rows, inner, back))
    early = shifted(back, "orb", -1)
    edges = tall_edges(edges, rows_a, rows_b, partner_rows, partner)
    received = [lax.ppermute(edges, "gy", swap) for swap in col_swaps]
    ends, band_back = bands(
        order, potentials, orbitals, partner, metric, coefficients,
        rows_a, rows_b, partner_rows,
    )
    edge_back, strip_fields = strips(steps, band_back, edges, received)
    edge_terms = shifted(edge_back, "orb", -1)
    fields, home = merged(inner, ends, strip_fields, orbitals, partner)
    updated, norms = partial_norms(home, early, edge_terms, metric)
    norms, fields = lax.optimization_barrier((norms, fields))
    along, across = norm_hops(gx, gy)
    for hop in along:
        norms = norms + lax.ppermute(norms, ("gx", "gy"), hop)
    norms = [norms] + [lax.ppermute(norms, ("gx", "gy"), hop) for hop in across]
    return (rescaled(updated, norms, rows * lanes * gx * gy), written(fields))


def solution(mesh):
    return jax.shard_map(
        local,
        mesh=mesh,
        in_specs=(
            P("orb", "gx", "gy"),
            P("orb", "gx", "gy"),
            P(None, "gx", "gy"),
            P("gx", "gy"),
            P("orb"),
        ),
        out_specs=(P("orb", "gx", "gy"), P("orb", "gx", "gy")),
        check_vma=False,
    )
```
